32 devices in a mesh: ctx: 4 (over y, x), fsdp: 8 (over z, core).
Axes of the slice: x: 2, y: 2, z: 4, core: 2. Of those that a mesh axis runs over, the one named last changes fastest.
Arguments:
- tokens: bfloat16 [8, 2048, 1024], P('fsdp', 'ctx'), may hold values from -6 to 6
- teacher: bfloat16 [8, 2048, 1024], P('fsdp', 'ctx'), may hold values from -6 to 6
- cotangent: bfloat16 [8, 2048, 1024], P('fsdp', 'ctx'), may hold values from -6 to 6
- lengths: int32 [8, 8], P('fsdp'), may hold values from 1 to 1789, as said below
- variate: int32 [8, 2048], P('fsdp'), may hold values from 0 to 7
- observed: int32 [8, 2048], P('fsdp'), may hold values from 0 to 1, as said below
- norm_gains: bfloat16 [4, 1024], P(None, 'fsdp'), may hold values from 0.5 to 2
- var_bias: bfloat16 [32], P('fsdp'), may hold values from -3 to 3
- qkv_weight: bfloat16 [1024, 3072], P('fsdp'), may hold values from -0.1875 to 0.1875
- out_weight: bfloat16 [1024, 1024], P('fsdp'), may hold values from -1 to 1
- ffn_in: bfloat16 [1024, 5632], P('fsdp'), may hold values from -0.1875 to 0.1875
- ffn_out: bfloat16 [2816, 1024], P('fsdp'), may hold values from -0.109375 to 0.109375
Outputs:
- loss: float32 [], replicated
- activations: bfloat16 [8, 2048, 1024], P('fsdp', 'ctx')
- input_grad: float32 [8, 2048, 1024], P('fsdp', 'ctx')
- gains_grad: float32 [4, 1024], P(None, 'fsdp')
- var_bias_grad: float32 [32], P('fsdp')
- qkv_weight_grad: float32 [1024, 3072], P('fsdp')
- out_weight_grad: float32 [1024, 1024], P('fsdp')
- ffn_in_grad: float32 [1024, 5632], P('fsdp')
- ffn_out_grad: float32 [2816, 1024], P('fsdp')
The draws below stay inside these ranges and needn't reach their ends.
Inputs may be any that keep to these rules, and one draw needn't show every extreme that they name: Each sequence's lengths sum to 2048. In each sequence exactly one document has length 1789; all others are at most 64. The first token of every sequence is observed.
All inputs are finite; a program needn't handle non-finite values.
Results may differ from the reference program's by a relative error of at most 0.018.
Values may be sent and summed in bfloat16 or wider, within the bound.
No kernel may reach another device: no remote copies, remote signals or barrier semaphores. Data moves between devices by JAX's collectives and lax.ppermute only.
A program may use at most 192 MiB of HBM per device.

```python
import math
import jax
import jax.numpy as jnp
from jax import lax

D = 1024
HEADS = 16
HEAD = 64
FF = 2816
TOK_DEV = 512
WINDOW = 1024
NDOC = 8
NVAR = 8
SEQS = 8
LENGTH = 2048
TOKENS = 16384


def draw_lengths(key, part):
    key = jax.random.fold_in(key, 11)
    pair_key, order_key = jax.random.split(key)
    quota = TOK_DEV // NDOC
    half_count = (NDOC - 2) // 2
    firsts = jax.random.randint(pair_key, (SEQS, half_count), 1, quota + 1)
    seconds = quota + 1 - firsts
    middle = jnp.full((SEQS, 1), quota, jnp.int32)
    longest = LENGTH - half_count * (quota + 1) - quota
    tail = jnp.full((SEQS, 1), longest, jnp.int32)
    values = jnp.concatenate([firsts, seconds, middle, tail], axis=1).astype(jnp.int32)
    row_keys = jax.random.split(order_key, SEQS)
    shuffled = jax.vmap(lambda one_key, row: jax.random.permutation(one_key, row))(row_keys, values)
    return shuffled.astype(jnp.int32)


def draw_observed(key, part):
    key = jax.random.fold_in(key, 23)
    positions = jnp.arange(LENGTH)[None, :]
    sequence = jnp.arange(SEQS)[:, None]
    permille = (300 + 600 * positions // LENGTH) * (35 + 65 * sequence // max(SEQS - 1, 1)) // 100
    rolled = jax.random.randint(key, (SEQS, LENGTH), 0, 1000)
    observed = (rolled < permille) | (positions == 0)
    return observed.astype(jnp.int32)


def set_ends(drawn, own_key, low, high):
    spot = [jax.random.randint(jax.random.fold_in(own_key, axis), (), 0, length) for axis, length in enumerate(drawn.shape)]
    widest = drawn.shape.index(max(drawn.shape))
    neighbour = spot[:widest] + [(spot[widest] + 1) % drawn.shape[widest]] + spot[widest + 1:]
    return drawn.at[tuple(spot)].set(low).at[tuple(neighbour)].set(high)


def level_of(stream_key, dims, cuts, least, high):
    def one(position, parts):
        heights = jax.random.uniform(jax.random.fold_in(jax.random.fold_in(stream_key, 6), position), (parts,), jnp.float32, least / len(cuts), high / len(cuts))
        return jnp.repeat(jnp.exp(heights), dims[position] // parts).reshape((-1,) + (1,) * (len(dims) - position - 1))

    level = one(*cuts[0])
    for cut in cuts[1:]:
        level = level * one(*cut)
    return level


def bell_draw(own_key, extent, deviation, reach, cuts=(), kind=jnp.bfloat16):
    array = deviation * jax.random.normal(own_key, extent, jnp.float32)
    if cuts:
        array = array * level_of(own_key, extent, cuts, -0.22, 0.18)
    return jnp.clip(array, -reach, reach).astype(kind)


def setup_inputs(seed: int = 0) -> dict:
    streams_of = jax.random.split(jax.random.key(seed), 13)
    tokens = bell_draw(streams_of[0], (SEQS, LENGTH, D), 1.0, 6.0, ((0, 8), (1, 4)))
    teacher = bell_draw(streams_of[1], (SEQS, LENGTH, D), 1.0, 6.0, ((0, 8), (1, 4)))
    cotangent = bell_draw(streams_of[2], (SEQS, LENGTH, D), 1.0, 6.0, ((0, 8), (1, 4)))
    lengths = draw_lengths(jax.random.fold_in(streams_of[12], 71), 0)
    variate = set_ends(jax.random.randint(streams_of[4], (SEQS, LENGTH), 0, NVAR), jax.random.fold_in(streams_of[4], 1), 0, NVAR - 1).astype(jnp.int32)
    observed = draw_observed(jax.random.fold_in(streams_of[12], 71), 0)
    norm_gains = jnp.clip(0.5 + 1.5 * jax.random.uniform(streams_of[6], (4, D), jnp.float32) ** level_of(streams_of[6], (4, D), ((1, 8),), -0.2, 0.2), 0.5, 2.0).astype(jnp.bfloat16)
    var_bias = bell_draw(streams_of[7], (2 * HEADS,), 1.0, 3.0, ((0, 8),))
    qkv_weight = bell_draw(streams_of[8], (D, 3 * D), D ** -0.5, 0.1875, ((0, 8),))
    out_weight = bell_draw(streams_of[9], (D, D), (D // 32) ** -0.5, 1.0, ((0, 8),))
    ffn_in = bell_draw(streams_of[10], (D, 2 * FF), D ** -0.5, 0.1875, ((0, 8),))
    ffn_out = bell_draw(streams_of[11], (FF, D), FF ** -0.5, 0.109375, ((0, 8),))
    return dict(tokens=tokens, teacher=teacher, cotangent=cotangent, lengths=lengths, variate=variate, observed=observed, norm_gains=norm_gains, var_bias=var_bias, qkv_weight=qkv_weight, out_weight=out_weight, ffn_in=ffn_in, ffn_out=ffn_out)


EPSILON = 1e-06
MASKED = -1e+30
HIGHEST = lax.Precision.HIGHEST

@jax.custom_vjp
def low(v):
    return lax.optimization_barrier(v.astype(jnp.bfloat16)).astype(jnp.float32)

@jax.custom_vjp
def low_back(v):
    return v

def low_keep(v):
    return (low(v), None)

def low_pass(kept, grad):
    return (grad,)

def back_keep(v):
    return (v, None)

def back_low(kept, grad):
    return (low(grad),)
low.defvjp(low_keep, low_pass)
low_back.defvjp(back_keep, back_low)

def matmul_full(left, right):
    return jnp.dot(left, right, precision=HIGHEST, preferred_element_type=jnp.float32)

def rms_scale(vector, scales):
    return vector * lax.rsqrt(lax.optimization_barrier(jnp.mean(vector * vector, axis=-1, keepdims=True)) + EPSILON) * scales

def rotary(positions):
    half_dim = HEAD // 2
    frequency = jnp.exp(jnp.arange(half_dim).astype(jnp.float32) * (-2.0 * math.log(10000.0) / HEAD))
    angles = positions.astype(jnp.float32)[:, None] * frequency[None, :]
    return (jnp.cos(angles)[:, None, :], jnp.sin(angles)[:, None, :])

def head_prep(vector, scales, cosine_table, sine_table):
    total_rows = vector.shape[0]
    heads_view = vector.reshape(total_rows, HEADS, HEAD)
    heads_view = heads_view * lax.rsqrt(lax.optimization_barrier(jnp.mean(heads_view * heads_view, axis=-1, keepdims=True)) + EPSILON)
    heads_view = heads_view * scales.reshape(HEADS, HEAD)
    front_half = heads_view[..., :HEAD // 2]
    back_half = heads_view[..., HEAD // 2:]
    turned = jnp.concatenate([front_half * cosine_table - back_half * sine_table, back_half * cosine_table + front_half * sine_table], axis=-1)
    return turned.reshape(total_rows, HEADS * HEAD)

def document_ids(doc_lengths, positions):
    doc_ends = jnp.cumsum(doc_lengths)
    return lax.optimization_barrier(jnp.sum((positions[:, None] >= doc_ends[None, :]).astype(jnp.int32), axis=1))

def seq_attention(query_rot, key_rot, value_low, bias_all, doc_lengths, variate_ids, observed_ids):
    seq_len = query_rot.shape[0]
    half_span = WINDOW // 2
    block_rows = min(512, seq_len)
    key_rows = block_rows + 2 * half_span
    scale_factor = HEAD ** (-0.5)
    query_pos = jnp.arange(seq_len, dtype=jnp.int32)
    query_doc = document_ids(doc_lengths, query_pos)
    key_pos = jnp.arange(seq_len + 2 * half_span, dtype=jnp.int32) - half_span
    key_doc = document_ids(doc_lengths, key_pos)
    key_var = jnp.pad(variate_ids, half_span)
    key_obs = jnp.pad(observed_ids, half_span)
    key_pad = jnp.pad(key_rot, ((half_span, half_span), (0, 0)))
    value_pad = jnp.pad(value_low, ((half_span, half_span), (0, 0)))

    def one_block(index):
        offset = (index * block_rows).astype(jnp.int32)
        queries = lax.dynamic_slice_in_dim(query_rot, offset, block_rows, 0).reshape(block_rows, HEADS, HEAD)
        keys_blk = lax.dynamic_slice_in_dim(key_pad, offset, key_rows, 0).reshape(key_rows, HEADS, HEAD)
        values_blk = lax.dynamic_slice_in_dim(value_pad, offset, key_rows, 0).reshape(key_rows, HEADS, HEAD)
        qpos_blk = lax.dynamic_slice_in_dim(query_pos, offset, block_rows, 0)
        qdoc_blk = lax.dynamic_slice_in_dim(query_doc, offset, block_rows, 0)
        qvar_blk = lax.dynamic_slice_in_dim(variate_ids, offset, block_rows, 0)
        kpos_blk = lax.dynamic_slice_in_dim(key_pos, offset, key_rows, 0)
        kdoc_blk = lax.dynamic_slice_in_dim(key_doc, offset, key_rows, 0)
        kvar_blk = lax.dynamic_slice_in_dim(key_var, offset, key_rows, 0)
        kobs_blk = lax.dynamic_slice_in_dim(key_obs, offset, key_rows, 0)
        relative = kpos_blk[None, :] - qpos_blk[:, None]
        inside = (kpos_blk >= 0) & (kpos_blk < seq_len)
        allowed = (jnp.abs(relative) <= half_span) & (kdoc_blk[None, :] == qdoc_blk[:, None]) & inside[None, :]
        allowed = allowed & ((kobs_blk[None, :] == 1) | (relative == 0))
        same_var = kvar_blk[None, :] == qvar_blk[:, None]
        raw = low_back(jnp.einsum('qhd,khd->hqk', queries, keys_blk, precision=HIGHEST))
        scores = raw * scale_factor + jnp.where(same_var[None], bias_all[:HEADS, None, None], bias_all[HEADS:, None, None])
        scores = jnp.where(allowed[None], scores, MASKED)
        top_score = lax.optimization_barrier(jnp.max(scores, axis=-1, keepdims=True))
        expo = jnp.exp(scores - top_score)
        prob_low = low(expo / lax.optimization_barrier(jnp.sum(expo, axis=-1, keepdims=True)))
        result = jnp.einsum('hqk,khd->qhd', prob_low, values_blk, precision=HIGHEST)
        return result.reshape(block_rows, HEADS * HEAD)
    outputs = lax.map(jax.checkpoint(one_block), jnp.arange(seq_len // block_rows).astype(jnp.int32))
    return outputs.reshape(seq_len, HEADS * HEAD)

def gated_unit(gate_up):
    gate_part = gate_up[:, :FF]
    up_part = gate_up[:, FF:]
    return gate_part / (1.0 + jnp.exp(-gate_part)) * up_part

def one_layer(inputs, gains_f, bias_f, w_qkv, w_attn, w_upper, w_lower, doc_lengths, variate_ids, observed_ids):
    seq_len = inputs.shape[0]
    normed = low(rms_scale(inputs, gains_f[0]))
    projected = low_back(matmul_full(normed, w_qkv))
    cosine_table, sine_table = rotary(jnp.arange(seq_len, dtype=jnp.int32))
    query_rot = low(head_prep(projected[:, :D], gains_f[2], cosine_table, sine_table))
    key_rot = low(head_prep(projected[:, D:2 * D], gains_f[3], cosine_table, sine_table))
    value_low = low(projected[:, 2 * D:])
    attended = seq_attention(query_rot, key_rot, value_low, bias_f, doc_lengths, variate_ids, observed_ids)
    attn = low(low_back(attended))
    mixed = inputs + low_back(matmul_full(attn, w_attn))
    normed_two = low(rms_scale(mixed, gains_f[1]))
    gate_up = low_back(matmul_full(normed_two, w_upper))
    hidden = low(gated_unit(gate_up))
    return mixed + low_back(matmul_full(hidden, w_lower))

def reference(tokens, teacher, cotangent, lengths, variate, observed, norm_gains, var_bias, qkv_weight, out_weight, ffn_in, ffn_out):

    def forward(inputs, gains_f, bias_f, w_qkv, w_attn, w_upper, w_lower):

        def per_sequence(packed):
            seq_inputs, doc_lengths, variate_ids, observed_ids = packed
            return one_layer(seq_inputs, gains_f, bias_f, w_qkv, w_attn, w_upper, w_lower, doc_lengths, variate_ids, observed_ids)
        return lax.map(jax.checkpoint(per_sequence), (inputs, lengths, variate, observed))
    final, pull_back = jax.vjp(forward, tokens.astype(jnp.float32), norm_gains.astype(jnp.float32), var_bias.astype(jnp.float32), qkv_weight.astype(jnp.float32), out_weight.astype(jnp.float32), ffn_in.astype(jnp.float32), ffn_out.astype(jnp.float32))
    valid_col = observed.astype(jnp.float32)[..., None]
    valid_total = jnp.sum(observed.astype(jnp.float32))
    distance = final - teacher.astype(jnp.float32)
    loss = jnp.sum(valid_col * distance * distance) / (valid_total * D)
    d_final = cotangent.astype(jnp.float32) + TOKENS * valid_col * distance / valid_total
    grads = pull_back(d_final)
    return (loss, final.astype(jnp.bfloat16), grads[0], grads[1], grads[2], grads[3], grads[4], grads[5], grads[6])
```

```python
import math

import jax
import jax.numpy as jnp
from jax import lax
from jax.experimental import pallas as pl
from jax.experimental.pallas import tpu as pltpu
from jax.sharding import PartitionSpec as P


D=1024; HEADS=16; HEAD=64; FF=2816; WINDOW=1024
EPSILON=1e-6; MASKED=-1e30
HALF=WINDOW//2
LANES=128
VAR_AT, LSE_AT, OBS_AT = 8, 32, 35
TILE=256
F32=jnp.float32; BF=jnp.bfloat16


def dot_nn(a,b): return lax.dot_general(a,b,(((1,),(0,)),((),())),preferred_element_type=F32)
def dot_nt(a,b): return lax.dot_general(a,b,(((1,),(1,)),((),())),preferred_element_type=F32)
def dot_tn(a,b): return lax.dot_general(a,b,(((0,),(0,)),((),())),preferred_element_type=F32)

def halves(v):
    high=v.astype(BF)
    return jnp.concatenate([high,(v-high.astype(F32)).astype(BF)],axis=1)

def thirds(v,rounded=lambda a: a.astype(BF).astype(F32)):
    high=rounded(v)
    rest=v-high
    mid=rounded(rest)
    return high,mid,rest-mid

def lane_of(shape): return lax.broadcasted_iota(jnp.int32,shape,1)

def place(v,at):
    high,mid,low=thirds(v)
    lane=lane_of(v.shape)%HEAD
    return jnp.where(lane==at,high,jnp.where(lane==at+1,mid,jnp.where(lane==at+2,low,0.0)))

def band(s,t,tiles,key_axis):
    if t not in (0,tiles-1): return s
    key=lax.broadcasted_iota(jnp.int32,s.shape,key_axis)
    query=lax.broadcasted_iota(jnp.int32,s.shape,1-key_axis)
    keep=key>=query if t==0 else key<=query
    return jnp.where(keep,s,MASKED)

def prep(u,gain,cosine,sine,mean_mat,swap_mat):
    mean=dot_nn(halves(u*u),mean_mat)
    c=lax.rsqrt(mean+EPSILON)
    n=u*c*gain
    return n*cosine+dot_nn(halves(n),swap_mat)*sine, c

def fwd_kernel(xn_ref,wq_ref,wk_ref,wv_ref,gq_ref,gk_ref,cos_ref,sin_ref,qb_ref,kb_ref,sv_ref,mean_ref,swap_ref,
               q_ref,k_ref,v_ref,attn_ref,lse_ref,cq_ref,ck_ref):
    rows=qb_ref.shape[0]; ext=kb_ref.shape[0]
    tiles=2*HALF//TILE+1
    mean_mat=mean_ref[...]; swap_mat=swap_ref[...]
    first=(lane_of((1,LANES))<HEAD)
    kf=dot_nn(xn_ref[...],wk_ref[...])
    for pair in range(2):
        col=slice(pair*LANES,(pair+1)*LANES)
        rot,c=prep(kf[:,col],gk_ref[:,col],cos_ref[...],sin_ref[...],mean_mat,swap_mat)
        k_ref[:,col]=rot.astype(BF)
        if pair==0: ck_ref[...]=c
        else: ck_ref[...]=jnp.where(lane_of((1,LANES))%HEAD==pair,c,ck_ref[...])
    v_ref[...]=dot_nn(xn_ref[...],wv_ref[...]).astype(BF)
    qf=dot_nn(xn_ref[HALF:HALF+rows,:],wq_ref[...])
    for pair in range(2):
        col=slice(pair*LANES,(pair+1)*LANES)
        rot,c=prep(qf[:,col],gq_ref[:,col],cos_ref[HALF:HALF+rows,:],sin_ref[HALF:HALF+rows,:],mean_mat,swap_mat)
        q_ref[:,col]=rot.astype(BF)
        if pair==0: cq_ref[...]=c
        else: cq_ref[...]=jnp.where(lane_of((1,LANES))%HEAD==pair,c,cq_ref[...])
    own=[first.astype(F32).astype(BF),(1.0-first.astype(F32)).astype(BF)]
    no_obs=(lane_of((1,LANES))%HEAD!=OBS_AT).astype(F32).astype(BF)
    diag=lax.broadcasted_iota(jnp.int32,(TILE,TILE),0)==lax.broadcasted_iota(jnp.int32,(TILE,TILE),1)
    for pair in range(2):
        col=slice(pair*LANES,(pair+1)*LANES)
        for i in range(rows//TILE):
            sums=[]
            for par in range(2):
                m,other=own[par],own[1-par]
                sv=sv_ref[2*pair+par:2*pair+par+1,:].astype(BF)*other
                qi=q_ref[i*TILE:(i+1)*TILE,col]*BF(HEAD**-0.5)*m+qb_ref[i*TILE:(i+1)*TILE,:]*sv
                acc=None
                for t in range(tiles):
                    at=slice((i+t)*TILE,(i+t+1)*TILE)
                    kt=k_ref[at,col]*m+kb_ref[at,:]*other
                    vt=v_ref[at,col]*m+other
                    s=band(dot_nt(qi,kt),t,tiles,1)
                    if t==tiles//2:
                        s=jnp.where(diag,dot_nt(qi*(m+other*no_obs),kt),s)
                    p=jnp.exp(s).astype(BF)
                    o=dot_nn(p,vt)
                    acc=o if acc is None else acc+o
                sums.append(acc)
            total=jnp.where(first,sums[1],sums[0])
            lse_ref[i*TILE:(i+1)*TILE,col]=jnp.log(total)
            out=jnp.where(first,sums[0],sums[1])/pltpu.roll(total,HEAD,1)
            attn_ref[i*TILE:(i+1)*TILE,col]=out.astype(BF)

def prep_back(rot,d_rot,c,gain,cosine,sine,mean_mat,swap_mat):
    x=rot.astype(F32)
    m=dot_nn(halves(x*d_rot),mean_mat)
    e=d_rot*cosine-dot_nn(halves(d_rot),swap_mat)*sine
    swapped=dot_nn(rot,swap_mat[:LANES])
    n=(x*cosine-swapped*sine)/gain
    return c*(gain*e-n*m), jnp.sum(e*n,axis=0,keepdims=True)

def bwd_kernel(q_ref,k_ref,v_ref,do_ref,attn_ref,lse_ref,cq_ref,ck_ref,gq_ref,gk_ref,cos_ref,sin_ref,qb_ref,kb_ref,sv_ref,
               mean_ref,swap_ref,cross_ref,spread_ref,
               dq_ref,dk_ref,dv_ref,dgq_ref,dgk_ref,bias_ref,dk_acc,dv_acc,ke_ref,ve_ref):
    rows=qb_ref.shape[0]; ext=kb_ref.shape[0]
    tiles=2*HALF//TILE+1
    mean_mat=mean_ref[...]; swap_mat=swap_ref[...]
    first=(lane_of((1,LANES))<HEAD)
    own=[first.astype(F32).astype(BF),(1.0-first.astype(F32)).astype(BF)]
    no_obs=(lane_of((1,LANES))%HEAD!=OBS_AT).astype(F32).astype(BF)
    diag=lax.broadcasted_iota(jnp.int32,(TILE,TILE),0)==lax.broadcasted_iota(jnp.int32,(TILE,TILE),1)
    lane=lane_of((1,LANES))%HEAD
    is_var=(lane>=VAR_AT)&(lane<VAR_AT+8)
    bias_ref[...]=jnp.zeros_like(bias_ref)
    def one_pair(pair,_):
        col=pl.ds(pl.multiple_of(pair*LANES,LANES),LANES)
        dk_acc[...]=jnp.zeros_like(dk_acc)
        dv_acc[...]=jnp.zeros_like(dv_acc)
        prod=do_ref[:,col].astype(F32)*attn_ref[:,col].astype(F32)
        delta=place(dot_nn(halves(prod),cross_ref[...]),0).astype(BF)
        lse=place(lse_ref[:,col],LSE_AT).astype(BF)
        dqs=[]
        for par in range(2):
            m,other=own[par],own[1-par]
            head=2*pair+par
            sv=sv_ref[pl.ds(head,1),:].astype(BF)*other
            qm=q_ref[:,col]*BF(HEAD**-0.5)*m
            qe=qm+qb_ref[...]*sv-lse*other
            dm=do_ref[:,col]*m
            de=dm-delta*other
            ke_ref[...]=k_ref[:,col]*m+kb_ref[...]*other
            ve_ref[...]=v_ref[:,col]*m+other
            parts=[]
            for i in range(rows//TILE):
                r=slice(i*TILE,(i+1)*TILE)
                dq=None
                for t in range(tiles):
                    at=slice((i+t)*TILE,(i+t+1)*TILE)
                    kt=ke_ref[at,:]
                    s=band(dot_nt(kt,qe[r]),t,tiles,0)
                    if t==tiles//2:
                        s=jnp.where(diag,dot_nt(kt,qe[r]*(m+other*no_obs)),s)
                    p=jnp.exp(s)
                    ds=(p*dot_nt(ve_ref[at,:],de[r])).astype(BF)
                    dv_acc[at,:]+=dot_nn(p.astype(BF),dm[r])
                    dk_acc[at,:]+=dot_nn(ds,qm[r])
                    part=dot_tn(ds,kt)
                    dq=part if dq is None else dq+part
                parts.append(dq)
            dq=jnp.concatenate(parts,axis=0)
            hot=jnp.where(is_var&(first!=(par==0)),dq*qb_ref[...].astype(F32),0.0)
            bias_ref[pl.ds(head,1),:]=jnp.sum(hot,axis=0,keepdims=True)
            dqs.append(dq)
        d_rot=jnp.where(first,dqs[0],dqs[1])*(HEAD**-0.5)
        spread=spread_ref[pair]
        cosq,sinq=cos_ref[HALF:HALF+rows,:],sin_ref[HALF:HALF+rows,:]
        du,dg=prep_back(q_ref[:,col],d_rot,dot_nn(halves(cq_ref[...]),spread),gq_ref[:,col],cosq,sinq,mean_mat,swap_mat)
        dq_ref[:,col]=du.astype(BF)
        dgq_ref[:,col]=dg
        du,dg=prep_back(k_ref[:,col],dk_acc[...],dot_nn(halves(ck_ref[...]),spread),gk_ref[:,col],cos_ref[...],sin_ref[...],mean_mat,swap_mat)
        dk_ref[:,col]=du.astype(BF)
        dgk_ref[:,col]=dg
        dv_ref[:,col]=dv_acc[...].astype(BF)
        return 0
    lax.fori_loop(0,2,one_pair,0)

def blockdiag():
    i=jnp.arange(LANES)
    mean=jnp.where(i[:,None]//HEAD==i[None]//HEAD,1.0/HEAD,0.0)
    cross=jnp.where(i[:,None]//HEAD!=i[None]//HEAD,1.0,0.0)
    swap=jnp.where(i[None]==i[:,None]+jnp.where(i[:,None]%HEAD<HEAD//2,HEAD//2,-(HEAD//2)),1.0,0.0)
    spread=jnp.stack([jnp.where(i[:,None]==pair+HEAD*(i[None]//HEAD),1.0,0.0) for pair in range(2)])
    two=lambda a: jnp.concatenate([a,a],axis=-2).astype(BF)
    return two(mean),two(swap),two(cross),two(spread)

def full(*shape):
    n=len(shape)
    return pl.BlockSpec(shape,lambda j:(0,)*n)
def colb(rows,width,off=0): return pl.BlockSpec((rows,width),lambda j:(0,j+off))
def lead(*shape): return pl.BlockSpec((None,)+shape,lambda j:(j,)+(0,)*len(shape))

def attention_forward(xn,w_qkv,gq,gk,cos,sin,qb,kb,sv,mats,groups=4):
    rows,ext=qb.shape[0],kb.shape[0]
    mean_mat,swap_mat,_,_=mats
    n=groups*256
    return pl.pallas_call(
        fwd_kernel,grid=(groups,),
        in_specs=[full(ext,D),colb(D,256),colb(D,256,groups),colb(D,256,2*groups),lead(1,256),lead(1,256),full(ext,LANES),full(ext,LANES),
                  full(rows,LANES),full(ext,LANES),lead(8,LANES),full(2*LANES,LANES),full(2*LANES,LANES)],
        out_specs=[colb(rows,256),colb(ext,256),colb(ext,256),colb(rows,256),colb(rows,256),lead(rows,LANES),lead(ext,LANES)],
        out_shape=[jax.ShapeDtypeStruct((rows,n),BF),jax.ShapeDtypeStruct((ext,n),BF),jax.ShapeDtypeStruct((ext,n),BF),
                   jax.ShapeDtypeStruct((rows,n),BF),jax.ShapeDtypeStruct((rows,n),F32),
                   jax.ShapeDtypeStruct((groups,rows,LANES),F32),jax.ShapeDtypeStruct((groups,ext,LANES),F32)],
        compiler_params=pltpu.CompilerParams(vmem_limit_bytes=56*2**20),
        name="attention_forward",
    )(xn,w_qkv,w_qkv,w_qkv,gq,gk,cos,sin,qb,kb,sv,mean_mat,swap_mat)

def attention_backward(q,k,v,do,attn,lse,cq,ck,gq,gk,cos,sin,qb,kb,sv,mats,groups=4):
    rows,ext=qb.shape[0],kb.shape[0]
    n=groups*256
    return pl.pallas_call(
        bwd_kernel,grid=(groups,),
        in_specs=[colb(rows,256),colb(ext,256),colb(ext,256),colb(rows,256),colb(rows,256),colb(rows,256),lead(rows,LANES),lead(ext,LANES),
                  lead(1,256),lead(1,256),full(ext,LANES),full(ext,LANES),full(rows,LANES),full(ext,LANES),lead(8,LANES),
                  full(2*LANES,LANES),full(2*LANES,LANES),full(2*LANES,LANES),full(2,2*LANES,LANES)],
        out_specs=[colb(rows,256),colb(ext,256),colb(ext,256),lead(1,256),lead(1,256),lead(8,LANES)],
        out_shape=[jax.ShapeDtypeStruct((rows,n),BF),jax.ShapeDtypeStruct((ext,n),BF),jax.ShapeDtypeStruct((ext,n),BF),
                   jax.ShapeDtypeStruct((groups,1,256),F32),jax.ShapeDtypeStruct((groups,1,256),F32),jax.ShapeDtypeStruct((groups,8,LANES),F32)],
        scratch_shapes=[pltpu.VMEM((ext,LANES),F32),pltpu.VMEM((ext,LANES),F32),pltpu.VMEM((ext,LANES),BF),pltpu.VMEM((ext,LANES),BF)],
        compiler_params=pltpu.CompilerParams(vmem_limit_bytes=56*2**20),
        name="attention_backward",
    )(q,k,v,do,attn,lse,cq,ck,gq,gk,cos,sin,qb,kb,sv,*mats)

def features(query_doc,query_var,key_doc,key_var,key_obs,key_inside):
    lane=jnp.arange(HEAD)[None,:]
    var_lane=(lane>=VAR_AT)&(lane<LSE_AT)
    def tile(a): return jnp.concatenate([a,a],axis=1).astype(BF)
    qv=var_lane&((lane-VAR_AT)%8==query_var[:,None])
    q=((lane<VAR_AT)&(lane==query_doc[:,None]))|qv|(lane==OBS_AT)
    kv=var_lane&((lane-VAR_AT)%8==key_var[:,None])
    closed=(lane<VAR_AT)&~((lane==key_doc[:,None])&key_inside[:,None])
    closed=closed|((lane==OBS_AT)&(key_obs[:,None]!=1))
    ones=kv|((lane>=LSE_AT)&(lane<LSE_AT+3))
    k=jnp.where(closed,MASKED,jnp.where(ones,1.0,0.0))
    return tile(q.astype(F32)),tile(k)

def head_scales(bias_f):
    high,mid,low=thirds(bias_f[:HEADS]-bias_f[HEADS:],lambda a: lax.reduce_precision(a,8,7))
    lane=jnp.arange(HEAD)[None,:]
    part=lambda a: a[:,None]
    s=jnp.where(lane<VAR_AT,1.0,jnp.where(lane<VAR_AT+8,part(high),jnp.where(lane<VAR_AT+16,part(mid),jnp.where(lane<LSE_AT,part(low),1.0))))
    s=jnp.where(lane>OBS_AT,0.0,s)
    s=jnp.concatenate([s,s],axis=1).reshape(HEADS//4,4,LANES)
    return jnp.concatenate([s,jnp.zeros_like(s)],axis=1)

def tables(pos):
    half=HEAD//2
    freq=jnp.exp(jnp.arange(half).astype(F32)*(-2.0*math.log(10000.0)/HEAD))
    ang=pos.astype(F32)[:,None]*freq[None,:]
    c,s=jnp.cos(ang),jnp.sin(ang)
    return jnp.concatenate([c,c,c,c],axis=1),jnp.concatenate([-s,s,-s,s],axis=1)


def shifted(shard, by):
    size = lax.axis_size("ctx")
    return lax.ppermute(shard, "ctx", [(i, i + by) for i in range(size) if 0 <= i + by < size])


def document_ids(doc_lengths, positions):
    doc_ends = jnp.cumsum(doc_lengths)
    return jnp.sum((positions[:, None] >= doc_ends[None, :]).astype(jnp.int32), axis=1)


def rms_scale(vector, scales):
    return vector * lax.rsqrt(jnp.mean(vector * vector, axis=-1, keepdims=True) + EPSILON) * scales


def gated_unit(gate_up):
    gate_part = gate_up[:, :FF]
    up_part = gate_up[:, FF:]
    return gate_part / (1.0 + jnp.exp(-gate_part)) * up_part


def per_device(tokens, teacher, cotangent, lengths, variate, observed, norm_gains, var_bias, qkv_weight, out_weight, ffn_in, ffn_out):
    rows = tokens.shape[1]
    n_context = lax.axis_size("ctx")
    n_shards = lax.axis_size("fsdp")
    ext = rows + 2 * HALF
    start = lax.axis_index("ctx") * rows
    seq_len = observed.shape[1]
    gains_n = norm_gains.shape[1]
    bias_n = var_bias.shape[0]

    own_count = jnp.sum(observed[0])
    small = jnp.zeros((16, gains_n), BF)
    small = small.at[:4].set(norm_gains).at[4, :bias_n].set(var_bias)
    small = small.at[5, 0].set((own_count // 256).astype(BF)).at[5, 1].set((own_count % 256).astype(BF))
    before, after = shifted(tokens[0], 1), shifted(tokens[0], -1)
    w_qkv = lax.all_gather(qkv_weight, "fsdp", axis=0, tiled=True)
    small = lax.all_gather(small, "fsdp", axis=0)
    w_attn = lax.all_gather(out_weight, "fsdp", axis=0, tiled=True)
    w_upper = lax.all_gather(ffn_in, "fsdp", axis=0, tiled=True)
    w_lower = lax.all_gather(ffn_out, "fsdp", axis=0, tiled=True)

    gains = jnp.moveaxis(small[:, :4], 0, 1).reshape(4, D).astype(F32)
    bias = small[:, 4, :bias_n].reshape(2 * HEADS).astype(F32)
    valid_total = jnp.sum(small[:, 5, 0].astype(F32) * 256.0 + small[:, 5, 1].astype(F32))

    key_pos = start - HALF + jnp.arange(ext, dtype=jnp.int32)
    inside = (key_pos >= 0) & (key_pos < seq_len)
    key_doc = document_ids(lengths[0], key_pos)
    key_var = lax.dynamic_slice_in_dim(jnp.pad(variate[0], HALF), start, ext, 0)
    key_obs = lax.dynamic_slice_in_dim(jnp.pad(observed[0], HALF), start, ext, 0)
    own = slice(HALF, HALF + rows)
    query_feat, key_feat = features(key_doc[own], key_var[own], key_doc, key_var, key_obs, inside)
    cosine, sine = tables(key_pos)
    scales = head_scales(bias)
    mats = blockdiag()
    gain_q, gain_k = gains[2].reshape(-1, 1, 256), gains[3].reshape(-1, 1, 256)

    inputs = jnp.concatenate([before, tokens[0], after], axis=0).astype(F32)
    inv = lax.rsqrt(jnp.mean(inputs * inputs, axis=-1, keepdims=True) + EPSILON)
    normed = (inputs * inv * gains[0]).astype(BF)

    q, k, v, attn, lse, c_q, c_k = attention_forward(normed, w_qkv, gain_q, gain_k, cosine, sine, query_feat, key_feat, scales, mats)
    mixed = tokens[0].astype(F32) + jnp.dot(attn, w_attn, preferred_element_type=F32)
    normed_two_f, norm_two_pull = jax.vjp(rms_scale, mixed, gains[1])
    normed_two = normed_two_f.astype(BF)
    gate_up = jnp.dot(normed_two, w_upper, preferred_element_type=F32)
    hidden_f, glu_pull = jax.vjp(gated_unit, gate_up)
    hidden = hidden_f.astype(BF)
    final = mixed + jnp.dot(hidden, w_lower, preferred_element_type=F32)
    valid_col = key_obs[own].astype(F32)[:, None]
    distance = final - teacher[0].astype(F32)
    squared = jnp.sum(valid_col * distance * distance)
    all_tokens = rows * n_context * n_shards
    d_final = cotangent[0].astype(F32) + all_tokens * valid_col * distance / valid_total
    d_final_low = d_final.astype(BF)
    grad_lower = dot_tn(hidden, d_final_low)
    ffn_out_part = lax.psum_scatter(grad_lower.astype(BF), "fsdp", scatter_dimension=0, tiled=True)
    d_hidden = dot_nt(d_final_low, w_lower)
    (d_gate_up,) = glu_pull(d_hidden)
    d_gate_low = d_gate_up.astype(BF)
    grad_upper = dot_tn(normed_two, d_gate_low)
    ffn_in_part = lax.psum_scatter(grad_upper.astype(BF), "fsdp", scatter_dimension=0, tiled=True)
    d_normed_two = dot_nt(d_gate_low, w_upper)
    d_mixed_part, grad_norm_two = norm_two_pull(d_normed_two)
    d_mixed = d_final + d_mixed_part
    d_mixed_low = d_mixed.astype(BF)
    d_attn = dot_nt(d_mixed_low, w_attn).astype(BF)
    grad_attn = dot_tn(attn, d_mixed_low)
    out_part = lax.psum_scatter(grad_attn.astype(BF), "fsdp", scatter_dimension=0, tiled=True)

    d_q, d_k, d_v, d_gain_q, d_gain_k, d_bias = attention_backward(
        q, k, v, d_attn, attn, lse, c_q, c_k, gain_q, gain_k, cosine, sine, query_feat, key_feat, scales, mats
    )
    grad_qkv = jnp.concatenate(
        [dot_tn(normed[own], d_q).astype(BF), dot_tn(normed, d_k).astype(BF), dot_tn(normed, d_v).astype(BF)], axis=1
    )
    qkv_part = lax.psum_scatter(grad_qkv, "fsdp", scatter_dimension=0, tiled=True)
    d_ext = dot_nt(d_k, w_qkv[:, D : 2 * D]) + dot_nt(d_v, w_qkv[:, 2 * D :])
    from_next = shifted(d_ext[:HALF].astype(BF), -1)
    from_prev = shifted(d_ext[HALF + rows :].astype(BF), 1)
    d_own = d_ext[own] + dot_nt(d_q, w_qkv[:, :D])
    unit = inputs * inv
    grad_norm_one = (
        jnp.sum(d_own * unit[own], axis=0)
        + jnp.sum(d_ext[:HALF] * unit[:HALF], axis=0)
        + jnp.sum(d_ext[HALF + rows :] * unit[HALF + rows :], axis=0)
    )
    d_own = d_own.at[rows - HALF :].add(from_next.astype(F32)).at[:HALF].add(from_prev.astype(F32))
    scaled = d_own * gains[0]
    input_grad = d_mixed + inv[own] * (scaled - unit[own] * jnp.mean(unit[own] * scaled, axis=-1, keepdims=True))

    same = jnp.sum(d_bias[:, :4], axis=-1).reshape(HEADS)
    sums = jnp.concatenate(
        [grad_norm_one, grad_norm_two, d_gain_q.reshape(D), d_gain_k.reshape(D), same, jnp.full((LANES,), squared)]
    )
    sums = lax.psum(jnp.pad(sums, (0, -sums.shape[0] % (8 * LANES))).reshape(-1, LANES), ("ctx", "fsdp")).reshape(-1)
    loss = sums[4 * D + HEADS] / (valid_total * D)
    me = lax.axis_index("fsdp")
    gains_grad = lax.dynamic_slice_in_dim(sums[: 4 * D].reshape(4, D), me * gains_n, gains_n, 1)
    bias_sum = sums[4 * D : 4 * D + HEADS]
    var_bias_grad = lax.dynamic_slice_in_dim(jnp.concatenate([bias_sum, -bias_sum]), me * bias_n, bias_n, 0)
    qkv_grad, out_grad, in_grad, low_grad = lax.psum((qkv_part, out_part, ffn_in_part, ffn_out_part), "ctx")
    return (
        loss,
        final.astype(BF)[None],
        input_grad[None],
        gains_grad,
        var_bias_grad,
        qkv_grad.astype(F32),
        out_grad.astype(F32),
        in_grad.astype(F32),
        low_grad.astype(F32),
    )


def solution(mesh):
    split = P("fsdp", "ctx", None)
    rows = P("fsdp", None)
    return jax.shard_map(
        per_device,
        mesh=mesh,
        in_specs=(split, split, split, rows, rows, rows, P(None, "fsdp"), P("fsdp"), rows, rows, rows, rows),
        out_specs=(P(), split, split, P(None, "fsdp"), P("fsdp"), rows, rows, rows, rows),
        check_vma=False,
    )
```

```python
import math

import jax
import jax.numpy as jnp
import numpy as np
from jax import lax
from jax.experimental import pallas as pl
from jax.experimental.pallas import tpu as pltpu
from jax.sharding import PartitionSpec as P


D=1024; HEADS=16; HEAD=64; FF=2816; WINDOW=1024
EPSILON=1e-6; MASKED=-1e30
HALF=WINDOW//2
LANES=128
VAR_AT, LSE_AT, OBS_AT = 8, 32, 35
TILE=256
F32=jnp.float32; BF=jnp.bfloat16


def dot_nn(a,b): return lax.dot_general(a,b,(((1,),(0,)),((),())),preferred_element_type=F32)
def dot_nt(a,b): return lax.dot_general(a,b,(((1,),(1,)),((),())),preferred_element_type=F32)
def dot_tn(a,b): return lax.dot_general(a,b,(((0,),(0,)),((),())),preferred_element_type=F32)

def halves(v):
    high=v.astype(BF)
    return jnp.concatenate([high,(v-high.astype(F32)).astype(BF)],axis=1)

def thirds(v,rounded=lambda a: a.astype(BF).astype(F32)):
    high=rounded(v)
    rest=v-high
    mid=rounded(rest)
    return high,mid,rest-mid

def lane_of(shape): return lax.broadcasted_iota(jnp.int32,shape,1)

def place(v,at):
    high,mid,low=thirds(v)
    lane=lane_of(v.shape)%HEAD
    return jnp.where(lane==at,high,jnp.where(lane==at+1,mid,jnp.where(lane==at+2,low,0.0)))

def band(s,t,tiles,key_axis):
    if t not in (0,tiles-1): return s
    key=lax.broadcasted_iota(jnp.int32,s.shape,key_axis)
    query=lax.broadcasted_iota(jnp.int32,s.shape,1-key_axis)
    keep=key>=query if t==0 else key<=query
    return jnp.where(keep,s,MASKED)

def prep(u,gain,cosine,sine,mean_mat,swap_mat):
    mean=dot_nn(halves(u*u),mean_mat)
    c=lax.rsqrt(mean+EPSILON)
    n=u*c*gain
    return n*cosine+dot_nn(halves(n),swap_mat)*sine, c

QUADS=4
SEND_ORDER=(3,1,2,0)
def position(slot): return jnp.where(slot==0,3,jnp.where(slot==3,0,slot))

def piece_copies(place_ref,pieces,w_ref,sem):
    me,core=place_ref[0],place_ref[1]
    half=w_ref.shape[1]//2
    copies=[[pltpu.make_async_copy(pieces[0],w_ref.at[me],sem.at[0])]]
    for slot in range(1,QUADS):
        copies.append([pltpu.make_async_copy(pieces[2*slot-1+side],
            w_ref.at[me^slot,pl.ds(pl.multiple_of((core if side==0 else 1-core)*half,half),half),:],sem.at[2*slot-1+side]) for side in range(2)])
    return copies

def await_quarter(place_ref,pieces,w_ref,sem):
    step=pl.program_id(0)
    copies=piece_copies(place_ref,pieces,w_ref,sem)
    @pl.when(step==0)
    def _():
        for group in copies:
            for copy in group: copy.start()
    slot=step^place_ref[0]
    for i,group in enumerate(copies):
        @pl.when(slot==i)
        def _(group=group):
            for copy in group: copy.wait()

def fwd_kernel(place_ref,xn_ref,p0,p1,p2,p3,p4,p5,p6,gq_ref,gk_ref,cos_ref,sin_ref,qb_ref,kb_ref,sv_ref,mean_ref,swap_ref,
               q_ref,k_ref,v_ref,attn_ref,lse_ref,cq_ref,ck_ref,wq_out,wkv_out,wattn_out,w_ref,sem):
    rows=qb_ref.shape[0]; ext=kb_ref.shape[0]
    await_quarter(place_ref,(p0,p1,p2,p3,p4,p5,p6),w_ref,sem)
    quad=pl.program_id(0)
    wq_out[...]=w_ref[quad,:,0:256]
    wkv_out[...]=w_ref[quad,:,256:768]
    wattn_out[...]=w_ref[quad,:,768:1024]
    tiles=2*HALF//TILE+1
    mean_mat=mean_ref[...]; swap_mat=swap_ref[...]
    first=(lane_of((1,LANES))<HEAD)
    kf=dot_nn(xn_ref[...],w_ref[quad,:,256:512])
    for pair in range(2):
        col=slice(pair*LANES,(pair+1)*LANES)
        rot,c=prep(kf[:,col],gk_ref[:,col],cos_ref[...],sin_ref[...],mean_mat,swap_mat)
        k_ref[:,col]=rot.astype(BF)
        if pair==0: ck_ref[...]=c
        else: ck_ref[...]=jnp.where(lane_of((1,LANES))%HEAD==pair,c,ck_ref[...])
    v_ref[...]=dot_nn(xn_ref[...],w_ref[quad,:,512:768]).astype(BF)
    qf=dot_nn(xn_ref[HALF:HALF+rows,:],w_ref[quad,:,0:256])
    for pair in range(2):
        col=slice(pair*LANES,(pair+1)*LANES)
        rot,c=prep(qf[:,col],gq_ref[:,col],cos_ref[HALF:HALF+rows,:],sin_ref[HALF:HALF+rows,:],mean_mat,swap_mat)
        q_ref[:,col]=rot.astype(BF)
        if pair==0: cq_ref[...]=c
        else: cq_ref[...]=jnp.where(lane_of((1,LANES))%HEAD==pair,c,cq_ref[...])
    own=[first.astype(F32).astype(BF),(1.0-first.astype(F32)).astype(BF)]
    no_obs=(lane_of((1,LANES))%HEAD!=OBS_AT).astype(F32).astype(BF)
    diag=lax.broadcasted_iota(jnp.int32,(TILE,TILE),0)==lax.broadcasted_iota(jnp.int32,(TILE,TILE),1)
    for pair in range(2):
        col=slice(pair*LANES,(pair+1)*LANES)
        for i in range(rows//TILE):
            sums=[]
            for par in range(2):
                m,other=own[par],own[1-par]
                sv=sv_ref[2*pair+par:2*pair+par+1,:].astype(BF)*other
                qi=q_ref[i*TILE:(i+1)*TILE,col]*BF(HEAD**-0.5)*m+qb_ref[i*TILE:(i+1)*TILE,:]*sv
                acc=None
                for t in range(tiles):
                    at=slice((i+t)*TILE,(i+t+1)*TILE)
                    kt=k_ref[at,col]*m+kb_ref[at,:]*other
                    vt=v_ref[at,col]*m+other
                    s=band(dot_nt(qi,kt),t,tiles,1)
                    if t==tiles//2:
                        s=jnp.where(diag,dot_nt(qi*(m+other*no_obs),kt),s)
                    p=jnp.exp(s).astype(BF)
                    o=dot_nn(p,vt)
                    acc=o if acc is None else acc+o
                sums.append(acc)
            total=jnp.where(first,sums[1],sums[0])
            lse_ref[i*TILE:(i+1)*TILE,col]=jnp.log(total)
            out=jnp.where(first,sums[0],sums[1])/pltpu.roll(total,HEAD,1)
            attn_ref[i*TILE:(i+1)*TILE,col]=out.astype(BF)

def prep_back(rot,d_rot,c,gain,cosine,sine,mean_mat,swap_mat):
    x=rot.astype(F32)
    m=dot_nn(halves(x*d_rot),mean_mat)
    e=d_rot*cosine-dot_nn(halves(d_rot),swap_mat)*sine
    swapped=dot_nn(rot,swap_mat[:LANES])
    n=(x*cosine-swapped*sine)/gain
    return c*(gain*e-n*m), jnp.sum(e*n,axis=0,keepdims=True)

def bwd_kernel(place_ref,q_ref,k_ref,v_ref,do_ref,attn_ref,lse_ref,cq_ref,ck_ref,gq_ref,gk_ref,cos_ref,sin_ref,qb_ref,kb_ref,sv_ref,
               mean_ref,swap_ref,cross_ref,spread_ref,
               dq_ref,dkv_ref,dgq_ref,dgk_ref,bias_ref,dk_acc,dv_acc,ke_ref,ve_ref):
    rows=qb_ref.shape[0]; ext=kb_ref.shape[0]
    tiles=2*HALF//TILE+1
    mean_mat=mean_ref[...]; swap_mat=swap_ref[...]
    first=(lane_of((1,LANES))<HEAD)
    own=[first.astype(F32).astype(BF),(1.0-first.astype(F32)).astype(BF)]
    no_obs=(lane_of((1,LANES))%HEAD!=OBS_AT).astype(F32).astype(BF)
    diag=lax.broadcasted_iota(jnp.int32,(TILE,TILE),0)==lax.broadcasted_iota(jnp.int32,(TILE,TILE),1)
    lane=lane_of((1,LANES))%HEAD
    is_var=(lane>=VAR_AT)&(lane<VAR_AT+8)
    bias_ref[...]=jnp.zeros_like(bias_ref)
    def one_pair(pair,_):
        col=pl.ds(pl.multiple_of(pair*LANES,LANES),LANES)
        dk_acc[...]=jnp.zeros_like(dk_acc)
        dv_acc[...]=jnp.zeros_like(dv_acc)
        prod=do_ref[:,col].astype(F32)*attn_ref[:,col].astype(F32)
        delta=place(dot_nn(halves(prod),cross_ref[...]),0).astype(BF)
        lse=place(lse_ref[:,col],LSE_AT).astype(BF)
        dqs=[]
        for par in range(2):
            m,other=own[par],own[1-par]
            head=2*pair+par
            sv=sv_ref[pl.ds(head,1),:].astype(BF)*other
            qm=q_ref[:,col]*BF(HEAD**-0.5)*m
            qe=qm+qb_ref[...]*sv-lse*other
            dm=do_ref[:,col]*m
            de=dm-delta*other
            ke_ref[...]=k_ref[:,col]*m+kb_ref[...]*other
            ve_ref[...]=v_ref[:,col]*m+other
            parts=[]
            for i in range(rows//TILE):
                r=slice(i*TILE,(i+1)*TILE)
                dq=None
                for t in range(tiles):
                    at=slice((i+t)*TILE,(i+t+1)*TILE)
                    kt=ke_ref[at,:]
                    s=band(dot_nt(kt,qe[r]),t,tiles,0)
                    if t==tiles//2:
                        s=jnp.where(diag,dot_nt(kt,qe[r]*(m+other*no_obs)),s)
                    p=jnp.exp(s)
                    ds=(p*dot_nt(ve_ref[at,:],de[r])).astype(BF)
                    dv_acc[at,:]+=dot_nn(p.astype(BF),dm[r])
                    dk_acc[at,:]+=dot_nn(ds,qm[r])
                    part=dot_tn(ds,kt)
                    dq=part if dq is None else dq+part
                parts.append(dq)
            dq=jnp.concatenate(parts,axis=0)
            hot=jnp.where(is_var&(first!=(par==0)),dq*qb_ref[...].astype(F32),0.0)
            bias_ref[pl.ds(head,1),:]=jnp.sum(hot,axis=0,keepdims=True)
            dqs.append(dq)
        d_rot=jnp.where(first,dqs[0],dqs[1])*(HEAD**-0.5)
        spread=spread_ref[pair]
        cosq,sinq=cos_ref[HALF:HALF+rows,:],sin_ref[HALF:HALF+rows,:]
        du,dg=prep_back(q_ref[:,col],d_rot,dot_nn(halves(cq_ref[...]),spread),gq_ref[:,col],cosq,sinq,mean_mat,swap_mat)
        dq_ref[:,col]=du.astype(BF)
        dgq_ref[:,col]=dg
        du,dg=prep_back(k_ref[:,col],dk_acc[...],dot_nn(halves(ck_ref[...]),spread),gk_ref[:,col],cos_ref[...],sin_ref[...],mean_mat,swap_mat)
        dkv_ref[:,col]=du.astype(BF)
        dgk_ref[:,col]=dg
        dkv_ref[:,pl.ds(pl.multiple_of(256+pair*LANES,LANES),LANES)]=dv_acc[...].astype(BF)
        return 0
    lax.fori_loop(0,2,one_pair,0)

def blockdiag():
    i=jnp.arange(LANES)
    mean=jnp.where(i[:,None]//HEAD==i[None]//HEAD,1.0/HEAD,0.0)
    cross=jnp.where(i[:,None]//HEAD!=i[None]//HEAD,1.0,0.0)
    swap=jnp.where(i[None]==i[:,None]+jnp.where(i[:,None]%HEAD<HEAD//2,HEAD//2,-(HEAD//2)),1.0,0.0)
    spread=jnp.stack([jnp.where(i[:,None]==pair+HEAD*(i[None]//HEAD),1.0,0.0) for pair in range(2)])
    two=lambda a: jnp.concatenate([a,a],axis=-2).astype(BF)
    return two(mean),two(swap),two(cross),two(spread)

def full(*shape):
    n=len(shape)
    return pl.BlockSpec(shape,lambda j,s:(0,)*n)
def colb(rows,width): return pl.BlockSpec((rows,width),lambda j,s:(0,j))
def lead(*shape): return pl.BlockSpec((None,)+shape,lambda j,s:(j,)+(0,)*len(shape))
ANYWHERE=pl.BlockSpec(memory_space=pl.ANY)

def attention_forward(place,xn,pieces,gq,gk,cos,sin,qb,kb,sv,mats):
    rows,ext=qb.shape[0],kb.shape[0]
    mean_mat,swap_mat,_,_=mats
    n=QUADS*256
    at=lambda j,s:(0,position(j^s[0]))
    return pl.pallas_call(
        fwd_kernel,
        grid_spec=pltpu.PrefetchScalarGridSpec(
            num_scalar_prefetch=1,grid=(QUADS,),
            in_specs=[full(ext,D)]+[ANYWHERE]*7+[lead(1,256),lead(1,256),full(ext,LANES),full(ext,LANES),
                      full(rows,LANES),full(ext,LANES),lead(8,LANES),full(2*LANES,LANES),full(2*LANES,LANES)],
            out_specs=[colb(rows,256),colb(ext,256),colb(ext,256),colb(rows,256),colb(rows,256),lead(rows,LANES),lead(ext,LANES),
                       pl.BlockSpec((D,256),at),pl.BlockSpec((D,512),at),colb(D,256)],
            scratch_shapes=[pltpu.VMEM((QUADS,D,1024),BF),pltpu.SemaphoreType.DMA((7,))]),
        out_shape=[jax.ShapeDtypeStruct((rows,n),BF),jax.ShapeDtypeStruct((ext,n),BF),jax.ShapeDtypeStruct((ext,n),BF),
                   jax.ShapeDtypeStruct((rows,n),BF),jax.ShapeDtypeStruct((rows,n),F32),
                   jax.ShapeDtypeStruct((QUADS,rows,LANES),F32),jax.ShapeDtypeStruct((QUADS,ext,LANES),F32),
                   jax.ShapeDtypeStruct((D,n),BF),jax.ShapeDtypeStruct((D,2*n),BF),jax.ShapeDtypeStruct((D,n),BF)],
        compiler_params=pltpu.CompilerParams(vmem_limit_bytes=56*2**20),
        cost_estimate=pl.CostEstimate(flops=45 * 10**9, bytes_accessed=40 * 10**6, transcendentals=0),
        name="attention_forward",
    )(place,xn,*pieces,gq,gk,cos,sin,qb,kb,sv,mean_mat,swap_mat)

def ffn_up_kernel(place_ref,x_ref,p0,p1,p2,p3,p4,p5,p6,out_ref,w_out,w_ref,sem):
    await_quarter(place_ref,(p0,p1,p2,p3,p4,p5,p6),w_ref,sem)
    step=pl.program_id(0)
    w_out[...]=w_ref[step]
    width=out_ref.shape[1]
    for begin in range(0,width,256):
        cols=slice(begin,min(begin+256,width))
        out_ref[:,cols]=dot_nn(x_ref[...],w_ref[step,:,cols])

def ffn_up(place,x,pieces):
    rows=x.shape[0]; width=pieces[0].shape[1]
    return pl.pallas_call(
        ffn_up_kernel,
        grid_spec=pltpu.PrefetchScalarGridSpec(
            num_scalar_prefetch=1,grid=(QUADS,),
            in_specs=[full(rows,D)]+[ANYWHERE]*7,
            out_specs=[colb(rows,width),colb(D,width)],
            scratch_shapes=[pltpu.VMEM((QUADS,D,width),BF),pltpu.SemaphoreType.DMA((7,))]),
        out_shape=[jax.ShapeDtypeStruct((rows,QUADS*width),F32),jax.ShapeDtypeStruct((D,QUADS*width),BF)],
        compiler_params=pltpu.CompilerParams(vmem_limit_bytes=56*2**20),
        cost_estimate=pl.CostEstimate(flops=10 * 10**9, bytes_accessed=30 * 10**6, transcendentals=0),
        name="ffn_up",
    )(place,x,*pieces)

def attention_backward(place,call,q,k,v,do,attn,lse,cq,ck,gq,gk,cos,sin,qb,kb,sv,mats):
    rows,ext=qb.shape[0],kb.shape[0]
    def quad(j,s): return s[0]^jnp.where(j==0,SEND_ORDER[2*call],SEND_ORDER[2*call+1])
    def col(rows,width): return pl.BlockSpec((rows,width),lambda j,s:(0,quad(j,s)))
    def led(*shape): return pl.BlockSpec((None,)+shape,lambda j,s:(quad(j,s),)+(0,)*len(shape))
    return pl.pallas_call(
        bwd_kernel,
        grid_spec=pltpu.PrefetchScalarGridSpec(
            num_scalar_prefetch=1,grid=(2,),
            in_specs=[col(rows,256),col(ext,256),col(ext,256),col(rows,256),col(rows,256),col(rows,256),led(rows,LANES),led(ext,LANES),
                      led(1,256),led(1,256),full(ext,LANES),full(ext,LANES),full(rows,LANES),full(ext,LANES),led(8,LANES),
                      full(2*LANES,LANES),full(2*LANES,LANES),full(2*LANES,LANES),full(2,2*LANES,LANES)],
            out_specs=[colb(rows,256),colb(ext,512),led(1,256),led(1,256),led(8,LANES)],
            scratch_shapes=[pltpu.VMEM((ext,LANES),F32),pltpu.VMEM((ext,LANES),F32),pltpu.VMEM((ext,LANES),BF),pltpu.VMEM((ext,LANES),BF)]),
        out_shape=[jax.ShapeDtypeStruct((rows,512),BF),jax.ShapeDtypeStruct((ext,1024),BF),
                   jax.ShapeDtypeStruct((QUADS,1,256),F32),jax.ShapeDtypeStruct((QUADS,1,256),F32),jax.ShapeDtypeStruct((QUADS,8,LANES),F32)],
        compiler_params=pltpu.CompilerParams(vmem_limit_bytes=56*2**20),
        cost_estimate=pl.CostEstimate(flops=38 * 10**9, bytes_accessed=20 * 10**6, transcendentals=0),
        name="attention_backward",
    )(place,q,k,v,do,attn,lse,cq,ck,gq,gk,cos,sin,qb,kb,sv,*mats)

def features(query_doc,query_var,key_doc,key_var,key_obs,key_inside):
    lane=jnp.arange(HEAD)[None,:]
    var_lane=(lane>=VAR_AT)&(lane<LSE_AT)
    def tile(a): return jnp.concatenate([a,a],axis=1).astype(BF)
    qv=var_lane&((lane-VAR_AT)%8==query_var[:,None])
    q=((lane<VAR_AT)&(lane==query_doc[:,None]))|qv|(lane==OBS_AT)
    kv=var_lane&((lane-VAR_AT)%8==key_var[:,None])
    closed=(lane<VAR_AT)&~((lane==key_doc[:,None])&key_inside[:,None])
    closed=closed|((lane==OBS_AT)&(key_obs[:,None]!=1))
    ones=kv|((lane>=LSE_AT)&(lane<LSE_AT+3))
    k=jnp.where(closed,MASKED,jnp.where(ones,1.0,0.0))
    return tile(q.astype(F32)),tile(k)

def head_scales(bias_f):
    high,mid,low=thirds(bias_f[:HEADS]-bias_f[HEADS:],lambda a: lax.reduce_precision(a,8,7))
    lane=jnp.arange(HEAD)[None,:]
    part=lambda a: a[:,None]
    s=jnp.where(lane<VAR_AT,1.0,jnp.where(lane<VAR_AT+8,part(high),jnp.where(lane<VAR_AT+16,part(mid),jnp.where(lane<LSE_AT,part(low),1.0))))
    s=jnp.where(lane>OBS_AT,0.0,s)
    s=jnp.concatenate([s,s],axis=1).reshape(HEADS//4,4,LANES)
    return jnp.concatenate([s,jnp.zeros_like(s)],axis=1)

def tables(pos):
    half=HEAD//2
    freq=jnp.exp(jnp.arange(half).astype(F32)*(-2.0*math.log(10000.0)/HEAD))
    ang=pos.astype(F32)[:,None]*freq[None,:]
    c,s=jnp.cos(ang),jnp.sin(ang)
    return jnp.concatenate([c,c,c,c],axis=1),jnp.concatenate([-s,s,-s,s],axis=1)


DIGITS = 34
LOWEST = -7


def tied(*values):
    return lax.optimization_barrier(values)


def permuted(shard, axis, flip):
    return lax.ppermute(shard, axis, [(i, i ^ flip) for i in range(lax.axis_size(axis))])


def shifted(shard, by):
    size = lax.axis_size("ctx")
    return lax.ppermute(shard, "ctx", [(i, i + by) for i in range(size) if 0 <= i + by < size])


def neighbours(shard):
    if lax.axis_size("ctx") != 4:
        return shifted(shard, 1), shifted(shard, -1)
    odd = lax.axis_index("ctx") % 2 == 1
    near = permuted(shard, "ctx", 1)
    far = lax.ppermute(near, "ctx", [(0, 2), (3, 1)])
    return jnp.where(odd, near, far), jnp.where(odd, far, near)


def returned(before, after):
    if lax.axis_size("ctx") != 4:
        return shifted(before, -1).astype(F32) + shifted(after, 1).astype(F32)
    odd = lax.axis_index("ctx") % 2 == 1
    far = lax.ppermute(jnp.where(odd, after, before), "ctx", [(1, 3), (2, 0)])
    near = jnp.where(odd, before, after).astype(F32) + far.astype(F32)
    return permuted(near.astype(BF), "ctx", 1).astype(F32)


def ctx_spread(part):
    size = lax.axis_size("ctx")
    return lax.all_to_all(jnp.broadcast_to(part[None], (size,) + part.shape), "ctx", 0, 0)


def halves_of(whole, core):
    half = whole.shape[0] // 2
    return lax.dynamic_slice_in_dim(whole, core * half, half, 0)


def corner_of(near, up):
    part = near.shape[0] // 2
    return jnp.concatenate([permuted(near[:part], "ctx", 2), permuted(up[part:], "ctx", 1)], axis=0)


def with_partner(piece):
    return piece, permuted(piece, "fsdp", 1)


def sides(left, core):
    count = lax.axis_size("fsdp")
    width = left.shape[1] // count
    blocks = [left[:, i * width : (i + 1) * width] for i in range(count)]
    even, odd = jnp.concatenate(blocks[0::2], axis=1), jnp.concatenate(blocks[1::2], axis=1)
    return jnp.where(core == 0, even, odd), jnp.where(core == 0, odd, even)


def added(*parts):
    return sum(part.astype(F32) for part in parts).astype(BF)


def joined(first, second):
    return jnp.concatenate([first, second], axis=0)


def core_scatter(total):
    size = lax.axis_size("fsdp")
    same_core = [[i for i in range(size) if i % 2 == core] for core in range(2)]
    return lax.psum_scatter(total, "fsdp", scatter_dimension=0, axis_index_groups=same_core, tiled=True)


def ctx_sum(part):
    size = lax.axis_size("ctx")
    parts = lax.all_to_all(part.reshape(size, part.shape[0] // size, part.shape[1]), "ctx", 0, 0)
    total = jnp.sum(parts.astype(F32), axis=0).astype(BF)
    return ctx_spread(total).reshape(part.shape)


def document_ids(doc_lengths, positions):
    doc_ends = jnp.cumsum(doc_lengths)
    return jnp.sum((positions[:, None] >= doc_ends[None, :]).astype(jnp.int32), axis=1)


def rms_scale(vector, scales):
    return vector * lax.rsqrt(jnp.mean(vector * vector, axis=-1, keepdims=True) + EPSILON) * scales


def gated_unit(gate_up):
    gate_part = gate_up[:, :FF]
    up_part = gate_up[:, FF:]
    return gate_part / (1.0 + jnp.exp(-gate_part)) * up_part


def digits_of(value):
    scaled = value * jnp.asarray(8.0 ** -(LOWEST + np.arange(DIGITS)), F32)
    return jnp.floor(scaled) - 8.0 * jnp.floor(scaled / 8.0)


def value_of(digits):
    return jnp.sum(digits * jnp.asarray(8.0 ** (LOWEST + np.arange(DIGITS)), F32))


def per_device(tokens, teacher, cotangent, lengths, variate, observed, norm_gains, var_bias, qkv_weight, out_weight, ffn_in, ffn_out):
    rows = tokens.shape[1]
    n_context = lax.axis_size("ctx")
    n_shards = lax.axis_size("fsdp")
    ext = rows + 2 * HALF
    start = lax.axis_index("ctx") * rows
    seq_len = observed.shape[1]
    gains_n = norm_gains.shape[1]
    bias_n = var_bias.shape[0]
    shard_id = lax.axis_index("fsdp")
    quartered = n_context == QUADS
    me = lax.axis_index("ctx") if quartered else jnp.int32(0)
    core = shard_id % 2 if quartered else jnp.int32(0)
    place = jnp.stack([me, core]).astype(jnp.int32)

    if quartered:
        quarter = lambda a, width, begin=0: lax.dynamic_slice_in_dim(a, begin + me * width, width, 1)
        shard = jnp.concatenate([quarter(qkv_weight, 256, i * D) for i in range(3)] + [quarter(out_weight, 256)], axis=1)
        whole = lax.all_gather(shard, "fsdp", axis=0, tiled=True)
        whole_in = lax.all_gather(quarter(ffn_in, FF // 2), "fsdp", axis=0, tiled=True)
    else:
        w_attention = jnp.concatenate([qkv_weight, out_weight], axis=1)
        w_attention = lax.all_gather(w_attention, "fsdp", axis=0, tiled=True)
        w_attention = jnp.swapaxes(w_attention.reshape(D, 4, QUADS, 256), 1, 2).reshape(D, QUADS, 1024)
        w_in = lax.all_gather(ffn_in, "fsdp", axis=0, tiled=True).reshape(D, QUADS, FF // 2)
    w_lower = lax.all_gather(ffn_out, "fsdp", axis=0, tiled=True)
    before, behind = neighbours(tokens[0])
    own_count = jnp.sum(observed[0])
    small = jnp.zeros((16, gains_n), BF)
    small = small.at[:4].set(norm_gains).at[4, :bias_n].set(var_bias)
    small = small.at[5, 0].set((own_count // 256).astype(BF)).at[5, 1].set((own_count % 256).astype(BF))
    small = lax.all_to_all(jnp.broadcast_to(small[None], (n_shards,) + small.shape), "fsdp", 0, 0)
    if quartered:
        mine = halves_of(whole, core)
        near, up = permuted(mine, "ctx", 1), permuted(mine, "ctx", 2)
        corner = corner_of(near, up)
        whole_in, corner = tied(whole_in, corner)
        pieces = (whole,) + with_partner(near) + with_partner(up) + with_partner(corner)
        mine_in = halves_of(whole_in, core)
        near_in, up_in = permuted(mine_in, "ctx", 1), permuted(mine_in, "ctx", 2)
    else:
        split = lambda w: (w[:, 0],) + tuple(w[i * D // 2 : (i + 1) * D // 2, j] for j in range(1, QUADS) for i in range(2))
        pieces, pieces_in = split(w_attention), split(w_in)

    gains = jnp.moveaxis(small[:, :4], 0, 1).reshape(4, D).astype(F32)
    bias = small[:, 4, :bias_n].reshape(2 * HEADS).astype(F32)
    valid_total = jnp.sum(small[:, 5, 0].astype(F32) * 256.0 + small[:, 5, 1].astype(F32))
    key_pos = start - HALF + jnp.arange(ext, dtype=jnp.int32)
    inside = (key_pos >= 0) & (key_pos < seq_len)
    key_doc = document_ids(lengths[0], key_pos)
    key_var = lax.dynamic_slice_in_dim(jnp.pad(variate[0], HALF), start, ext, 0)
    key_obs = lax.dynamic_slice_in_dim(jnp.pad(observed[0], HALF), start, ext, 0)
    own = slice(HALF, HALF + rows)
    query_feat, key_feat = features(key_doc[own], key_var[own], key_doc, key_var, key_obs, inside)
    cosine, sine = tables(key_pos)
    scales = head_scales(bias)
    mats = blockdiag()
    gain_q, gain_k = gains[2].reshape(-1, 1, 256), gains[3].reshape(-1, 1, 256)

    inputs = jnp.concatenate([before, tokens[0], behind], axis=0).astype(F32)
    inv = lax.rsqrt(jnp.mean(inputs * inputs, axis=-1, keepdims=True) + EPSILON)
    normed = (inputs * inv * gains[0]).astype(BF)

    q, k, v, attn, lse, c_q, c_k, w_q, w_kv, w_attn = attention_forward(
        place, normed, pieces, gain_q, gain_k, cosine, sine, query_feat, key_feat, scales, mats
    )
    if quartered:
        near_in, up_in, attn = tied(near_in, up_in, attn)
        corner_in = corner_of(near_in, up_in)
        pieces_in = (whole_in,) + with_partner(near_in) + with_partner(up_in) + with_partner(corner_in)
    mixed = tokens[0].astype(F32) + jnp.dot(attn, w_attn, preferred_element_type=F32)
    normed_two_f, norm_two_pull = jax.vjp(lambda m: rms_scale(m, gains[1]), mixed)
    normed_two = normed_two_f.astype(BF)
    gate_up, w_upper = ffn_up(place, normed_two, pieces_in)
    hidden_f, glu_pull = jax.vjp(gated_unit, gate_up)
    hidden = hidden_f.astype(BF)
    final = mixed + jnp.dot(hidden, w_lower, preferred_element_type=F32)
    valid_col = key_obs[own].astype(F32)[:, None]
    distance = final - teacher[0].astype(F32)
    squared = jnp.sum(valid_col * distance * distance)
    all_tokens = rows * n_context * n_shards
    d_final = cotangent[0].astype(F32) + all_tokens * valid_col * distance / valid_total
    d_final_low = d_final.astype(BF)

    low_grad = dot_tn(hidden, d_final_low).astype(BF)
    d_final_low, low_grad = tied(d_final_low, low_grad)
    low_part = lax.psum_scatter(low_grad, "fsdp", scatter_dimension=0, tiled=True)
    d_hidden = dot_nt(d_final_low, w_lower)
    (d_gate_up,) = glu_pull(d_hidden)
    d_gate_low = d_gate_up.astype(BF)
    if quartered:
        own_two, other_two = sides(normed_two, core)
        theirs = dot_tn(other_two, d_gate_low).astype(BF)
        d_gate_low, theirs = tied(d_gate_low, theirs)
        swapped = permuted(theirs, "fsdp", 1)
        d_normed_two = dot_nt(d_gate_low, w_upper)
        d_gate_low, d_normed_two = tied(d_gate_low, d_normed_two)
        in_chip = (dot_tn(own_two, d_gate_low) + swapped.astype(F32)).astype(BF)
        part = lambda j: lax.dynamic_slice_in_dim(in_chip, (me ^ j) * (FF // 2), FF // 2, 1)
        cut = in_chip.shape[0] // 2
        last = part(3)
    else:
        d_normed_two = dot_nt(d_gate_low, w_upper)
        in_part = lax.psum_scatter(dot_tn(normed_two, d_gate_low).astype(BF), "fsdp", scatter_dimension=0, tiled=True)
        in_grad = lax.psum(in_part, "ctx").astype(F32)
        last = in_part
    (d_mixed_part,) = norm_two_pull(d_normed_two)
    d_mixed = d_final + d_mixed_part
    d_mixed_low = d_mixed.astype(BF)
    out_grad = dot_tn(attn, d_mixed_low).astype(BF)
    d_attn = dot_nt(d_mixed_low, w_attn).astype(BF)

    d_attn, last, out_grad = tied(d_attn, last, out_grad)
    out_part = lax.psum_scatter(out_grad, "fsdp", scatter_dimension=0, tiled=True)
    if quartered:
        last_near, last_up = permuted(last[:cut], "ctx", 1), permuted(last[cut:], "ctx", 2)
    saved = (q, k, v, d_attn, attn, lse, c_q, c_k, gain_q, gain_k, cosine, sine, query_feat, key_feat, scales, mats)
    d_q1, d_kv1, gain_q1, gain_k1, bias_1 = attention_backward(place, 0, *saved)
    if quartered:
        own_normed, other_normed = sides(normed, core)
        theirs = [dot_tn(other_normed[own], d_q1).astype(BF), dot_tn(other_normed, d_kv1).astype(BF)]
        last_near, last_up, theirs = tied(last_near, last_up, theirs)
        swapped = [permuted(t, "fsdp", 1) for t in theirs]
        one, two = part(1), part(2)
        one, two = joined(one[:cut], added(one[cut:], last_up)), joined(added(two[:cut], last_near), two[cut:])
        d_q1, d_kv1, one, two = tied(d_q1, d_kv1, one, two)
        in_near, in_up = permuted(one, "ctx", 1), permuted(two, "ctx", 2)
        first_q = (dot_tn(own_normed[own], d_q1) + swapped[0].astype(F32)).astype(BF)
        first_kv = (dot_tn(own_normed, d_kv1) + swapped[1].astype(F32)).astype(BF)
        quarters = {3: jnp.concatenate([first_q[:, :256], first_kv[:, :512]], axis=1), 1: jnp.concatenate([first_q[:, 256:], first_kv[:, 512:]], axis=1)}
        d_attn, quarters, low_part = tied(d_attn, quarters, low_part)
        last_near, last_up = permuted(quarters[3][:cut], "ctx", 1), permuted(quarters[3][cut:], "ctx", 2)
        saved = saved[:3] + (d_attn,) + saved[4:]
    d_q2, d_kv2, gain_q2, gain_k2, bias_2 = attention_backward(place, 1, *saved)
    done_first = ((me ^ jnp.arange(QUADS)) % 2 == 1)[:, None, None]
    d_gain_q = jnp.where(done_first, gain_q1, gain_q2).reshape(D)
    d_gain_k = jnp.where(done_first, gain_k1, gain_k2).reshape(D)
    same = jnp.sum(jnp.where(done_first, bias_1, bias_2)[:, :4], axis=-1).reshape(HEADS)
    d_bias = jnp.concatenate([same, -same])

    if quartered:
        extra = jnp.zeros((n_shards, D // n_shards, LANES), F32)
        extra = extra.at[:, 0, :gains_n].set(d_gain_q.reshape(n_shards, gains_n)).at[:, 1, :gains_n].set(d_gain_k.reshape(n_shards, gains_n))
        extra = extra.at[:, 2, :bias_n].set(d_bias.reshape(n_shards, bias_n)).at[:, 3, :DIGITS].set(digits_of(squared)[None])
        extra = extra.reshape(n_shards // 2, 2, D // n_shards, LANES).astype(BF)
        own_extra = jnp.where(core == 0, extra[:, 0], extra[:, 1]).reshape(-1, LANES)
        other_extra = jnp.where(core == 0, extra[:, 1], extra[:, 0]).reshape(-1, LANES)
        theirs = [dot_tn(other_normed[own], d_q2).astype(BF), dot_tn(other_normed, d_kv2).astype(BF), other_extra]
        theirs, in_near, in_up, out_part = tied(theirs, in_near, in_up, out_part)
        swapped = [permuted(t, "fsdp", 1) for t in theirs]
        in_total = added(part(0), in_near, in_up)
        d_q2, d_kv2, in_total = tied(d_q2, d_kv2, in_total)
        in_part = core_scatter(in_total)
        second_q = (dot_tn(own_normed[own], d_q2) + swapped[0].astype(F32)).astype(BF)
        second_kv = (dot_tn(own_normed, d_kv2) + swapped[1].astype(F32)).astype(BF)
        quarters[2] = jnp.concatenate([second_q[:, :256], second_kv[:, :512]], axis=1)
        quarters[0] = jnp.concatenate([second_q[:, 256:], second_kv[:, 512:]], axis=1)
        one = joined(quarters[1][:cut], added(quarters[1][cut:], last_up))
        two = joined(added(quarters[2][:cut], last_near), quarters[2][cut:])
        d_kv2, d_q2, one, two = tied(d_kv2, d_q2, one, two)
        near, up = permuted(one, "ctx", 1), permuted(two, "ctx", 2)
    d_ext = dot_nt(d_kv1, w_kv[:, : 2 * 512]) + dot_nt(d_kv2, w_kv[:, 2 * 512 :])
    from_others = returned(d_ext[:HALF].astype(BF), d_ext[HALF + rows :].astype(BF))
    d_own = d_ext[own] + dot_nt(d_q1, w_q[:, : 2 * 256]) + dot_nt(d_q2, w_q[:, 2 * 256 :])
    if quartered:
        qkv_total = jnp.concatenate([added(quarters[0], near, up), added(own_extra, swapped[2])], axis=1)
        qkv_part = core_scatter(qkv_total)
        spread = ctx_spread(qkv_part)
        qkv_grad = jnp.transpose(spread[:, :, : 3 * 256].reshape(QUADS, -1, 3, 256), (1, 2, 0, 3)).reshape(-1, 3 * D).astype(F32)
        sums = jnp.sum(spread[:, :, 3 * 256 :].astype(F32), axis=0)
        squared = value_of(sums[3, :DIGITS])
        gain_rows, var_bias_grad = sums[:2, :gains_n], sums[2, :bias_n]
        in_grad = jnp.swapaxes(ctx_spread(in_part), 0, 1).reshape(-1, 2 * FF).astype(F32)
        other_grads = ctx_sum(joined(out_part, low_part)).astype(F32)
    else:
        order = [SEND_ORDER.index(j) for j in range(QUADS)]
        natural = lambda first, second, width: jnp.concatenate([first, second], axis=1).reshape(-1, QUADS, width)[:, jnp.array(order)]
        grad_q = dot_tn(normed[own], natural(d_q1, d_q2, 256).reshape(rows, D))
        grad_kv = dot_tn(normed, jnp.swapaxes(natural(d_kv1, d_kv2, 512).reshape(ext, QUADS, 2, 256), 1, 2).reshape(ext, 2 * D))
        grad_qkv = jnp.concatenate([grad_q, grad_kv], axis=1).astype(BF)
        qkv_grad = lax.psum(lax.psum_scatter(grad_qkv, "fsdp", scatter_dimension=0, tiled=True), "ctx").astype(F32)
        other_grads = lax.psum(joined(out_part, low_part), "ctx").astype(F32)
        sums = jnp.concatenate([d_gain_q, d_gain_k, d_bias, squared[None]])
        sums = lax.psum(jnp.pad(sums, (0, -sums.shape[0] % (8 * LANES))).reshape(-1, LANES), ("ctx", "fsdp")).reshape(-1)
        gain_rows = lax.dynamic_slice_in_dim(sums[: 2 * D].reshape(2, D), shard_id * gains_n, gains_n, 1)
        var_bias_grad = lax.dynamic_slice_in_dim(sums[2 * D : 2 * D + 2 * HEADS], shard_id * bias_n, bias_n, 0)
        squared = sums[2 * D + 2 * HEADS]
    loss = squared / (valid_total * D)
    own_gains = norm_gains.astype(F32)
    gain_one = jnp.sum(qkv_weight.astype(F32) * qkv_grad, axis=1) / own_gains[0]
    gain_two = jnp.sum(ffn_in.astype(F32) * in_grad, axis=1) / own_gains[1]
    gains_grad = jnp.concatenate([gain_one[None], gain_two[None], gain_rows], axis=0)
    unit = inputs[own] * inv[own]
    scaled = (d_own + from_others) * gains[0]
    input_grad = d_mixed + inv[own] * (scaled - unit * jnp.mean(unit * scaled, axis=-1, keepdims=True))
    return (
        loss,
        final.astype(BF)[None],
        input_grad[None],
        gains_grad,
        var_bias_grad,
        qkv_grad,
        other_grads[: out_part.shape[0]],
        in_grad,
        other_grads[out_part.shape[0] :],
    )


def solution(mesh):
    split = P("fsdp", "ctx", None)
    rows = P("fsdp", None)
    return jax.shard_map(
        per_device,
        mesh=mesh,
        in_specs=(split, split, split, rows, rows, rows, P(None, "fsdp"), P("fsdp"), rows, rows, rows, rows),
        out_specs=(P(), split, split, P(None, "fsdp"), P("fsdp"), rows, rows, rows, rows),
        check_vma=False,
    )
```

```python
import math

import jax
import jax.numpy as jnp
import numpy as np
from jax import lax
from jax.experimental import pallas as pl
from jax.experimental.pallas import tpu as pltpu
from jax.sharding import PartitionSpec as P


D=1024; HEADS=16; HEAD=64; FF=2816; WINDOW=1024
EPSILON=1e-6; MASKED=-1e30
HALF=WINDOW//2
LANES=128
VAR_AT, LSE_AT, OBS_AT = 8, 32, 35
TILE=256
F32=jnp.float32; BF=jnp.bfloat16


def dot_nn(a,b): return lax.dot_general(a,b,(((1,),(0,)),((),())),preferred_element_type=F32)
def dot_nt(a,b): return lax.dot_general(a,b,(((1,),(1,)),((),())),preferred_element_type=F32)
def dot_tn(a,b): return lax.dot_general(a,b,(((0,),(0,)),((),())),preferred_element_type=F32)

def halves(v):
    high=v.astype(BF)
    return jnp.concatenate([high,(v-high.astype(F32)).astype(BF)],axis=1)

def thirds(v,rounded=lambda a: a.astype(BF).astype(F32)):
    high=rounded(v)
    rest=v-high
    mid=rounded(rest)
    return high,mid,rest-mid

def lane_of(shape): return lax.broadcasted_iota(jnp.int32,shape,1)

def place(v,at):
    high,mid,low=thirds(v)
    lane=lane_of(v.shape)%HEAD
    return jnp.where(lane==at,high,jnp.where(lane==at+1,mid,jnp.where(lane==at+2,low,0.0)))

def band(s,t,tiles,key_axis):
    if t not in (0,tiles-1): return s
    key=lax.broadcasted_iota(jnp.int32,s.shape,key_axis)
    query=lax.broadcasted_iota(jnp.int32,s.shape,1-key_axis)
    keep=key>=query if t==0 else key<=query
    return jnp.where(keep,s,MASKED)

def prep(u,gain,cosine,sine,mean_mat,swap_mat):
    mean=dot_nn(halves(u*u),mean_mat)
    c=lax.rsqrt(mean+EPSILON)
    n=u*c*gain
    return n*cosine+dot_nn(halves(n),swap_mat)*sine, c

QUADS=4
SEND_ORDER=(3,1,2,0)
def position(slot): return jnp.where(slot==0,3,jnp.where(slot==3,0,slot))

def piece_copies(place_ref,pieces,w_ref,sem):
    me,core=place_ref[0],place_ref[1]
    half=w_ref.shape[1]//2
    copies=[[pltpu.make_async_copy(pieces[0],w_ref.at[me],sem.at[0])]]
    for slot in range(1,QUADS):
        copies.append([pltpu.make_async_copy(pieces[2*slot-1+side],
            w_ref.at[me^slot,pl.ds(pl.multiple_of((core if side==0 else 1-core)*half,half),half),:],sem.at[2*slot-1+side]) for side in range(2)])
    return copies

def await_quarter(place_ref,pieces,w_ref,sem):
    step=pl.program_id(0)
    copies=piece_copies(place_ref,pieces,w_ref,sem)
    @pl.when(step==0)
    def _():
        for group in copies:
            for copy in group: copy.start()
    slot=step^place_ref[0]
    for i,group in enumerate(copies):
        @pl.when(slot==i)
        def _(group=group):
            for copy in group: copy.wait()

def fwd_kernel(place_ref,xn_ref,p0,p1,p2,p3,p4,p5,p6,gq_ref,gk_ref,cos_ref,sin_ref,qb_ref,kb_ref,sv_ref,mean_ref,swap_ref,
               q_ref,k_ref,v_ref,attn_ref,lse_ref,cq_ref,ck_ref,wq_out,wkv_out,wattn_out,w_ref,sem):
    rows=qb_ref.shape[0]; ext=kb_ref.shape[0]
    await_quarter(place_ref,(p0,p1,p2,p3,p4,p5,p6),w_ref,sem)
    quad=pl.program_id(0)
    wq_out[...]=w_ref[quad,:,0:256]
    wkv_out[...]=w_ref[quad,:,256:768]
    wattn_out[...]=w_ref[quad,:,768:1024]
    tiles=2*HALF//TILE+1
    mean_mat=mean_ref[...]; swap_mat=swap_ref[...]
    first=(lane_of((1,LANES))<HEAD)
    kf=dot_nn(xn_ref[...],w_ref[quad,:,256:512])
    for pair in range(2):
        col=slice(pair*LANES,(pair+1)*LANES)
        rot,c=prep(kf[:,col],gk_ref[:,col],cos_ref[...],sin_ref[...],mean_mat,swap_mat)
        k_ref[:,col]=rot.astype(BF)
        if pair==0: ck_ref[...]=c
        else: ck_ref[...]=jnp.where(lane_of((1,LANES))%HEAD==pair,c,ck_ref[...])
    v_ref[...]=dot_nn(xn_ref[...],w_ref[quad,:,512:768]).astype(BF)
    qf=dot_nn(xn_ref[HALF:HALF+rows,:],w_ref[quad,:,0:256])
    for pair in range(2):
        col=slice(pair*LANES,(pair+1)*LANES)
        rot,c=prep(qf[:,col],gq_ref[:,col],cos_ref[HALF:HALF+rows,:],sin_ref[HALF:HALF+rows,:],mean_mat,swap_mat)
        q_ref[:,col]=rot.astype(BF)
        if pair==0: cq_ref[...]=c
        else: cq_ref[...]=jnp.where(lane_of((1,LANES))%HEAD==pair,c,cq_ref[...])
    own=[first.astype(F32).astype(BF),(1.0-first.astype(F32)).astype(BF)]
    no_obs=(lane_of((1,LANES))%HEAD!=OBS_AT).astype(F32).astype(BF)
    diag=lax.broadcasted_iota(jnp.int32,(TILE,TILE),0)==lax.broadcasted_iota(jnp.int32,(TILE,TILE),1)
    for pair in range(2):
        col=slice(pair*LANES,(pair+1)*LANES)
        for i in range(rows//TILE):
            sums=[]
            for par in range(2):
                m,other=own[par],own[1-par]
                sv=sv_ref[2*pair+par:2*pair+par+1,:].astype(BF)*other
                qi=q_ref[i*TILE:(i+1)*TILE,col]*BF(HEAD**-0.5)*m+qb_ref[i*TILE:(i+1)*TILE,:]*sv
                acc=None
                for t in range(tiles):
                    at=slice((i+t)*TILE,(i+t+1)*TILE)
                    kt=k_ref[at,col]*m+kb_ref[at,:]*other
                    vt=v_ref[at,col]*m+other
                    s=band(dot_nt(qi,kt),t,tiles,1)
                    if t==tiles//2:
                        s=jnp.where(diag,dot_nt(qi*(m+other*no_obs),kt),s)
                    p=jnp.exp(s).astype(BF)
                    o=dot_nn(p,vt)
                    acc=o if acc is None else acc+o
                sums.append(acc)
            total=jnp.where(first,sums[1],sums[0])
            lse_ref[i*TILE:(i+1)*TILE,col]=jnp.log(total)
            out=jnp.where(first,sums[0],sums[1])/pltpu.roll(total,HEAD,1)
            attn_ref[i*TILE:(i+1)*TILE,col]=out.astype(BF)

def prep_back(rot,d_rot,c,gain,cosine,sine,mean_mat,swap_mat):
    x=rot.astype(F32)
    m=dot_nn(halves(x*d_rot),mean_mat)
    e=d_rot*cosine-dot_nn(halves(d_rot),swap_mat)*sine
    swapped=dot_nn(rot,swap_mat[:LANES])
    n=(x*cosine-swapped*sine)/gain
    return c*(gain*e-n*m), jnp.sum(e*n,axis=0,keepdims=True)

def bwd_kernel(place_ref,q_ref,k_ref,v_ref,do_ref,attn_ref,lse_ref,cq_ref,ck_ref,gq_ref,gk_ref,cos_ref,sin_ref,qb_ref,kb_ref,sv_ref,
               mean_ref,swap_ref,cross_ref,spread_ref,
               dq_ref,dkv_ref,dgq_ref,dgk_ref,bias_ref,dk_acc,dv_acc,ke_ref,ve_ref):
    rows=qb_ref.shape[0]; ext=kb_ref.shape[0]
    tiles=2*HALF//TILE+1
    mean_mat=mean_ref[...]; swap_mat=swap_ref[...]
    first=(lane_of((1,LANES))<HEAD)
    own=[first.astype(F32).astype(BF),(1.0-first.astype(F32)).astype(BF)]
    no_obs=(lane_of((1,LANES))%HEAD!=OBS_AT).astype(F32).astype(BF)
    diag=lax.broadcasted_iota(jnp.int32,(TILE,TILE),0)==lax.broadcasted_iota(jnp.int32,(TILE,TILE),1)
    lane=lane_of((1,LANES))%HEAD
    is_var=(lane>=VAR_AT)&(lane<VAR_AT+8)
    bias_ref[...]=jnp.zeros_like(bias_ref)
    def one_pair(pair,_):
        col=pl.ds(pl.multiple_of(pair*LANES,LANES),LANES)
        dk_acc[...]=jnp.zeros_like(dk_acc)
        dv_acc[...]=jnp.zeros_like(dv_acc)
        prod=do_ref[:,col].astype(F32)*attn_ref[:,col].astype(F32)
        delta=place(dot_nn(halves(prod),cross_ref[...]),0).astype(BF)
        lse=place(lse_ref[:,col],LSE_AT).astype(BF)
        dqs=[]
        for par in range(2):
            m,other=own[par],own[1-par]
            head=2*pair+par
            sv=sv_ref[pl.ds(head,1),:].astype(BF)*other
            qm=q_ref[:,col]*BF(HEAD**-0.5)*m
            qe=qm+qb_ref[...]*sv-lse*other
            dm=do_ref[:,col]*m
            de=dm-delta*other
            ke_ref[...]=k_ref[:,col]*m+kb_ref[...]*other
            ve_ref[...]=v_ref[:,col]*m+other
            parts=[]
            for i in range(rows//TILE):
                r=slice(i*TILE,(i+1)*TILE)
                dq=None
                for t in range(tiles):
                    at=slice((i+t)*TILE,(i+t+1)*TILE)
                    kt=ke_ref[at,:]
                    s=band(dot_nt(kt,qe[r]),t,tiles,0)
                    if t==tiles//2:
                        s=jnp.where(diag,dot_nt(kt,qe[r]*(m+other*no_obs)),s)
                    p=jnp.exp(s)
                    ds=(p*dot_nt(ve_ref[at,:],de[r])).astype(BF)
                    dv_acc[at,:]+=dot_nn(p.astype(BF),dm[r])
                    dk_acc[at,:]+=dot_nn(ds,qm[r])
                    part=dot_tn(ds,kt)
                    dq=part if dq is None else dq+part
                parts.append(dq)
            dq=jnp.concatenate(parts,axis=0)
            hot=jnp.where(is_var&(first!=(par==0)),dq*qb_ref[...].astype(F32),0.0)
            bias_ref[pl.ds(head,1),:]=jnp.sum(hot,axis=0,keepdims=True)
            dqs.append(dq)
        d_rot=jnp.where(first,dqs[0],dqs[1])*(HEAD**-0.5)
        spread=spread_ref[pair]
        cosq,sinq=cos_ref[HALF:HALF+rows,:],sin_ref[HALF:HALF+rows,:]
        du,dg=prep_back(q_ref[:,col],d_rot,dot_nn(halves(cq_ref[...]),spread),gq_ref[:,col],cosq,sinq,mean_mat,swap_mat)
        dq_ref[:,col]=du.astype(BF)
        dgq_ref[:,col]=dg
        du,dg=prep_back(k_ref[:,col],dk_acc[...],dot_nn(halves(ck_ref[...]),spread),gk_ref[:,col],cos_ref[...],sin_ref[...],mean_mat,swap_mat)
        dkv_ref[:,col]=du.astype(BF)
        dgk_ref[:,col]=dg
        dkv_ref[:,pl.ds(pl.multiple_of(256+pair*LANES,LANES),LANES)]=dv_acc[...].astype(BF)
        return 0
    lax.fori_loop(0,2,one_pair,0)

def blockdiag():
    i=jnp.arange(LANES)
    mean=jnp.where(i[:,None]//HEAD==i[None]//HEAD,1.0/HEAD,0.0)
    cross=jnp.where(i[:,None]//HEAD!=i[None]//HEAD,1.0,0.0)
    swap=jnp.where(i[None]==i[:,None]+jnp.where(i[:,None]%HEAD<HEAD//2,HEAD//2,-(HEAD//2)),1.0,0.0)
    spread=jnp.stack([jnp.where(i[:,None]==pair+HEAD*(i[None]//HEAD),1.0,0.0) for pair in range(2)])
    two=lambda a: jnp.concatenate([a,a],axis=-2).astype(BF)
    return two(mean),two(swap),two(cross),two(spread)

def full(*shape):
    n=len(shape)
    return pl.BlockSpec(shape,lambda j,s:(0,)*n)
def colb(rows,width): return pl.BlockSpec((rows,width),lambda j,s:(0,j))
def lead(*shape): return pl.BlockSpec((None,)+shape,lambda j,s:(j,)+(0,)*len(shape))
ANYWHERE=pl.BlockSpec(memory_space=pltpu.HBM)

def attention_forward(place,xn,pieces,gq,gk,cos,sin,qb,kb,sv,mats):
    rows,ext=qb.shape[0],kb.shape[0]
    mean_mat,swap_mat,_,_=mats
    n=QUADS*256
    at=lambda j,s:(0,position(j^s[0]))
    return pl.pallas_call(
        fwd_kernel,
        grid_spec=pltpu.PrefetchScalarGridSpec(
            num_scalar_prefetch=1,grid=(QUADS,),
            in_specs=[full(ext,D)]+[ANYWHERE]*7+[lead(1,256),lead(1,256),full(ext,LANES),full(ext,LANES),
                      full(rows,LANES),full(ext,LANES),lead(8,LANES),full(2*LANES,LANES),full(2*LANES,LANES)],
            out_specs=[colb(rows,256),colb(ext,256),colb(ext,256),colb(rows,256),colb(rows,256),lead(rows,LANES),lead(ext,LANES),
                       pl.BlockSpec((D,256),at),pl.BlockSpec((D,512),at),colb(D,256)],
            scratch_shapes=[pltpu.VMEM((QUADS,D,1024),BF),pltpu.SemaphoreType.DMA((7,))]),
        out_shape=[jax.ShapeDtypeStruct((rows,n),BF),jax.ShapeDtypeStruct((ext,n),BF),jax.ShapeDtypeStruct((ext,n),BF),
                   jax.ShapeDtypeStruct((rows,n),BF),jax.ShapeDtypeStruct((rows,n),F32),
                   jax.ShapeDtypeStruct((QUADS,rows,LANES),F32),jax.ShapeDtypeStruct((QUADS,ext,LANES),F32),
                   jax.ShapeDtypeStruct((D,n),BF),jax.ShapeDtypeStruct((D,2*n),BF),jax.ShapeDtypeStruct((D,n),BF)],
        compiler_params=pltpu.CompilerParams(vmem_limit_bytes=56*2**20),
        cost_estimate=pl.CostEstimate(flops=10**6, bytes_accessed=10**4, transcendentals=0),
        name="attention_forward",
    )(place,xn,*pieces,gq,gk,cos,sin,qb,kb,sv,mean_mat,swap_mat)

def feed_forward_kernel(place_ref,weight_ref,gain_ref,obs_ref,x_in,mixed_in,teacher_in,cot_in,low_in,attn_in,p0,p1,p2,p3,p4,p5,p6,
                        hidden_out,d_up_out,act_out,d_low_out,d_mixed_out,d_mixed_low_out,d_attn_out,sum_ref,
                        w_ref,low_ref,attn_ref,x_ref,mixed_ref,teacher_ref,cot_ref,gate_up_ref,hidden_ref,act_ref,d_low_ref,d_final_ref,acc_ref,
                        in_sem,piece_sem,out_sem):
    arrivals=[pltpu.make_async_copy(src,dst,in_sem.at[i]) for i,(src,dst) in enumerate(
        [(x_in,x_ref),(mixed_in,mixed_ref),(low_in,low_ref),(teacher_in,teacher_ref),(cot_in,cot_ref),(attn_in,attn_ref)])]
    pieces=piece_copies(place_ref,(p0,p1,p2,p3,p4,p5,p6),w_ref,piece_sem)
    arrivals[0].start()
    for group in pieces:
        for copy in group: copy.start()
    for copy in arrivals[1:]: copy.start()
    sent=[]
    def send(ref,out):
        copy=pltpu.make_async_copy(ref,out,out_sem.at[len(sent)])
        copy.start(); sent.append(copy)
    arrivals[0].wait()
    width=w_ref.shape[2]
    tiles=[slice(begin,min(begin+256,width)) for begin in range(0,width,256)]
    for half in range(2):
        for quarter in (half,half+2):
            slot=place_ref[0]^quarter
            for i,group in enumerate(pieces):
                @pl.when(slot==i)
                def _(group=group):
                    for copy in group: copy.wait()
        for tile in tiles:
            at=slice(half*width+tile.start,half*width+tile.stop); up_at=slice(FF+at.start,FF+at.stop)
            gate=dot_nn(x_ref[...],w_ref[half,:,tile])
            up=dot_nn(x_ref[...],w_ref[half+2,:,tile])
            gate_up_ref[:,at]=gate.astype(BF)
            gate_up_ref[:,up_at]=up.astype(BF)
            hidden_ref[:,at]=(gate/(1.0+jnp.exp(-gate))*up).astype(BF)
    send(hidden_ref,hidden_out)
    for copy in arrivals[1:]: copy.wait()
    total=jnp.zeros((1,256),F32)
    for begin in range(0,D,256):
        cols=slice(begin,begin+256)
        final=mixed_ref[:,cols]+dot_nn(hidden_ref[...],low_ref[:,cols])
        act_ref[:,cols]=final.astype(BF)
        distance=final-teacher_ref[:,cols].astype(F32)
        seen=obs_ref[...]*distance
        total=total+jnp.sum(seen*distance,axis=0,keepdims=True)
        d_final=cot_ref[:,cols].astype(F32)+weight_ref[0]*seen
        d_final_ref[:,cols]=d_final
        d_low_ref[:,cols]=d_final.astype(BF)
    sum_ref[...]=total
    send(act_ref,act_out)
    send(d_low_ref,d_low_out)
    for begin in range(0,FF,256):
        cols=slice(begin,begin+256); ups=slice(FF+begin,FF+begin+256)
        d_hidden=dot_nt(d_low_ref[...],low_ref[cols,:])
        gate=gate_up_ref[:,cols].astype(F32); up=gate_up_ref[:,ups].astype(F32)
        sig=1.0/(1.0+jnp.exp(-gate))
        gate_up_ref[:,cols]=(d_hidden*up*(sig*(1.0+gate*(1.0-sig)))).astype(BF)
        gate_up_ref[:,ups]=(d_hidden*(gate*sig)).astype(BF)
    send(gate_up_ref,d_up_out)
    for begin in range(0,D,256):
        part=None
        for quarter in range(QUADS):
            one=dot_nt(gate_up_ref[:,quarter*width:(quarter+1)*width],w_ref[quarter,begin:begin+256,:])
            part=one if part is None else part+one
        acc_ref[:,begin:begin+256]=part
    mixed=mixed_ref[...]
    c=lax.rsqrt(jnp.mean(mixed*mixed,axis=1,keepdims=True)+EPSILON)
    scaled=acc_ref[...]*gain_ref[...]
    unit=mixed*c
    d_mixed=d_final_ref[...]+c*(scaled-unit*jnp.mean(unit*scaled,axis=1,keepdims=True))
    d_final_ref[...]=d_mixed
    send(d_final_ref,d_mixed_out)
    x_ref[...]=d_mixed.astype(BF)
    send(x_ref,d_mixed_low_out)
    for begin in range(0,D,256):
        teacher_ref[:,begin:begin+256]=dot_nt(x_ref[...],attn_ref[begin:begin+256,:]).astype(BF)
    send(teacher_ref,d_attn_out)
    for copy in sent: copy.wait()

def feed_forward(place,weight,gain,obs,x,mixed,teacher,cotangent,w_lower,w_attn,pieces):
    rows=x.shape[0]; width=pieces[0].shape[1]
    low=jax.ShapeDtypeStruct((rows,D),BF)
    smem=pl.BlockSpec(memory_space=pltpu.SMEM); vmem=pl.BlockSpec(memory_space=pltpu.VMEM)
    square=pltpu.VMEM((rows,D),BF); wide=pltpu.VMEM((rows,D),F32)
    return pl.pallas_call(
        feed_forward_kernel,
        in_specs=[smem,smem,vmem,vmem]+[ANYWHERE]*13,
        out_specs=[ANYWHERE]*7+[vmem],
        out_shape=[jax.ShapeDtypeStruct((rows,FF),BF),jax.ShapeDtypeStruct((rows,2*FF),BF),low,low,jax.ShapeDtypeStruct((rows,D),F32),low,low,
                   jax.ShapeDtypeStruct((1,256),F32)],
        scratch_shapes=[pltpu.VMEM((QUADS,D,width),BF),pltpu.VMEM((FF,D),BF),pltpu.VMEM((D,D),BF),square,wide,square,square,
                        pltpu.VMEM((rows,2*FF),BF),pltpu.VMEM((rows,FF),BF),square,square,wide,wide,
                        pltpu.SemaphoreType.DMA((6,)),pltpu.SemaphoreType.DMA((7,)),pltpu.SemaphoreType.DMA((7,))],
        compiler_params=pltpu.CompilerParams(vmem_limit_bytes=58*2**20),
        cost_estimate=pl.CostEstimate(flops=10**6, bytes_accessed=10**4, transcendentals=0),
        name="feed_forward",
    )(place,weight,gain,obs,x,mixed,teacher,cotangent,w_lower,w_attn,*pieces)

def attention_backward(place,call,q,k,v,do,attn,lse,cq,ck,gq,gk,cos,sin,qb,kb,sv,mats):
    rows,ext=qb.shape[0],kb.shape[0]
    def quad(j,s): return s[0]^jnp.where(j==0,SEND_ORDER[2*call],SEND_ORDER[2*call+1])
    def col(rows,width): return pl.BlockSpec((rows,width),lambda j,s:(0,quad(j,s)))
    def led(*shape): return pl.BlockSpec((None,)+shape,lambda j,s:(quad(j,s),)+(0,)*len(shape))
    return pl.pallas_call(
        bwd_kernel,
        grid_spec=pltpu.PrefetchScalarGridSpec(
            num_scalar_prefetch=1,grid=(2,),
            in_specs=[col(rows,256),col(ext,256),col(ext,256),col(rows,256),col(rows,256),col(rows,256),led(rows,LANES),led(ext,LANES),
                      led(1,256),led(1,256),full(ext,LANES),full(ext,LANES),full(rows,LANES),full(ext,LANES),led(8,LANES),
                      full(2*LANES,LANES),full(2*LANES,LANES),full(2*LANES,LANES),full(2,2*LANES,LANES)],
            out_specs=[colb(rows,256),colb(ext,512),led(1,256),led(1,256),led(8,LANES)],
            scratch_shapes=[pltpu.VMEM((ext,LANES),F32),pltpu.VMEM((ext,LANES),F32),pltpu.VMEM((ext,LANES),BF),pltpu.VMEM((ext,LANES),BF)]),
        out_shape=[jax.ShapeDtypeStruct((rows,512),BF),jax.ShapeDtypeStruct((ext,1024),BF),
                   jax.ShapeDtypeStruct((QUADS,1,256),F32),jax.ShapeDtypeStruct((QUADS,1,256),F32),jax.ShapeDtypeStruct((QUADS,8,LANES),F32)],
        compiler_params=pltpu.CompilerParams(vmem_limit_bytes=56*2**20),
        cost_estimate=pl.CostEstimate(flops=10**6, bytes_accessed=10**4, transcendentals=0),
        name="attention_backward",
    )(place,q,k,v,do,attn,lse,cq,ck,gq,gk,cos,sin,qb,kb,sv,*mats)

def finish_kernel(layout,spread_ref,weight_ref,grad_ref,sum_ref):
    total=None
    for quarter in range(QUADS):
        for begin,width,base in layout:
            at=slice(base+quarter*width,base+(quarter+1)*width)
            grad=spread_ref[quarter,:,begin:begin+width].astype(F32)
            grad_ref[:,at]=grad
            part=jnp.sum(grad*weight_ref[:,at].astype(F32),axis=1,keepdims=True)
            total=part if total is None else total+part
    sum_ref[...]=total

def finish(spread,weight,layout):
    vmem=pl.BlockSpec(memory_space=pltpu.VMEM)
    return pl.pallas_call(
        lambda *refs: finish_kernel(layout,*refs),in_specs=[vmem]*2,out_specs=[vmem]*2,
        out_shape=[jax.ShapeDtypeStruct(weight.shape,F32),jax.ShapeDtypeStruct((weight.shape[0],1),F32)],
        compiler_params=pltpu.CompilerParams(vmem_limit_bytes=32*2**20),
        cost_estimate=pl.CostEstimate(flops=10**6, bytes_accessed=10**4, transcendentals=0),
        name="finish",
    )(spread,weight)

def features(query_doc,query_var,key_doc,key_var,key_obs,key_inside):
    lane=jnp.arange(HEAD)[None,:]
    var_lane=(lane>=VAR_AT)&(lane<LSE_AT)
    def tile(a): return jnp.concatenate([a,a],axis=1).astype(BF)
    qv=var_lane&((lane-VAR_AT)%8==query_var[:,None])
    q=((lane<VAR_AT)&(lane==query_doc[:,None]))|qv|(lane==OBS_AT)
    kv=var_lane&((lane-VAR_AT)%8==key_var[:,None])
    closed=(lane<VAR_AT)&~((lane==key_doc[:,None])&key_inside[:,None])
    closed=closed|((lane==OBS_AT)&(key_obs[:,None]!=1))
    ones=kv|((lane>=LSE_AT)&(lane<LSE_AT+3))
    k=jnp.where(closed,MASKED,jnp.where(ones,1.0,0.0))
    return tile(q.astype(F32)),tile(k)

def head_scales(bias_f):
    high,mid,low=thirds(bias_f[:HEADS]-bias_f[HEADS:],lambda a: lax.reduce_precision(a,8,7))
    lane=jnp.arange(HEAD)[None,:]
    part=lambda a: a[:,None]
    s=jnp.where(lane<VAR_AT,1.0,jnp.where(lane<VAR_AT+8,part(high),jnp.where(lane<VAR_AT+16,part(mid),jnp.where(lane<LSE_AT,part(low),1.0))))
    s=jnp.where(lane>OBS_AT,0.0,s)
    s=jnp.concatenate([s,s],axis=1).reshape(HEADS//4,4,LANES)
    return jnp.concatenate([s,jnp.zeros_like(s)],axis=1)

def tables(pos):
    half=HEAD//2
    freq=jnp.exp(jnp.arange(half).astype(F32)*(-2.0*math.log(10000.0)/HEAD))
    ang=pos.astype(F32)[:,None]*freq[None,:]
    c,s=jnp.cos(ang),jnp.sin(ang)
    return jnp.concatenate([c,c,c,c],axis=1),jnp.concatenate([-s,s,-s,s],axis=1)


DIGITS = 34
LOWEST = -7


def tied(*values):
    return lax.optimization_barrier(values)


def permuted(shard, axis, flip):
    return lax.ppermute(shard, axis, [(i, i ^ flip) for i in range(lax.axis_size(axis))])


def shifted(shard, by):
    size = lax.axis_size("ctx")
    return lax.ppermute(shard, "ctx", [(i, i + by) for i in range(size) if 0 <= i + by < size])


def returned_far(before, after):
    odd = lax.axis_index("ctx") % 2 == 1
    return lax.ppermute(jnp.where(odd, after, before), "ctx", [(1, 3), (2, 0)])


def returned_near(before, after, far):
    odd = lax.axis_index("ctx") % 2 == 1
    return permuted(added(jnp.where(odd, before, after), far), "ctx", 1)


def ctx_spread(part):
    size = lax.axis_size("ctx")
    return lax.all_to_all(jnp.broadcast_to(part[None], (size,) + part.shape), "ctx", 0, 0)


def halves_of(whole, core):
    half = whole.shape[0] // 2
    return lax.dynamic_slice_in_dim(whole, core * half, half, 0)


def corner_of(near, up):
    part = near.shape[0] // 2
    return jnp.concatenate([permuted(near[:part], "ctx", 2), permuted(up[part:], "ctx", 1)], axis=0)


def with_partner(piece):
    return piece, permuted(piece, "fsdp", 1)


def sides(left, core):
    count = lax.axis_size("fsdp")
    width = left.shape[1] // count
    blocks = [left[:, i * width : (i + 1) * width] for i in range(count)]
    even, odd = jnp.concatenate(blocks[0::2], axis=1), jnp.concatenate(blocks[1::2], axis=1)
    return jnp.where(core == 0, even, odd), jnp.where(core == 0, odd, even)


def added(*parts):
    return sum(part.astype(F32) for part in parts).astype(BF)


def joined(first, second):
    return jnp.concatenate([first, second], axis=0)


def core_scatter(total):
    size = lax.axis_size("fsdp")
    same_core = [[i for i in range(size) if i % 2 == core] for core in range(2)]
    return lax.psum_scatter(total, "fsdp", scatter_dimension=0, axis_index_groups=same_core, tiled=True)


def ctx_parts(part):
    size = lax.axis_size("ctx")
    return lax.all_to_all(part.reshape(size, part.shape[0] // size, part.shape[1]), "ctx", 0, 0)


def ctx_joined(parts):
    total = jnp.sum(parts.astype(F32), axis=0).astype(BF)
    return ctx_spread(total).reshape(-1, parts.shape[2])


def document_ids(doc_lengths, positions):
    doc_ends = jnp.cumsum(doc_lengths)
    return jnp.sum((positions[:, None] >= doc_ends[None, :]).astype(jnp.int32), axis=1)


def rms_scale(vector, scales):
    return vector * lax.rsqrt(jnp.mean(vector * vector, axis=-1, keepdims=True) + EPSILON) * scales


def digits_of(value):
    scaled = value * jnp.asarray(8.0 ** -(LOWEST + np.arange(DIGITS)), F32)
    return jnp.floor(scaled) - 8.0 * jnp.floor(scaled / 8.0)


def value_of(digits):
    return jnp.sum(digits * jnp.asarray(8.0 ** (LOWEST + np.arange(DIGITS)), F32))


def per_device(tokens, teacher, cotangent, lengths, variate, observed, norm_gains, var_bias, qkv_weight, out_weight, ffn_in, ffn_out):
    rows = tokens.shape[1]
    n_context = lax.axis_size("ctx")
    n_shards = lax.axis_size("fsdp")
    ext = rows + 2 * HALF
    start = lax.axis_index("ctx") * rows
    seq_len = observed.shape[1]
    gains_n = norm_gains.shape[1]
    bias_n = var_bias.shape[0]
    shard_id = lax.axis_index("fsdp")
    quartered = n_context == QUADS
    me = lax.axis_index("ctx") if quartered else jnp.int32(0)
    core = shard_id % 2 if quartered else jnp.int32(0)
    place = jnp.stack([me, core]).astype(jnp.int32)

    if quartered:
        quarter = lambda a, width, begin=0: lax.dynamic_slice_in_dim(a, begin + me * width, width, 1)
        shard = jnp.concatenate([quarter(qkv_weight, 256, i * D) for i in range(3)] + [quarter(out_weight, 256)], axis=1)
        whole = lax.all_gather(shard, "fsdp", axis=0, tiled=True)
        whole_in = lax.all_gather(quarter(ffn_in, FF // 2), "fsdp", axis=0, tiled=True)
    else:
        w_attention = jnp.concatenate([qkv_weight, out_weight], axis=1)
        w_attention = lax.all_gather(w_attention, "fsdp", axis=0, tiled=True)
        w_attention = jnp.swapaxes(w_attention.reshape(D, 4, QUADS, 256), 1, 2).reshape(D, QUADS, 1024)
        w_in = lax.all_gather(ffn_in, "fsdp", axis=0, tiled=True).reshape(D, QUADS, FF // 2)
    w_lower = lax.all_gather(ffn_out, "fsdp", axis=0, tiled=True)
    own_count = jnp.sum(observed[0])
    small = jnp.zeros((16, gains_n), BF)
    small = small.at[:4].set(norm_gains).at[4, :bias_n].set(var_bias)
    small = small.at[5, 0].set((own_count // 256).astype(BF)).at[5, 1].set((own_count % 256).astype(BF))
    if quartered:
        beside = permuted(tokens[0], "ctx", 1)
        mine = halves_of(whole, core)
        mine, small, beside = tied(mine, small, beside)
        across = lax.ppermute(beside, "ctx", [(0, 2), (3, 1)])
        odd = me % 2 == 1
        before, behind = jnp.where(odd, beside, across), jnp.where(odd, across, beside)
        near, up = permuted(mine, "ctx", 1), permuted(mine, "ctx", 2)
    else:
        before, behind = shifted(tokens[0], 1), shifted(tokens[0], -1)
        split = lambda w: (w[:, 0],) + tuple(w[i * D // 2 : (i + 1) * D // 2, j] for j in range(1, QUADS) for i in range(2))
        pieces, pieces_in = split(w_attention), split(w_in)

    small = lax.all_to_all(jnp.broadcast_to(small[None], (n_shards,) + small.shape), "fsdp", 0, 0)

    before, behind, small = tied(before, behind, small)

    gains = jnp.moveaxis(small[:, :4], 0, 1).reshape(4, D).astype(F32)
    bias = small[:, 4, :bias_n].reshape(2 * HEADS).astype(F32)
    valid_total = jnp.sum(small[:, 5, 0].astype(F32) * 256.0 + small[:, 5, 1].astype(F32))
    key_pos = start - HALF + jnp.arange(ext, dtype=jnp.int32)
    inside = (key_pos >= 0) & (key_pos < seq_len)
    key_doc = document_ids(lengths[0], key_pos)
    key_var = lax.dynamic_slice_in_dim(jnp.pad(variate[0], HALF), start, ext, 0)
    key_obs = lax.dynamic_slice_in_dim(jnp.pad(observed[0], HALF), start, ext, 0)
    own = slice(HALF, HALF + rows)
    query_feat, key_feat = features(key_doc[own], key_var[own], key_doc, key_var, key_obs, inside)
    cosine, sine = tables(key_pos)
    scales = head_scales(bias)
    mats = blockdiag()
    gain_q, gain_k = gains[2].reshape(-1, 1, 256), gains[3].reshape(-1, 1, 256)

    inputs = jnp.concatenate([before, tokens[0], behind], axis=0).astype(F32)
    inv = lax.rsqrt(jnp.mean(inputs * inputs, axis=-1, keepdims=True) + EPSILON)
    normed = (inputs * inv * gains[0]).astype(BF)

    if quartered:
        near, up, normed, whole_in = tied(near, up, normed, whole_in)
        corner = corner_of(near, up)
        mine_in = halves_of(whole_in, core)
        in_by = [permuted(mine_in, "ctx", flip) for flip in (1, 2, 3)]
        pieces = (whole,) + with_partner(near) + with_partner(up) + with_partner(corner)

    q, k, v, attn, lse, c_q, c_k, w_q, w_kv, w_attn = attention_forward(
        place, normed, pieces, gain_q, gain_k, cosine, sine, query_feat, key_feat, scales, mats
    )
    if quartered:
        in_by, attn = tied(in_by, attn)
        pieces_in = (whole_in,) + sum((with_partner(piece) for piece in in_by), ())
    mixed = tokens[0].astype(F32) + jnp.dot(attn, w_attn, preferred_element_type=F32)
    normed_two = rms_scale(mixed, gains[1]).astype(BF)
    valid_col = key_obs[own].astype(F32)[:, None]
    all_tokens = rows * n_context * n_shards
    hidden, d_gate_low, activations, d_final_low, d_mixed, d_mixed_low, d_attn, squared = feed_forward(
        place, (all_tokens / valid_total)[None], gains[1:2], valid_col, normed_two, mixed, teacher[0], cotangent[0], w_lower, w_attn, pieces_in
    )
    squared = jnp.sum(squared)

    if quartered:
        own_two, other_two = sides(normed_two, core)
        theirs = dot_tn(other_two, d_gate_low).astype(BF)
        hidden, theirs = tied(hidden, theirs)
        swapped = permuted(theirs, "fsdp", 1)
    low_grad = dot_tn(hidden, d_final_low).astype(BF)
    d_mixed_low, low_grad = tied(d_mixed_low, low_grad)
    low_part = lax.psum_scatter(low_grad, "fsdp", scatter_dimension=0, tiled=True)
    out_grad = dot_tn(attn, d_mixed_low).astype(BF)
    if quartered:
        d_gate_low, out_grad = tied(d_gate_low, out_grad)
        in_chip = (dot_tn(own_two, d_gate_low) + swapped.astype(F32)).astype(BF)
        part = lambda j: lax.dynamic_slice_in_dim(in_chip, (me ^ j) * (FF // 2), FF // 2, 1)
        cut = in_chip.shape[0] // 2
        last = part(3)
        d_attn, last = tied(d_attn, last)
        last_near, last_up = permuted(last[:cut], "ctx", 1), permuted(last[cut:], "ctx", 2)
    else:
        in_part = lax.psum_scatter(dot_tn(normed_two, d_gate_low).astype(BF), "fsdp", scatter_dimension=0, tiled=True)
        in_grad = lax.psum(in_part, "ctx").astype(F32)

    d_attn, out_grad = tied(d_attn, out_grad)
    out_part = lax.psum_scatter(out_grad, "fsdp", scatter_dimension=0, tiled=True)
    saved = (q, k, v, d_attn, attn, lse, c_q, c_k, gain_q, gain_k, cosine, sine, query_feat, key_feat, scales, mats)
    d_q1, d_kv1, gain_q1, gain_k1, bias_1 = attention_backward(place, 0, *saved)
    if quartered:
        d_q1, d_kv1, last_near, last_up = tied(d_q1, d_kv1, last_near, last_up)
        d_q1, d_kv1, low_part = tied(d_q1, d_kv1, low_part)
        own_normed, other_normed = sides(normed, core)
        theirs = [dot_tn(other_normed[own], d_q1).astype(BF), dot_tn(other_normed, d_kv1).astype(BF)]
        one, two = part(1), part(2)
        one, two = joined(one[:cut], added(one[cut:], last_up)), joined(added(two[:cut], last_near), two[cut:])
        theirs, d_q1, d_kv1, one, two = tied(theirs, d_q1, d_kv1, one, two)
        swapped = [permuted(t, "fsdp", 1) for t in theirs]
        in_near, in_up = permuted(one, "ctx", 1), permuted(two, "ctx", 2)
        first_q = (dot_tn(own_normed[own], d_q1) + swapped[0].astype(F32)).astype(BF)
        first_kv = (dot_tn(own_normed, d_kv1) + swapped[1].astype(F32)).astype(BF)
        three = jnp.concatenate([first_q[:, :256], first_kv[:, :512]], axis=1)
        one = jnp.concatenate([first_q[:, 256:], first_kv[:, 512:]], axis=1)
        d_attn, three, one = tied(d_attn, three, one)
        last_near, last_up = permuted(three[:cut], "ctx", 1), permuted(three[cut:], "ctx", 2)
        saved = saved[:3] + (d_attn,) + saved[4:]
    d_q2, d_kv2, gain_q2, gain_k2, bias_2 = attention_backward(place, 1, *saved)
    done_first = ((me ^ jnp.arange(QUADS)) % 2 == 1)[:, None, None]
    d_gain_q = jnp.where(done_first, gain_q1, gain_q2).reshape(D)
    d_gain_k = jnp.where(done_first, gain_k1, gain_k2).reshape(D)
    same = jnp.sum(jnp.where(done_first, bias_1, bias_2)[:, :4], axis=-1).reshape(HEADS)
    d_bias = jnp.concatenate([same, -same])

    if quartered:
        extra = jnp.zeros((n_shards, D // n_shards, LANES), F32)
        extra = extra.at[:, 0, :gains_n].set(d_gain_q.reshape(n_shards, gains_n)).at[:, 1, :gains_n].set(d_gain_k.reshape(n_shards, gains_n))
        extra = extra.at[:, 2, :bias_n].set(d_bias.reshape(n_shards, bias_n)).at[:, 3, :DIGITS].set(digits_of(squared)[None])
        extra = extra.reshape(n_shards // 2, 2, D // n_shards, LANES).astype(BF)
        own_extra = jnp.where(core == 0, extra[:, 0], extra[:, 1]).reshape(-1, LANES)
        other_extra = jnp.where(core == 0, extra[:, 1], extra[:, 0]).reshape(-1, LANES)
        d_q2, d_kv2, last_near, last_up = tied(d_q2, d_kv2, last_near, last_up)
        d_q2, d_kv2, in_near, in_up, out_part = tied(d_q2, d_kv2, in_near, in_up, out_part)
        in_total = added(part(0), in_near, in_up)
        d_q2, d_kv2, in_total = tied(d_q2, d_kv2, in_total)
        in_part = core_scatter(in_total)
        other_grads = ctx_parts(joined(out_part, low_part))
    d_ext = dot_nt(d_kv1, w_kv[:, : 2 * 512]) + dot_nt(d_kv2, w_kv[:, 2 * 512 :])
    to_before, to_behind = d_ext[:HALF].astype(BF), d_ext[HALF + rows :].astype(BF)
    if quartered:
        to_before, to_behind, d_q2, d_kv2 = tied(to_before, to_behind, d_q2, d_kv2)
        far = returned_far(to_before, to_behind)
        theirs = [dot_tn(other_normed[own], d_q2).astype(BF), dot_tn(other_normed, d_kv2).astype(BF), other_extra]
        theirs, d_q2, d_kv2, other_grads = tied(theirs, d_q2, d_kv2, other_grads)
        other_grads = ctx_joined(other_grads)
        swapped = [permuted(t, "fsdp", 1) for t in theirs]
        second_q = (dot_tn(own_normed[own], d_q2) + swapped[0].astype(F32)).astype(BF)
        second_kv = (dot_tn(own_normed, d_kv2) + swapped[1].astype(F32)).astype(BF)
        two = jnp.concatenate([second_q[:, :256], second_kv[:, :512]], axis=1)
        one = joined(one[:cut], added(one[cut:], last_up))
        two = joined(added(two[:cut], last_near), two[cut:])
        one, two, far = tied(one, two, far)
        near, up = permuted(one, "ctx", 1), permuted(two, "ctx", 2)
        in_part, other_grads, far = tied(in_part, other_grads, far)
        near, up, in_part, far = tied(near, up, in_part, far)
        from_others = returned_near(to_before, to_behind, far)
        in_spread = ctx_spread(in_part)
        qkv_total = added(jnp.concatenate([second_q[:, 256:], second_kv[:, 512:]], axis=1), near, up)
        qkv_total = jnp.concatenate([qkv_total, added(own_extra, swapped[2])], axis=1)
        qkv_part = core_scatter(qkv_total)
        qkv_part, in_spread = tied(qkv_part, in_spread)
        spread = ctx_spread(qkv_part)
        from_others, spread = tied(from_others, spread)
        from_others = from_others.astype(F32)
        qkv_grad, gain_one = finish(spread, qkv_weight, tuple((i * 256, 256, i * D) for i in range(3)))
        sums = jnp.sum(spread[:, :, 3 * 256 :].astype(F32), axis=0)
        squared = value_of(sums[3, :DIGITS])
        gain_rows, var_bias_grad = sums[:2, :gains_n], sums[2, :bias_n]
        in_grad, gain_two = finish(in_spread, ffn_in, ((0, FF // 2, 0),))
    else:
        from_others = shifted(to_before, -1).astype(F32) + shifted(to_behind, 1).astype(F32)
        order = [SEND_ORDER.index(j) for j in range(QUADS)]
        natural = lambda first, second, width: jnp.concatenate([first, second], axis=1).reshape(-1, QUADS, width)[:, jnp.array(order)]
        grad_q = dot_tn(normed[own], natural(d_q1, d_q2, 256).reshape(rows, D))
        grad_kv = dot_tn(normed, jnp.swapaxes(natural(d_kv1, d_kv2, 512).reshape(ext, QUADS, 2, 256), 1, 2).reshape(ext, 2 * D))
        grad_qkv = jnp.concatenate([grad_q, grad_kv], axis=1).astype(BF)
        qkv_grad = lax.psum(lax.psum_scatter(grad_qkv, "fsdp", scatter_dimension=0, tiled=True), "ctx").astype(F32)
        other_grads = lax.psum(joined(out_part, low_part), "ctx").astype(F32)
        sums = jnp.concatenate([d_gain_q, d_gain_k, d_bias, squared[None]])
        sums = lax.psum(jnp.pad(sums, (0, -sums.shape[0] % (8 * LANES))).reshape(-1, LANES), ("ctx", "fsdp")).reshape(-1)
        gain_rows = lax.dynamic_slice_in_dim(sums[: 2 * D].reshape(2, D), shard_id * gains_n, gains_n, 1)
        var_bias_grad = lax.dynamic_slice_in_dim(sums[2 * D : 2 * D + 2 * HEADS], shard_id * bias_n, bias_n, 0)
        squared = sums[2 * D + 2 * HEADS]
    d_own = d_ext[own] + dot_nt(d_q1, w_q[:, : 2 * 256]) + dot_nt(d_q2, w_q[:, 2 * 256 :])
    loss = squared / (valid_total * D)
    own_gains = norm_gains.astype(F32)
    if not quartered:
        gain_one = jnp.sum(qkv_weight.astype(F32) * qkv_grad, axis=1)
        gain_two = jnp.sum(ffn_in.astype(F32) * in_grad, axis=1)
    gain_one, gain_two = gain_one.reshape(1, -1) / own_gains[:1], gain_two.reshape(1, -1) / own_gains[1:2]
    gains_grad = jnp.concatenate([gain_one, gain_two, gain_rows], axis=0)
    unit = inputs[own] * inv[own]
    scaled = (d_own + from_others) * gains[0]
    input_grad = d_mixed + inv[own] * (scaled - unit * jnp.mean(unit * scaled, axis=-1, keepdims=True))
    other_grads = other_grads.astype(F32)
    return (
        loss,
        activations[None],
        input_grad[None],
        gains_grad,
        var_bias_grad,
        qkv_grad,
        other_grads[: out_part.shape[0]],
        in_grad,
        other_grads[out_part.shape[0] :],
    )


def solution(mesh):
    split = P("fsdp", "ctx", None)
    rows = P("fsdp", None)
    return jax.shard_map(
        per_device,
        mesh=mesh,
        in_specs=(split, split, split, rows, rows, rows, P(None, "fsdp"), P("fsdp"), rows, rows, rows, rows),
        out_specs=(P(), split, split, P(None, "fsdp"), P("fsdp"), rows, rows, rows, rows),
        check_vma=False,
    )
```

```python
import math

import jax
import jax.numpy as jnp
import numpy as np
from jax import lax
from jax.experimental import pallas as pl
from jax.experimental.pallas import tpu as pltpu
from jax.sharding import PartitionSpec as P


D=1024; HEADS=16; HEAD=64; FF=2816; WINDOW=1024
EPSILON=1e-6; MASKED=-1e30
HALF=WINDOW//2
LANES=128
VAR_AT, LSE_AT, OBS_AT = 8, 32, 35
TILE=256
F32=jnp.float32; BF=jnp.bfloat16


def dot_nn(a,b): return lax.dot_general(a,b,(((1,),(0,)),((),())),preferred_element_type=F32)
def dot_nt(a,b): return lax.dot_general(a,b,(((1,),(1,)),((),())),preferred_element_type=F32)
def dot_tn(a,b): return lax.dot_general(a,b,(((0,),(0,)),((),())),preferred_element_type=F32)

def halves(v):
    high=v.astype(BF)
    return jnp.concatenate([high,(v-high.astype(F32)).astype(BF)],axis=1)

def thirds(v,rounded=lambda a: a.astype(BF).astype(F32)):
    high=rounded(v)
    rest=v-high
    mid=rounded(rest)
    return high,mid,rest-mid

def lane_of(shape): return lax.broadcasted_iota(jnp.int32,shape,1)

def place(v,at):
    high,mid,low=thirds(v)
    lane=lane_of(v.shape)%HEAD
    return jnp.where(lane==at,high,jnp.where(lane==at+1,mid,jnp.where(lane==at+2,low,0.0)))

def band(s,t,tiles,key_axis):
    if t not in (0,tiles-1): return s
    key=lax.broadcasted_iota(jnp.int32,s.shape,key_axis)
    query=lax.broadcasted_iota(jnp.int32,s.shape,1-key_axis)
    keep=key>=query if t==0 else key<=query
    return jnp.where(keep,s,MASKED)

def prep(u,gain,cosine,sine,mean_mat,swap_mat):
    mean=dot_nn(halves(u*u),mean_mat)
    c=lax.rsqrt(mean+EPSILON)
    n=u*c*gain
    return n*cosine+dot_nn(halves(n),swap_mat)*sine, c

QUADS=4
SEND_ORDER=(3,1,2,0)
def position(slot): return jnp.where(slot==0,3,jnp.where(slot==3,0,slot))

def piece_copies(place_ref,pieces,w_ref,sem):
    me,core=place_ref[0],place_ref[1]
    half=w_ref.shape[1]//2
    copies=[[pltpu.make_async_copy(pieces[0],w_ref.at[me],sem.at[0])]]
    for slot in range(1,QUADS):
        copies.append([pltpu.make_async_copy(pieces[2*slot-1+side],
            w_ref.at[me^slot,pl.ds(pl.multiple_of((core if side==0 else 1-core)*half,half),half),:],sem.at[2*slot-1+side]) for side in range(2)])
    return copies

def await_quarter(place_ref,pieces,w_ref,sem):
    step=pl.program_id(0)
    copies=piece_copies(place_ref,pieces,w_ref,sem)
    @pl.when(step==0)
    def _():
        for group in copies:
            for copy in group: copy.start()
    slot=step^place_ref[0]
    for i,group in enumerate(copies):
        @pl.when(slot==i)
        def _(group=group):
            for copy in group: copy.wait()

def fwd_kernel(place_ref,xn_ref,p0,p1,p2,p3,p4,p5,p6,gq_ref,gk_ref,cos_ref,sin_ref,qb_ref,kb_ref,sv_ref,mean_ref,swap_ref,
               q_ref,k_ref,v_ref,attn_ref,lse_ref,cq_ref,ck_ref,wq_out,wkv_out,wattn_out,w_ref,sem):
    rows=qb_ref.shape[0]; ext=kb_ref.shape[0]
    await_quarter(place_ref,(p0,p1,p2,p3,p4,p5,p6),w_ref,sem)
    quad=pl.program_id(0)
    wq_out[...]=w_ref[quad,:,0:256]
    wkv_out[...]=w_ref[quad,:,256:768]
    wattn_out[...]=w_ref[quad,:,768:1024]
    tiles=2*HALF//TILE+1
    mean_mat=mean_ref[...]; swap_mat=swap_ref[...]
    first=(lane_of((1,LANES))<HEAD)
    kf=dot_nn(xn_ref[...],w_ref[quad,:,256:512])
    for pair in range(2):
        col=slice(pair*LANES,(pair+1)*LANES)
        rot,c=prep(kf[:,col],gk_ref[:,col],cos_ref[...],sin_ref[...],mean_mat,swap_mat)
        k_ref[:,col]=rot.astype(BF)
        if pair==0: ck_ref[...]=c
        else: ck_ref[...]=jnp.where(lane_of((1,LANES))%HEAD==pair,c,ck_ref[...])
    v_ref[...]=dot_nn(xn_ref[...],w_ref[quad,:,512:768]).astype(BF)
    qf=dot_nn(xn_ref[HALF:HALF+rows,:],w_ref[quad,:,0:256])
    for pair in range(2):
        col=slice(pair*LANES,(pair+1)*LANES)
        rot,c=prep(qf[:,col],gq_ref[:,col],cos_ref[HALF:HALF+rows,:],sin_ref[HALF:HALF+rows,:],mean_mat,swap_mat)
        q_ref[:,col]=rot.astype(BF)
        if pair==0: cq_ref[...]=c
        else: cq_ref[...]=jnp.where(lane_of((1,LANES))%HEAD==pair,c,cq_ref[...])
    own=[first.astype(F32).astype(BF),(1.0-first.astype(F32)).astype(BF)]
    no_obs=(lane_of((1,LANES))%HEAD!=OBS_AT).astype(F32).astype(BF)
    diag=lax.broadcasted_iota(jnp.int32,(TILE,TILE),0)==lax.broadcasted_iota(jnp.int32,(TILE,TILE),1)
    for pair in range(2):
        col=slice(pair*LANES,(pair+1)*LANES)
        for i in range(rows//TILE):
            sums=[]
            for par in range(2):
                m,other=own[par],own[1-par]
                sv=sv_ref[2*pair+par:2*pair+par+1,:].astype(BF)*other
                qi=q_ref[i*TILE:(i+1)*TILE,col]*BF(HEAD**-0.5)*m+qb_ref[i*TILE:(i+1)*TILE,:]*sv
                acc=None
                for t in range(tiles):
                    at=slice((i+t)*TILE,(i+t+1)*TILE)
                    kt=k_ref[at,col]*m+kb_ref[at,:]*other
                    vt=v_ref[at,col]*m+other
                    s=band(dot_nt(qi,kt),t,tiles,1)
                    if t==tiles//2:
                        s=jnp.where(diag,dot_nt(qi*(m+other*no_obs),kt),s)
                    p=jnp.exp(s).astype(BF)
                    o=dot_nn(p,vt)
                    acc=o if acc is None else acc+o
                sums.append(acc)
            total=jnp.where(first,sums[1],sums[0])
            lse_ref[i*TILE:(i+1)*TILE,col]=jnp.log(total)
            out=jnp.where(first,sums[0],sums[1])/pltpu.roll(total,HEAD,1)
            attn_ref[i*TILE:(i+1)*TILE,col]=out.astype(BF)

def prep_back(rot,d_rot,c,gain,cosine,sine,mean_mat,swap_mat):
    x=rot.astype(F32)
    m=dot_nn(halves(x*d_rot),mean_mat)
    e=d_rot*cosine-dot_nn(halves(d_rot),swap_mat)*sine
    swapped=dot_nn(rot,swap_mat[:LANES])
    n=(x*cosine-swapped*sine)/gain
    return c*(gain*e-n*m), jnp.sum(e*n,axis=0,keepdims=True)

def bwd_kernel(place_ref,q_ref,k_ref,v_ref,do_ref,attn_ref,lse_ref,cq_ref,ck_ref,gq_ref,gk_ref,cos_ref,sin_ref,qb_ref,kb_ref,sv_ref,
               mean_ref,swap_ref,cross_ref,spread_ref,
               dq_ref,dkv_ref,dgq_ref,dgk_ref,bias_ref,dk_acc,dv_acc,ke_ref,ve_ref):
    rows=qb_ref.shape[0]; ext=kb_ref.shape[0]
    tiles=2*HALF//TILE+1
    mean_mat=mean_ref[...]; swap_mat=swap_ref[...]
    first=(lane_of((1,LANES))<HEAD)
    own=[first.astype(F32).astype(BF),(1.0-first.astype(F32)).astype(BF)]
    no_obs=(lane_of((1,LANES))%HEAD!=OBS_AT).astype(F32).astype(BF)
    diag=lax.broadcasted_iota(jnp.int32,(TILE,TILE),0)==lax.broadcasted_iota(jnp.int32,(TILE,TILE),1)
    lane=lane_of((1,LANES))%HEAD
    is_var=(lane>=VAR_AT)&(lane<VAR_AT+8)
    bias_ref[...]=jnp.zeros_like(bias_ref)
    def one_pair(pair,_):
        col=pl.ds(pl.multiple_of(pair*LANES,LANES),LANES)
        dk_acc[...]=jnp.zeros_like(dk_acc)
        dv_acc[...]=jnp.zeros_like(dv_acc)
        prod=do_ref[:,col].astype(F32)*attn_ref[:,col].astype(F32)
        delta=place(dot_nn(halves(prod),cross_ref[...]),0).astype(BF)
        lse=place(lse_ref[:,col],LSE_AT).astype(BF)
        dqs=[]
        for par in range(2):
            m,other=own[par],own[1-par]
            head=2*pair+par
            sv=sv_ref[pl.ds(head,1),:].astype(BF)*other
            qm=q_ref[:,col]*BF(HEAD**-0.5)*m
            qe=qm+qb_ref[...]*sv-lse*other
            dm=do_ref[:,col]*m
            de=dm-delta*other
            ke_ref[...]=k_ref[:,col]*m+kb_ref[...]*other
            ve_ref[...]=v_ref[:,col]*m+other
            parts=[]
            for i in range(rows//TILE):
                r=slice(i*TILE,(i+1)*TILE)
                dq=None
                for t in range(tiles):
                    at=slice((i+t)*TILE,(i+t+1)*TILE)
                    kt=ke_ref[at,:]
                    s=band(dot_nt(kt,qe[r]),t,tiles,0)
                    if t==tiles//2:
                        s=jnp.where(diag,dot_nt(kt,qe[r]*(m+other*no_obs)),s)
                    p=jnp.exp(s)
                    ds=(p*dot_nt(ve_ref[at,:],de[r])).astype(BF)
                    dv_acc[at,:]+=dot_nn(p.astype(BF),dm[r])
                    dk_acc[at,:]+=dot_nn(ds,qm[r])
                    part=dot_tn(ds,kt)
                    dq=part if dq is None else dq+part
                parts.append(dq)
            dq=jnp.concatenate(parts,axis=0)
            hot=jnp.where(is_var&(first!=(par==0)),dq*qb_ref[...].astype(F32),0.0)
            bias_ref[pl.ds(head,1),:]=jnp.sum(hot,axis=0,keepdims=True)
            dqs.append(dq)
        d_rot=jnp.where(first,dqs[0],dqs[1])*(HEAD**-0.5)
        spread=spread_ref[pair]
        cosq,sinq=cos_ref[HALF:HALF+rows,:],sin_ref[HALF:HALF+rows,:]
        du,dg=prep_back(q_ref[:,col],d_rot,dot_nn(halves(cq_ref[...]),spread),gq_ref[:,col],cosq,sinq,mean_mat,swap_mat)
        dq_ref[:,col]=du.astype(BF)
        dgq_ref[:,col]=dg
        du,dg=prep_back(k_ref[:,col],dk_acc[...],dot_nn(halves(ck_ref[...]),spread),gk_ref[:,col],cos_ref[...],sin_ref[...],mean_mat,swap_mat)
        dkv_ref[:,col]=du.astype(BF)
        dgk_ref[:,col]=dg
        dkv_ref[:,pl.ds(pl.multiple_of(256+pair*LANES,LANES),LANES)]=dv_acc[...].astype(BF)
        return 0
    lax.fori_loop(0,2,one_pair,0)

def blockdiag():
    i=jnp.arange(LANES)
    mean=jnp.where(i[:,None]//HEAD==i[None]//HEAD,1.0/HEAD,0.0)
    cross=jnp.where(i[:,None]//HEAD!=i[None]//HEAD,1.0,0.0)
    swap=jnp.where(i[None]==i[:,None]+jnp.where(i[:,None]%HEAD<HEAD//2,HEAD//2,-(HEAD//2)),1.0,0.0)
    spread=jnp.stack([jnp.where(i[:,None]==pair+HEAD*(i[None]//HEAD),1.0,0.0) for pair in range(2)])
    two=lambda a: jnp.concatenate([a,a],axis=-2).astype(BF)
    return two(mean),two(swap),two(cross),two(spread)

def full(*shape):
    n=len(shape)
    return pl.BlockSpec(shape,lambda j,s:(0,)*n)
def colb(rows,width): return pl.BlockSpec((rows,width),lambda j,s:(0,j))
def lead(*shape): return pl.BlockSpec((None,)+shape,lambda j,s:(j,)+(0,)*len(shape))
ANYWHERE=pl.BlockSpec(memory_space=pltpu.HBM)

def attention_forward(place,xn,pieces,gq,gk,cos,sin,qb,kb,sv,mats):
    rows,ext=qb.shape[0],kb.shape[0]
    mean_mat,swap_mat,_,_=mats
    n=QUADS*256
    at=lambda j,s:(0,position(j^s[0]))
    return pl.pallas_call(
        fwd_kernel,
        grid_spec=pltpu.PrefetchScalarGridSpec(
            num_scalar_prefetch=1,grid=(QUADS,),
            in_specs=[full(ext,D)]+[ANYWHERE]*7+[lead(1,256),lead(1,256),full(ext,LANES),full(ext,LANES),
                      full(rows,LANES),full(ext,LANES),lead(8,LANES),full(2*LANES,LANES),full(2*LANES,LANES)],
            out_specs=[colb(rows,256),colb(ext,256),colb(ext,256),colb(rows,256),colb(rows,256),lead(rows,LANES),lead(ext,LANES),
                       pl.BlockSpec((D,256),at),pl.BlockSpec((D,512),at),colb(D,256)],
            scratch_shapes=[pltpu.VMEM((QUADS,D,1024),BF),pltpu.SemaphoreType.DMA((7,))]),
        out_shape=[jax.ShapeDtypeStruct((rows,n),BF),jax.ShapeDtypeStruct((ext,n),BF),jax.ShapeDtypeStruct((ext,n),BF),
                   jax.ShapeDtypeStruct((rows,n),BF),jax.ShapeDtypeStruct((rows,n),F32),
                   jax.ShapeDtypeStruct((QUADS,rows,LANES),F32),jax.ShapeDtypeStruct((QUADS,ext,LANES),F32),
                   jax.ShapeDtypeStruct((D,n),BF),jax.ShapeDtypeStruct((D,2*n),BF),jax.ShapeDtypeStruct((D,n),BF)],
        compiler_params=pltpu.CompilerParams(vmem_limit_bytes=56*2**20),
        cost_estimate=pl.CostEstimate(flops=10**6, bytes_accessed=10**4, transcendentals=0),
        name="attention_forward",
    )(place,xn,*pieces,gq,gk,cos,sin,qb,kb,sv,mean_mat,swap_mat)

def feed_forward_kernel(place_ref,weight_ref,gain_ref,obs_ref,x_in,mixed_in,teacher_in,cot_in,low_in,attn_in,p0,p1,p2,p3,p4,p5,p6,
                        hidden_out,d_up_out,act_out,d_low_out,d_mixed_out,d_mixed_low_out,d_attn_out,sum_ref,
                        w_ref,low_ref,attn_ref,x_ref,mixed_ref,teacher_ref,cot_ref,gate_up_ref,hidden_ref,act_ref,d_low_ref,d_final_ref,acc_ref,
                        in_sem,piece_sem,out_sem):
    arrivals=[pltpu.make_async_copy(src,dst,in_sem.at[i]) for i,(src,dst) in enumerate(
        [(x_in,x_ref),(mixed_in,mixed_ref),(low_in,low_ref),(teacher_in,teacher_ref),(cot_in,cot_ref),(attn_in,attn_ref)])]
    pieces=piece_copies(place_ref,(p0,p1,p2,p3,p4,p5,p6),w_ref,piece_sem)
    arrivals[0].start()
    for group in pieces:
        for copy in group: copy.start()
    for copy in arrivals[1:]: copy.start()
    sent=[]
    def send(ref,out):
        copy=pltpu.make_async_copy(ref,out,out_sem.at[len(sent)])
        copy.start(); sent.append(copy)
    arrivals[0].wait()
    width=w_ref.shape[2]
    tiles=[slice(begin,min(begin+256,width)) for begin in range(0,width,256)]
    for half in range(2):
        for quarter in (half,half+2):
            slot=place_ref[0]^quarter
            for i,group in enumerate(pieces):
                @pl.when(slot==i)
                def _(group=group):
                    for copy in group: copy.wait()
        for tile in tiles:
            at=slice(half*width+tile.start,half*width+tile.stop); up_at=slice(FF+at.start,FF+at.stop)
            gate=dot_nn(x_ref[...],w_ref[half,:,tile])
            up=dot_nn(x_ref[...],w_ref[half+2,:,tile])
            gate_up_ref[:,at]=gate.astype(BF)
            gate_up_ref[:,up_at]=up.astype(BF)
            hidden_ref[:,at]=(gate/(1.0+jnp.exp(-gate))*up).astype(BF)
    send(hidden_ref,hidden_out)
    for copy in arrivals[1:]: copy.wait()
    total=jnp.zeros((1,256),F32)
    for begin in range(0,D,256):
        cols=slice(begin,begin+256)
        final=mixed_ref[:,cols]+dot_nn(hidden_ref[...],low_ref[:,cols])
        act_ref[:,cols]=final.astype(BF)
        distance=final-teacher_ref[:,cols].astype(F32)
        seen=obs_ref[...]*distance
        total=total+jnp.sum(seen*distance,axis=0,keepdims=True)
        d_final=cot_ref[:,cols].astype(F32)+weight_ref[0]*seen
        d_final_ref[:,cols]=d_final
        d_low_ref[:,cols]=d_final.astype(BF)
    sum_ref[...]=total
    send(act_ref,act_out)
    send(d_low_ref,d_low_out)
    for begin in range(0,FF,256):
        cols=slice(begin,begin+256); ups=slice(FF+begin,FF+begin+256)
        d_hidden=dot_nt(d_low_ref[...],low_ref[cols,:])
        gate=gate_up_ref[:,cols].astype(F32); up=gate_up_ref[:,ups].astype(F32)
        sig=1.0/(1.0+jnp.exp(-gate))
        gate_up_ref[:,cols]=(d_hidden*up*(sig*(1.0+gate*(1.0-sig)))).astype(BF)
        gate_up_ref[:,ups]=(d_hidden*(gate*sig)).astype(BF)
    send(gate_up_ref,d_up_out)
    for begin in range(0,D,256):
        part=None
        for quarter in range(QUADS):
            one=dot_nt(gate_up_ref[:,quarter*width:(quarter+1)*width],w_ref[quarter,begin:begin+256,:])
            part=one if part is None else part+one
        acc_ref[:,begin:begin+256]=part
    mixed=mixed_ref[...]
    c=lax.rsqrt(jnp.mean(mixed*mixed,axis=1,keepdims=True)+EPSILON)
    scaled=acc_ref[...]*gain_ref[...]
    unit=mixed*c
    d_mixed=d_final_ref[...]+c*(scaled-unit*jnp.mean(unit*scaled,axis=1,keepdims=True))
    d_final_ref[...]=d_mixed
    send(d_final_ref,d_mixed_out)
    x_ref[...]=d_mixed.astype(BF)
    send(x_ref,d_mixed_low_out)
    for begin in range(0,D,256):
        teacher_ref[:,begin:begin+256]=dot_nt(x_ref[...],attn_ref[begin:begin+256,:]).astype(BF)
    send(teacher_ref,d_attn_out)
    for copy in sent: copy.wait()

def feed_forward(place,weight,gain,obs,x,mixed,teacher,cotangent,w_lower,w_attn,pieces):
    rows=x.shape[0]; width=pieces[0].shape[1]
    low=jax.ShapeDtypeStruct((rows,D),BF)
    smem=pl.BlockSpec(memory_space=pltpu.SMEM); vmem=pl.BlockSpec(memory_space=pltpu.VMEM)
    square=pltpu.VMEM((rows,D),BF); wide=pltpu.VMEM((rows,D),F32)
    return pl.pallas_call(
        feed_forward_kernel,
        in_specs=[smem,smem,vmem,vmem]+[ANYWHERE]*13,
        out_specs=[ANYWHERE]*7+[vmem],
        out_shape=[jax.ShapeDtypeStruct((rows,FF),BF),jax.ShapeDtypeStruct((rows,2*FF),BF),low,low,jax.ShapeDtypeStruct((rows,D),F32),low,low,
                   jax.ShapeDtypeStruct((1,256),F32)],
        scratch_shapes=[pltpu.VMEM((QUADS,D,width),BF),pltpu.VMEM((FF,D),BF),pltpu.VMEM((D,D),BF),square,wide,square,square,
                        pltpu.VMEM((rows,2*FF),BF),pltpu.VMEM((rows,FF),BF),square,square,wide,wide,
                        pltpu.SemaphoreType.DMA((6,)),pltpu.SemaphoreType.DMA((7,)),pltpu.SemaphoreType.DMA((7,))],
        compiler_params=pltpu.CompilerParams(vmem_limit_bytes=58*2**20),
        cost_estimate=pl.CostEstimate(flops=10**6, bytes_accessed=10**4, transcendentals=0),
        name="feed_forward",
    )(place,weight,gain,obs,x,mixed,teacher,cotangent,w_lower,w_attn,*pieces)

def attention_backward(place,call,q,k,v,do,attn,lse,cq,ck,gq,gk,cos,sin,qb,kb,sv,mats):
    rows,ext=qb.shape[0],kb.shape[0]
    def quad(j,s): return s[0]^jnp.where(j==0,SEND_ORDER[2*call],SEND_ORDER[2*call+1])
    def col(rows,width): return pl.BlockSpec((rows,width),lambda j,s:(0,quad(j,s)))
    def led(*shape): return pl.BlockSpec((None,)+shape,lambda j,s:(quad(j,s),)+(0,)*len(shape))
    return pl.pallas_call(
        bwd_kernel,
        grid_spec=pltpu.PrefetchScalarGridSpec(
            num_scalar_prefetch=1,grid=(2,),
            in_specs=[col(rows,256),col(ext,256),col(ext,256),col(rows,256),col(rows,256),col(rows,256),led(rows,LANES),led(ext,LANES),
                      led(1,256),led(1,256),full(ext,LANES),full(ext,LANES),full(rows,LANES),full(ext,LANES),led(8,LANES),
                      full(2*LANES,LANES),full(2*LANES,LANES),full(2*LANES,LANES),full(2,2*LANES,LANES)],
            out_specs=[colb(rows,256),colb(ext,512),led(1,256),led(1,256),led(8,LANES)],
            scratch_shapes=[pltpu.VMEM((ext,LANES),F32),pltpu.VMEM((ext,LANES),F32),pltpu.VMEM((ext,LANES),BF),pltpu.VMEM((ext,LANES),BF)]),
        out_shape=[jax.ShapeDtypeStruct((rows,512),BF),jax.ShapeDtypeStruct((ext,1024),BF),
                   jax.ShapeDtypeStruct((QUADS,1,256),F32),jax.ShapeDtypeStruct((QUADS,1,256),F32),jax.ShapeDtypeStruct((QUADS,8,LANES),F32)],
        compiler_params=pltpu.CompilerParams(vmem_limit_bytes=56*2**20),
        cost_estimate=pl.CostEstimate(flops=10**6, bytes_accessed=10**4, transcendentals=0),
        name="attention_backward",
    )(place,q,k,v,do,attn,lse,cq,ck,gq,gk,cos,sin,qb,kb,sv,*mats)

def finish_kernel(layout,spread_ref,weight_ref,grad_ref,sum_ref):
    total=None
    for quarter in range(QUADS):
        for begin,width,base in layout:
            at=slice(base+quarter*width,base+(quarter+1)*width)
            grad=spread_ref[quarter,:,begin:begin+width].astype(F32)
            grad_ref[:,at]=grad
            part=jnp.sum(grad*weight_ref[:,at].astype(F32),axis=1,keepdims=True)
            total=part if total is None else total+part
    sum_ref[...]=total

def finish(spread,weight,layout):
    vmem=pl.BlockSpec(memory_space=pltpu.VMEM)
    return pl.pallas_call(
        lambda *refs: finish_kernel(layout,*refs),in_specs=[vmem]*2,out_specs=[vmem]*2,
        out_shape=[jax.ShapeDtypeStruct(weight.shape,F32),jax.ShapeDtypeStruct((weight.shape[0],1),F32)],
        compiler_params=pltpu.CompilerParams(vmem_limit_bytes=32*2**20),
        cost_estimate=pl.CostEstimate(flops=10**6, bytes_accessed=10**4, transcendentals=0),
        name="finish",
    )(spread,weight)

def features(query_doc,query_var,key_doc,key_var,key_obs,key_inside):
    lane=jnp.arange(HEAD)[None,:]
    var_lane=(lane>=VAR_AT)&(lane<LSE_AT)
    def tile(a): return jnp.concatenate([a,a],axis=1).astype(BF)
    qv=var_lane&((lane-VAR_AT)%8==query_var[:,None])
    q=((lane<VAR_AT)&(lane==query_doc[:,None]))|qv|(lane==OBS_AT)
    kv=var_lane&((lane-VAR_AT)%8==key_var[:,None])
    closed=(lane<VAR_AT)&~((lane==key_doc[:,None])&key_inside[:,None])
    closed=closed|((lane==OBS_AT)&(key_obs[:,None]!=1))
    ones=kv|((lane>=LSE_AT)&(lane<LSE_AT+3))
    k=jnp.where(closed,MASKED,jnp.where(ones,1.0,0.0))
    return tile(q.astype(F32)),tile(k)

def head_scales(bias_f):
    high,mid,low=thirds(bias_f[:HEADS]-bias_f[HEADS:],lambda a: lax.reduce_precision(a,8,7))
    lane=jnp.arange(HEAD)[None,:]
    part=lambda a: a[:,None]
    s=jnp.where(lane<VAR_AT,1.0,jnp.where(lane<VAR_AT+8,part(high),jnp.where(lane<VAR_AT+16,part(mid),jnp.where(lane<LSE_AT,part(low),1.0))))
    s=jnp.where(lane>OBS_AT,0.0,s)
    s=jnp.concatenate([s,s],axis=1).reshape(HEADS//4,4,LANES)
    return jnp.concatenate([s,jnp.zeros_like(s)],axis=1)

def tables(pos):
    half=HEAD//2
    freq=jnp.exp(jnp.arange(half).astype(F32)*(-2.0*math.log(10000.0)/HEAD))
    ang=pos.astype(F32)[:,None]*freq[None,:]
    c,s=jnp.cos(ang),jnp.sin(ang)
    return jnp.concatenate([c,c,c,c],axis=1),jnp.concatenate([-s,s,-s,s],axis=1)


DIGITS = 34
LOWEST = -7


def tied(*values):
    return lax.optimization_barrier(values)


def permuted(shard, axis, flip):
    return lax.ppermute(shard, axis, [(i, i ^ flip) for i in range(lax.axis_size(axis))])


def shifted(shard, by):
    size = lax.axis_size("ctx")
    return lax.ppermute(shard, "ctx", [(i, i + by) for i in range(size) if 0 <= i + by < size])


def returned_far(before, after):
    odd = lax.axis_index("ctx") % 2 == 1
    return lax.ppermute(jnp.where(odd, after, before), "ctx", [(1, 3), (2, 0)])


def returned_near(before, after, far):
    odd = lax.axis_index("ctx") % 2 == 1
    return permuted(added(jnp.where(odd, before, after), far), "ctx", 1)


def ctx_spread(part):
    size = lax.axis_size("ctx")
    return lax.all_to_all(jnp.broadcast_to(part[None], (size,) + part.shape), "ctx", 0, 0)


def halves_of(whole, core):
    half = whole.shape[0] // 2
    return lax.dynamic_slice_in_dim(whole, core * half, half, 0)


def corner_of(near, up):
    part = near.shape[0] // 2
    return jnp.concatenate([permuted(near[:part], "ctx", 2), permuted(up[part:], "ctx", 1)], axis=0)


def with_partner(piece):
    return piece, permuted(piece, "fsdp", 1)


def sides(left, core):
    count = lax.axis_size("fsdp")
    width = left.shape[1] // count
    blocks = [left[:, i * width : (i + 1) * width] for i in range(count)]
    even, odd = jnp.concatenate(blocks[0::2], axis=1), jnp.concatenate(blocks[1::2], axis=1)
    return jnp.where(core == 0, even, odd), jnp.where(core == 0, odd, even)


def added(*parts):
    return sum(part.astype(F32) for part in parts).astype(BF)


def joined(first, second):
    return jnp.concatenate([first, second], axis=0)


def core_scatter(total):
    size = lax.axis_size("fsdp")
    same_core = [[i for i in range(size) if i % 2 == core] for core in range(2)]
    return lax.psum_scatter(total, "fsdp", scatter_dimension=0, axis_index_groups=same_core, tiled=True)


def ctx_parts(part):
    size = lax.axis_size("ctx")
    return lax.all_to_all(part.reshape(size, part.shape[0] // size, part.shape[1]), "ctx", 0, 0)


def ctx_joined(parts):
    total = jnp.sum(parts.astype(F32), axis=0).astype(BF)
    return ctx_spread(total).reshape(-1, parts.shape[2])


def document_ids(doc_lengths, positions):
    doc_ends = jnp.cumsum(doc_lengths)
    return jnp.sum((positions[:, None] >= doc_ends[None, :]).astype(jnp.int32), axis=1)


def rms_scale(vector, scales):
    return vector * lax.rsqrt(jnp.mean(vector * vector, axis=-1, keepdims=True) + EPSILON) * scales


def digits_of(value):
    scaled = value * jnp.asarray(8.0 ** -(LOWEST + np.arange(DIGITS)), F32)
    return jnp.floor(scaled) - 8.0 * jnp.floor(scaled / 8.0)


def value_of(digits):
    return jnp.sum(digits * jnp.asarray(8.0 ** (LOWEST + np.arange(DIGITS)), F32))


def per_device(tokens, teacher, cotangent, lengths, variate, observed, norm_gains, var_bias, qkv_weight, out_weight, ffn_in, ffn_out):
    rows = tokens.shape[1]
    n_context = lax.axis_size("ctx")
    n_shards = lax.axis_size("fsdp")
    ext = rows + 2 * HALF
    start = lax.axis_index("ctx") * rows
    seq_len = observed.shape[1]
    gains_n = norm_gains.shape[1]
    bias_n = var_bias.shape[0]
    shard_id = lax.axis_index("fsdp")
    quartered = n_context == QUADS
    me = lax.axis_index("ctx") if quartered else jnp.int32(0)
    core = shard_id % 2 if quartered else jnp.int32(0)
    place = jnp.stack([me, core]).astype(jnp.int32)

    if quartered:
        quarter = lambda a, width, begin=0: lax.dynamic_slice_in_dim(a, begin + me * width, width, 1)
        shard = jnp.concatenate([quarter(qkv_weight, 256, i * D) for i in range(3)] + [quarter(out_weight, 256)], axis=1)
        whole = lax.all_gather(shard, "fsdp", axis=0, tiled=True)
        whole_in = lax.all_gather(quarter(ffn_in, FF // 2), "fsdp", axis=0, tiled=True)
    else:
        w_attention = jnp.concatenate([qkv_weight, out_weight], axis=1)
        w_attention = lax.all_gather(w_attention, "fsdp", axis=0, tiled=True)
        w_attention = jnp.swapaxes(w_attention.reshape(D, 4, QUADS, 256), 1, 2).reshape(D, QUADS, 1024)
        w_in = lax.all_gather(ffn_in, "fsdp", axis=0, tiled=True).reshape(D, QUADS, FF // 2)
    w_lower = lax.all_gather(ffn_out, "fsdp", axis=0, tiled=True)
    own_count = jnp.sum(observed[0])
    small = jnp.zeros((16, gains_n), BF)
    small = small.at[:4].set(norm_gains).at[4, :bias_n].set(var_bias)
    small = small.at[5, 0].set((own_count // 256).astype(BF)).at[5, 1].set((own_count % 256).astype(BF))
    if quartered:
        beside = permuted(tokens[0], "ctx", 1)
        mine = halves_of(whole, core)
        mine, small = tied(mine, small)
        across = lax.ppermute(beside, "ctx", [(0, 2), (3, 1)])
        odd = me % 2 == 1
        before, behind = jnp.where(odd, beside, across), jnp.where(odd, across, beside)
        near, up = permuted(mine, "ctx", 1), permuted(mine, "ctx", 2)
    else:
        before, behind = shifted(tokens[0], 1), shifted(tokens[0], -1)
        split = lambda w: (w[:, 0],) + tuple(w[i * D // 2 : (i + 1) * D // 2, j] for j in range(1, QUADS) for i in range(2))
        pieces, pieces_in = split(w_attention), split(w_in)

    small = lax.all_to_all(jnp.broadcast_to(small[None], (n_shards,) + small.shape), "fsdp", 0, 0)

    before, behind, small = tied(before, behind, small)

    gains = jnp.moveaxis(small[:, :4], 0, 1).reshape(4, D).astype(F32)
    bias = small[:, 4, :bias_n].reshape(2 * HEADS).astype(F32)
    valid_total = jnp.sum(small[:, 5, 0].astype(F32) * 256.0 + small[:, 5, 1].astype(F32))
    key_pos = start - HALF + jnp.arange(ext, dtype=jnp.int32)
    inside = (key_pos >= 0) & (key_pos < seq_len)
    key_doc = document_ids(lengths[0], key_pos)
    key_var = lax.dynamic_slice_in_dim(jnp.pad(variate[0], HALF), start, ext, 0)
    key_obs = lax.dynamic_slice_in_dim(jnp.pad(observed[0], HALF), start, ext, 0)
    own = slice(HALF, HALF + rows)
    query_feat, key_feat = features(key_doc[own], key_var[own], key_doc, key_var, key_obs, inside)
    cosine, sine = tables(key_pos)
    scales = head_scales(bias)
    mats = blockdiag()
    gain_q, gain_k = gains[2].reshape(-1, 1, 256), gains[3].reshape(-1, 1, 256)

    inputs = jnp.concatenate([before, tokens[0], behind], axis=0).astype(F32)
    inv = lax.rsqrt(jnp.mean(inputs * inputs, axis=-1, keepdims=True) + EPSILON)
    normed = (inputs * inv * gains[0]).astype(BF)

    if quartered:
        near, up, normed, whole_in = tied(near, up, normed, whole_in)
        corner = corner_of(near, up)
        mine_in = halves_of(whole_in, core)
        in_by = [permuted(mine_in, "ctx", flip) for flip in (1, 2, 3)]
        pieces = (whole,) + with_partner(near) + with_partner(up) + with_partner(corner)

    q, k, v, attn, lse, c_q, c_k, w_q, w_kv, w_attn = attention_forward(
        place, normed, pieces, gain_q, gain_k, cosine, sine, query_feat, key_feat, scales, mats
    )
    if quartered:
        in_by, attn = tied(in_by, attn)
        pieces_in = (whole_in,) + sum((with_partner(piece) for piece in in_by), ())
    mixed = tokens[0].astype(F32) + jnp.dot(attn, w_attn, preferred_element_type=F32)
    normed_two = rms_scale(mixed, gains[1]).astype(BF)
    valid_col = key_obs[own].astype(F32)[:, None]
    all_tokens = rows * n_context * n_shards
    hidden, d_gate_low, activations, d_final_low, d_mixed, d_mixed_low, d_attn, squared = feed_forward(
        place, (all_tokens / valid_total)[None], gains[1:2], valid_col, normed_two, mixed, teacher[0], cotangent[0], w_lower, w_attn, pieces_in
    )
    squared = jnp.sum(squared)

    if quartered:
        own_two, other_two = sides(normed_two, core)
        theirs = dot_tn(other_two, d_gate_low).astype(BF)
        hidden, theirs = tied(hidden, theirs)
        swapped = permuted(theirs, "fsdp", 1)
    low_grad = dot_tn(hidden, d_final_low).astype(BF)
    d_mixed_low, low_grad = tied(d_mixed_low, low_grad)
    low_part = lax.psum_scatter(low_grad, "fsdp", scatter_dimension=0, tiled=True)
    out_grad = dot_tn(attn, d_mixed_low).astype(BF)
    if quartered:
        d_gate_low, out_grad = tied(d_gate_low, out_grad)
        in_chip = (dot_tn(own_two, d_gate_low) + swapped.astype(F32)).astype(BF)
        part = lambda j: lax.dynamic_slice_in_dim(in_chip, (me ^ j) * (FF // 2), FF // 2, 1)
        cut = in_chip.shape[0] // 2
        last = part(3)
        d_attn, last = tied(d_attn, last)
        last_near, last_up = permuted(last[:cut], "ctx", 1), permuted(last[cut:], "ctx", 2)
    else:
        in_part = lax.psum_scatter(dot_tn(normed_two, d_gate_low).astype(BF), "fsdp", scatter_dimension=0, tiled=True)
        in_grad = lax.psum(in_part, "ctx").astype(F32)

    d_attn, out_grad = tied(d_attn, out_grad)
    out_part = lax.psum_scatter(out_grad, "fsdp", scatter_dimension=0, tiled=True)
    saved = (q, k, v, d_attn, attn, lse, c_q, c_k, gain_q, gain_k, cosine, sine, query_feat, key_feat, scales, mats)
    d_q1, d_kv1, gain_q1, gain_k1, bias_1 = attention_backward(place, 0, *saved)
    if quartered:
        d_q1, d_kv1, last_near, last_up = tied(d_q1, d_kv1, last_near, last_up)
        d_q1, d_kv1, low_part = tied(d_q1, d_kv1, low_part)
        own_normed, other_normed = sides(normed, core)
        theirs = [dot_tn(other_normed[own], d_q1).astype(BF), dot_tn(other_normed, d_kv1).astype(BF)]
        one, two = part(1), part(2)
        one, two = joined(one[:cut], added(one[cut:], last_up)), joined(added(two[:cut], last_near), two[cut:])
        theirs, d_q1, d_kv1, one, two = tied(theirs, d_q1, d_kv1, one, two)
        swapped = [permuted(t, "fsdp", 1) for t in theirs]
        in_near, in_up = permuted(one, "ctx", 1), permuted(two, "ctx", 2)
        first_q = (dot_tn(own_normed[own], d_q1) + swapped[0].astype(F32)).astype(BF)
        first_kv = (dot_tn(own_normed, d_kv1) + swapped[1].astype(F32)).astype(BF)
        three = jnp.concatenate([first_q[:, :256], first_kv[:, :512]], axis=1)
        one = jnp.concatenate([first_q[:, 256:], first_kv[:, 512:]], axis=1)
        d_attn, three, one = tied(d_attn, three, one)
        last_near, last_up = permuted(three[:cut], "ctx", 1), permuted(three[cut:], "ctx", 2)
        saved = saved[:3] + (d_attn,) + saved[4:]
    d_q2, d_kv2, gain_q2, gain_k2, bias_2 = attention_backward(place, 1, *saved)
    done_first = ((me ^ jnp.arange(QUADS)) % 2 == 1)[:, None, None]
    d_gain_q = jnp.where(done_first, gain_q1, gain_q2).reshape(D)
    d_gain_k = jnp.where(done_first, gain_k1, gain_k2).reshape(D)
    same = jnp.sum(jnp.where(done_first, bias_1, bias_2)[:, :4], axis=-1).reshape(HEADS)
    d_bias = jnp.concatenate([same, -same])

    if quartered:
        extra = jnp.zeros((n_shards, D // n_shards, LANES), F32)
        extra = extra.at[:, 0, :gains_n].set(d_gain_q.reshape(n_shards, gains_n)).at[:, 1, :gains_n].set(d_gain_k.reshape(n_shards, gains_n))
        extra = extra.at[:, 2, :bias_n].set(d_bias.reshape(n_shards, bias_n)).at[:, 3, :DIGITS].set(digits_of(squared)[None])
        extra = extra.reshape(n_shards // 2, 2, D // n_shards, LANES).astype(BF)
        own_extra = jnp.where(core == 0, extra[:, 0], extra[:, 1]).reshape(-1, LANES)
        other_extra = jnp.where(core == 0, extra[:, 1], extra[:, 0]).reshape(-1, LANES)
        d_q2, d_kv2, last_near, last_up = tied(d_q2, d_kv2, last_near, last_up)
        d_q2, d_kv2, in_near, in_up, out_part = tied(d_q2, d_kv2, in_near, in_up, out_part)
        in_total = added(part(0), in_near, in_up)
        d_q2, d_kv2, in_total = tied(d_q2, d_kv2, in_total)
        in_part = core_scatter(in_total)
        other_grads = ctx_parts(joined(out_part, low_part))
    d_ext = dot_nt(d_kv1, w_kv[:, : 2 * 512]) + dot_nt(d_kv2, w_kv[:, 2 * 512 :])
    to_before, to_behind = d_ext[:HALF].astype(BF), d_ext[HALF + rows :].astype(BF)
    if quartered:
        to_before, to_behind, d_q2, d_kv2, other_grads = tied(to_before, to_behind, d_q2, d_kv2, other_grads)
        far = returned_far(to_before, to_behind)
        theirs = [dot_tn(other_normed[own], d_q2).astype(BF), dot_tn(other_normed, d_kv2).astype(BF), other_extra]
        theirs, d_q2, d_kv2, far, in_part = tied(theirs, d_q2, d_kv2, far, in_part)
        swapped = [permuted(t, "fsdp", 1) for t in theirs]
        second_q = (dot_tn(own_normed[own], d_q2) + swapped[0].astype(F32)).astype(BF)
        second_kv = (dot_tn(own_normed, d_kv2) + swapped[1].astype(F32)).astype(BF)
        two = jnp.concatenate([second_q[:, :256], second_kv[:, :512]], axis=1)
        one = joined(one[:cut], added(one[cut:], last_up))
        two = joined(added(two[:cut], last_near), two[cut:])
        near, up = permuted(one, "ctx", 1), permuted(two, "ctx", 2)
        other_grads = ctx_joined(other_grads)
        near, up, in_part, far, other_grads = tied(near, up, in_part, far, other_grads)
        from_others = returned_near(to_before, to_behind, far)
        in_spread = ctx_spread(in_part)
        qkv_total = added(jnp.concatenate([second_q[:, 256:], second_kv[:, 512:]], axis=1), near, up)
        qkv_total = jnp.concatenate([qkv_total, added(own_extra, swapped[2])], axis=1)
        qkv_part = core_scatter(qkv_total)
        qkv_part, in_spread = tied(qkv_part, in_spread)
        spread = ctx_spread(qkv_part)
        from_others, spread = tied(from_others, spread)
        from_others = from_others.astype(F32)
        qkv_grad, gain_one = finish(spread, qkv_weight, tuple((i * 256, 256, i * D) for i in range(3)))
        sums = jnp.sum(spread[:, :, 3 * 256 :].astype(F32), axis=0)
        squared = value_of(sums[3, :DIGITS])
        gain_rows, var_bias_grad = sums[:2, :gains_n], sums[2, :bias_n]
        in_grad, gain_two = finish(in_spread, ffn_in, ((0, FF // 2, 0),))
    else:
        from_others = shifted(to_before, -1).astype(F32) + shifted(to_behind, 1).astype(F32)
        order = [SEND_ORDER.index(j) for j in range(QUADS)]
        natural = lambda first, second, width: jnp.concatenate([first, second], axis=1).reshape(-1, QUADS, width)[:, jnp.array(order)]
        grad_q = dot_tn(normed[own], natural(d_q1, d_q2, 256).reshape(rows, D))
        grad_kv = dot_tn(normed, jnp.swapaxes(natural(d_kv1, d_kv2, 512).reshape(ext, QUADS, 2, 256), 1, 2).reshape(ext, 2 * D))
        grad_qkv = jnp.concatenate([grad_q, grad_kv], axis=1).astype(BF)
        qkv_grad = lax.psum(lax.psum_scatter(grad_qkv, "fsdp", scatter_dimension=0, tiled=True), "ctx").astype(F32)
        other_grads = lax.psum(joined(out_part, low_part), "ctx").astype(F32)
        sums = jnp.concatenate([d_gain_q, d_gain_k, d_bias, squared[None]])
        sums = lax.psum(jnp.pad(sums, (0, -sums.shape[0] % (8 * LANES))).reshape(-1, LANES), ("ctx", "fsdp")).reshape(-1)
        gain_rows = lax.dynamic_slice_in_dim(sums[: 2 * D].reshape(2, D), shard_id * gains_n, gains_n, 1)
        var_bias_grad = lax.dynamic_slice_in_dim(sums[2 * D : 2 * D + 2 * HEADS], shard_id * bias_n, bias_n, 0)
        squared = sums[2 * D + 2 * HEADS]
    d_own = d_ext[own] + dot_nt(d_q1, w_q[:, : 2 * 256]) + dot_nt(d_q2, w_q[:, 2 * 256 :])
    loss = squared / (valid_total * D)
    own_gains = norm_gains.astype(F32)
    if not quartered:
        gain_one = jnp.sum(qkv_weight.astype(F32) * qkv_grad, axis=1)
        gain_two = jnp.sum(ffn_in.astype(F32) * in_grad, axis=1)
    gain_one, gain_two = gain_one.reshape(1, -1) / own_gains[:1], gain_two.reshape(1, -1) / own_gains[1:2]
    gains_grad = jnp.concatenate([gain_one, gain_two, gain_rows], axis=0)
    unit = inputs[own] * inv[own]
    scaled = (d_own + from_others) * gains[0]
    input_grad = d_mixed + inv[own] * (scaled - unit * jnp.mean(unit * scaled, axis=-1, keepdims=True))
    other_grads = other_grads.astype(F32)
    return (
        loss,
        activations[None],
        input_grad[None],
        gains_grad,
        var_bias_grad,
        qkv_grad,
        other_grads[: out_part.shape[0]],
        in_grad,
        other_grads[out_part.shape[0] :],
    )


def solution(mesh):
    split = P("fsdp", "ctx", None)
    rows = P("fsdp", None)
    return jax.shard_map(
        per_device,
        mesh=mesh,
        in_specs=(split, split, split, rows, rows, rows, P(None, "fsdp"), P("fsdp"), rows, rows, rows, rows),
        out_specs=(P(), split, split, P(None, "fsdp"), P("fsdp"), rows, rows, rows, rows),
        check_vma=False,
    )
```

```python
import math

import jax
import jax.numpy as jnp
import numpy as np
from jax import lax
from jax.experimental import pallas as pl
from jax.experimental.pallas import tpu as pltpu
from jax.sharding import PartitionSpec as P


D=1024; HEADS=16; HEAD=64; FF=2816; WINDOW=1024
EPSILON=1e-6; MASKED=-1e30
HALF=WINDOW//2
LANES=128
VAR_AT, LSE_AT, OBS_AT = 8, 32, 35
TILE=256
F32=jnp.float32; BF=jnp.bfloat16


def dot_nn(a,b): return lax.dot_general(a,b,(((1,),(0,)),((),())),preferred_element_type=F32)
def dot_nt(a,b): return lax.dot_general(a,b,(((1,),(1,)),((),())),preferred_element_type=F32)
def dot_tn(a,b): return lax.dot_general(a,b,(((0,),(0,)),((),())),preferred_element_type=F32)

def halves(v):
    high=v.astype(BF)
    return jnp.concatenate([high,(v-high.astype(F32)).astype(BF)],axis=1)

def thirds(v,rounded=lambda a: a.astype(BF).astype(F32)):
    high=rounded(v)
    rest=v-high
    mid=rounded(rest)
    return high,mid,rest-mid

def lane_of(shape): return lax.broadcasted_iota(jnp.int32,shape,1)

def place(v,at):
    high,mid,low=thirds(v)
    lane=lane_of(v.shape)%HEAD
    return jnp.where(lane==at,high,jnp.where(lane==at+1,mid,jnp.where(lane==at+2,low,0.0)))

def band(s,t,tiles,key_axis):
    if t not in (0,tiles-1): return s
    key=lax.broadcasted_iota(jnp.int32,s.shape,key_axis)
    query=lax.broadcasted_iota(jnp.int32,s.shape,1-key_axis)
    keep=key>=query if t==0 else key<=query
    return jnp.where(keep,s,MASKED)

def prep(u,gain,cosine,sine,mean_mat,swap_mat):
    mean=dot_nn(halves(u*u),mean_mat)
    c=lax.rsqrt(mean+EPSILON)
    n=u*c*gain
    return n*cosine+dot_nn(halves(n),swap_mat)*sine, c

QUADS=4
SEND_ORDER=(3,1,2,0)
def position(slot): return jnp.where(slot==0,3,jnp.where(slot==3,0,slot))

def piece_copies(place_ref,pieces,w_ref,sem):
    me,core=place_ref[0],place_ref[1]
    half=w_ref.shape[1]//2
    copies=[[pltpu.make_async_copy(pieces[0],w_ref.at[me],sem.at[0])]]
    for slot in range(1,QUADS):
        copies.append([pltpu.make_async_copy(pieces[2*slot-1+side],
            w_ref.at[me^slot,pl.ds(pl.multiple_of((core if side==0 else 1-core)*half,half),half),:],sem.at[2*slot-1+side]) for side in range(2)])
    return copies

def await_quarter(place_ref,pieces,w_ref,sem):
    step=pl.program_id(0)
    copies=piece_copies(place_ref,pieces,w_ref,sem)
    @pl.when(step==0)
    def _():
        for group in copies:
            for copy in group: copy.start()
    slot=step^place_ref[0]
    for i,group in enumerate(copies):
        @pl.when(slot==i)
        def _(group=group):
            for copy in group: copy.wait()

def fwd_kernel(place_ref,xn_ref,p0,p1,p2,p3,p4,p5,p6,gq_ref,gk_ref,cos_ref,sin_ref,qb_ref,kb_ref,sv_ref,mean_ref,swap_ref,
               q_ref,k_ref,v_ref,attn_ref,lse_ref,cq_ref,ck_ref,wq_out,wkv_out,wattn_out,w_ref,sem):
    rows=qb_ref.shape[0]; ext=kb_ref.shape[0]
    await_quarter(place_ref,(p0,p1,p2,p3,p4,p5,p6),w_ref,sem)
    quad=pl.program_id(0)
    wq_out[...]=w_ref[quad,:,0:256]
    wkv_out[...]=w_ref[quad,:,256:768]
    wattn_out[...]=w_ref[quad,:,768:1024]
    tiles=2*HALF//TILE+1
    mean_mat=mean_ref[...]; swap_mat=swap_ref[...]
    first=(lane_of((1,LANES))<HEAD)
    kf=dot_nn(xn_ref[...],w_ref[quad,:,256:512])
    for pair in range(2):
        col=slice(pair*LANES,(pair+1)*LANES)
        rot,c=prep(kf[:,col],gk_ref[:,col],cos_ref[...],sin_ref[...],mean_mat,swap_mat)
        k_ref[:,col]=rot.astype(BF)
        if pair==0: ck_ref[...]=c
        else: ck_ref[...]=jnp.where(lane_of((1,LANES))%HEAD==pair,c,ck_ref[...])
    v_ref[...]=dot_nn(xn_ref[...],w_ref[quad,:,512:768]).astype(BF)
    qf=dot_nn(xn_ref[HALF:HALF+rows,:],w_ref[quad,:,0:256])
    for pair in range(2):
        col=slice(pair*LANES,(pair+1)*LANES)
        rot,c=prep(qf[:,col],gq_ref[:,col],cos_ref[HALF:HALF+rows,:],sin_ref[HALF:HALF+rows,:],mean_mat,swap_mat)
        q_ref[:,col]=rot.astype(BF)
        if pair==0: cq_ref[...]=c
        else: cq_ref[...]=jnp.where(lane_of((1,LANES))%HEAD==pair,c,cq_ref[...])
    own=[first.astype(F32).astype(BF),(1.0-first.astype(F32)).astype(BF)]
    no_obs=(lane_of((1,LANES))%HEAD!=OBS_AT).astype(F32).astype(BF)
    diag=lax.broadcasted_iota(jnp.int32,(TILE,TILE),0)==lax.broadcasted_iota(jnp.int32,(TILE,TILE),1)
    for pair in range(2):
        col=slice(pair*LANES,(pair+1)*LANES)
        for i in range(rows//TILE):
            sums=[]
            for par in range(2):
                m,other=own[par],own[1-par]
                sv=sv_ref[2*pair+par:2*pair+par+1,:].astype(BF)*other
                qi=q_ref[i*TILE:(i+1)*TILE,col]*BF(HEAD**-0.5)*m+qb_ref[i*TILE:(i+1)*TILE,:]*sv
                acc=None
                for t in range(tiles):
                    at=slice((i+t)*TILE,(i+t+1)*TILE)
                    kt=k_ref[at,col]*m+kb_ref[at,:]*other
                    vt=v_ref[at,col]*m+other
                    s=band(dot_nt(qi,kt),t,tiles,1)
                    if t==tiles//2:
                        s=jnp.where(diag,dot_nt(qi*(m+other*no_obs),kt),s)
                    p=jnp.exp(s).astype(BF)
                    o=dot_nn(p,vt)
                    acc=o if acc is None else acc+o
                sums.append(acc)
            total=jnp.where(first,sums[1],sums[0])
            lse_ref[i*TILE:(i+1)*TILE,col]=jnp.log(total)
            out=jnp.where(first,sums[0],sums[1])/pltpu.roll(total,HEAD,1)
            attn_ref[i*TILE:(i+1)*TILE,col]=out.astype(BF)

def prep_back(rot,d_rot,c,gain,cosine,sine,mean_mat,swap_mat):
    x=rot.astype(F32)
    m=dot_nn(halves(x*d_rot),mean_mat)
    e=d_rot*cosine-dot_nn(halves(d_rot),swap_mat)*sine
    swapped=dot_nn(rot,swap_mat[:LANES])
    n=(x*cosine-swapped*sine)/gain
    return c*(gain*e-n*m), jnp.sum(e*n,axis=0,keepdims=True)

def bwd_kernel(place_ref,q_ref,k_ref,v_ref,do_ref,attn_ref,lse_ref,cq_ref,ck_ref,gq_ref,gk_ref,cos_ref,sin_ref,qb_ref,kb_ref,sv_ref,
               mean_ref,swap_ref,cross_ref,spread_ref,
               dq_ref,dkv_ref,dgq_ref,dgk_ref,bias_ref,dk_acc,dv_acc,ke_ref,ve_ref):
    rows=qb_ref.shape[0]; ext=kb_ref.shape[0]
    tiles=2*HALF//TILE+1
    mean_mat=mean_ref[...]; swap_mat=swap_ref[...]
    first=(lane_of((1,LANES))<HEAD)
    own=[first.astype(F32).astype(BF),(1.0-first.astype(F32)).astype(BF)]
    no_obs=(lane_of((1,LANES))%HEAD!=OBS_AT).astype(F32).astype(BF)
    diag=lax.broadcasted_iota(jnp.int32,(TILE,TILE),0)==lax.broadcasted_iota(jnp.int32,(TILE,TILE),1)
    lane=lane_of((1,LANES))%HEAD
    is_var=(lane>=VAR_AT)&(lane<VAR_AT+8)
    bias_ref[...]=jnp.zeros_like(bias_ref)
    def one_pair(pair,_):
        col=pl.ds(pl.multiple_of(pair*LANES,LANES),LANES)
        dk_acc[...]=jnp.zeros_like(dk_acc)
        dv_acc[...]=jnp.zeros_like(dv_acc)
        prod=do_ref[:,col].astype(F32)*attn_ref[:,col].astype(F32)
        delta=place(dot_nn(halves(prod),cross_ref[...]),0).astype(BF)
        lse=place(lse_ref[:,col],LSE_AT).astype(BF)
        dqs=[]
        for par in range(2):
            m,other=own[par],own[1-par]
            head=2*pair+par
            sv=sv_ref[pl.ds(head,1),:].astype(BF)*other
            qm=q_ref[:,col]*BF(HEAD**-0.5)*m
            qe=qm+qb_ref[...]*sv-lse*other
            dm=do_ref[:,col]*m
            de=dm-delta*other
            ke_ref[...]=k_ref[:,col]*m+kb_ref[...]*other
            ve_ref[...]=v_ref[:,col]*m+other
            parts=[]
            for i in range(rows//TILE):
                r=slice(i*TILE,(i+1)*TILE)
                dq=None
                for t in range(tiles):
                    at=slice((i+t)*TILE,(i+t+1)*TILE)
                    kt=ke_ref[at,:]
                    s=band(dot_nt(kt,qe[r]),t,tiles,0)
                    if t==tiles//2:
                        s=jnp.where(diag,dot_nt(kt,qe[r]*(m+other*no_obs)),s)
                    p=jnp.exp(s)
                    ds=(p*dot_nt(ve_ref[at,:],de[r])).astype(BF)
                    dv_acc[at,:]+=dot_nn(p.astype(BF),dm[r])
                    dk_acc[at,:]+=dot_nn(ds,qm[r])
                    part=dot_tn(ds,kt)
                    dq=part if dq is None else dq+part
                parts.append(dq)
            dq=jnp.concatenate(parts,axis=0)
            hot=jnp.where(is_var&(first!=(par==0)),dq*qb_ref[...].astype(F32),0.0)
            bias_ref[pl.ds(head,1),:]=jnp.sum(hot,axis=0,keepdims=True)
            dqs.append(dq)
        d_rot=jnp.where(first,dqs[0],dqs[1])*(HEAD**-0.5)
        spread=spread_ref[pair]
        cosq,sinq=cos_ref[HALF:HALF+rows,:],sin_ref[HALF:HALF+rows,:]
        du,dg=prep_back(q_ref[:,col],d_rot,dot_nn(halves(cq_ref[...]),spread),gq_ref[:,col],cosq,sinq,mean_mat,swap_mat)
        dq_ref[:,col]=du.astype(BF)
        dgq_ref[:,col]=dg
        du,dg=prep_back(k_ref[:,col],dk_acc[...],dot_nn(halves(ck_ref[...]),spread),gk_ref[:,col],cos_ref[...],sin_ref[...],mean_mat,swap_mat)
        dkv_ref[:,col]=du.astype(BF)
        dgk_ref[:,col]=dg
        dkv_ref[:,pl.ds(pl.multiple_of(256+pair*LANES,LANES),LANES)]=dv_acc[...].astype(BF)
        return 0
    lax.fori_loop(0,2,one_pair,0)

def blockdiag():
    i=jnp.arange(LANES)
    mean=jnp.where(i[:,None]//HEAD==i[None]//HEAD,1.0/HEAD,0.0)
    cross=jnp.where(i[:,None]//HEAD!=i[None]//HEAD,1.0,0.0)
    swap=jnp.where(i[None]==i[:,None]+jnp.where(i[:,None]%HEAD<HEAD//2,HEAD//2,-(HEAD//2)),1.0,0.0)
    spread=jnp.stack([jnp.where(i[:,None]==pair+HEAD*(i[None]//HEAD),1.0,0.0) for pair in range(2)])
    two=lambda a: jnp.concatenate([a,a],axis=-2).astype(BF)
    return two(mean),two(swap),two(cross),two(spread)

def full(*shape):
    n=len(shape)
    return pl.BlockSpec(shape,lambda j,s:(0,)*n)
def colb(rows,width): return pl.BlockSpec((rows,width),lambda j,s:(0,j))
def lead(*shape): return pl.BlockSpec((None,)+shape,lambda j,s:(j,)+(0,)*len(shape))
ANYWHERE=pl.BlockSpec(memory_space=pltpu.HBM)

def attention_forward(place,xn,pieces,gq,gk,cos,sin,qb,kb,sv,mats):
    rows,ext=qb.shape[0],kb.shape[0]
    mean_mat,swap_mat,_,_=mats
    n=QUADS*256
    at=lambda j,s:(0,position(j^s[0]))
    return pl.pallas_call(
        fwd_kernel,
        grid_spec=pltpu.PrefetchScalarGridSpec(
            num_scalar_prefetch=1,grid=(QUADS,),
            in_specs=[full(ext,D)]+[ANYWHERE]*7+[lead(1,256),lead(1,256),full(ext,LANES),full(ext,LANES),
                      full(rows,LANES),full(ext,LANES),lead(8,LANES),full(2*LANES,LANES),full(2*LANES,LANES)],
            out_specs=[colb(rows,256),colb(ext,256),colb(ext,256),colb(rows,256),colb(rows,256),lead(rows,LANES),lead(ext,LANES),
                       pl.BlockSpec((D,256),at),pl.BlockSpec((D,512),at),colb(D,256)],
            scratch_shapes=[pltpu.VMEM((QUADS,D,1024),BF),pltpu.SemaphoreType.DMA((7,))]),
        out_shape=[jax.ShapeDtypeStruct((rows,n),BF),jax.ShapeDtypeStruct((ext,n),BF),jax.ShapeDtypeStruct((ext,n),BF),
                   jax.ShapeDtypeStruct((rows,n),BF),jax.ShapeDtypeStruct((rows,n),F32),
                   jax.ShapeDtypeStruct((QUADS,rows,LANES),F32),jax.ShapeDtypeStruct((QUADS,ext,LANES),F32),
                   jax.ShapeDtypeStruct((D,n),BF),jax.ShapeDtypeStruct((D,2*n),BF),jax.ShapeDtypeStruct((D,n),BF)],
        compiler_params=pltpu.CompilerParams(vmem_limit_bytes=56*2**20),
        cost_estimate=pl.CostEstimate(flops=10**6, bytes_accessed=10**4, transcendentals=0),
        name="attention_forward",
    )(place,xn,*pieces,gq,gk,cos,sin,qb,kb,sv,mean_mat,swap_mat)

def feed_forward_kernel(place_ref,weight_ref,gain_ref,obs_ref,x_in,mixed_in,teacher_in,cot_in,low_in,attn_in,p0,p1,p2,p3,p4,p5,p6,
                        hidden_out,d_up_out,act_out,d_low_out,d_mixed_out,d_mixed_low_out,d_attn_out,sum_ref,
                        w_ref,low_ref,attn_ref,x_ref,mixed_ref,teacher_ref,cot_ref,gate_up_ref,hidden_ref,act_ref,d_low_ref,d_final_ref,acc_ref,
                        in_sem,piece_sem,out_sem):
    arrivals=[pltpu.make_async_copy(src,dst,in_sem.at[i]) for i,(src,dst) in enumerate(
        [(x_in,x_ref),(mixed_in,mixed_ref),(low_in,low_ref),(teacher_in,teacher_ref),(cot_in,cot_ref),(attn_in,attn_ref)])]
    pieces=piece_copies(place_ref,(p0,p1,p2,p3,p4,p5,p6),w_ref,piece_sem)
    arrivals[0].start()
    for group in pieces:
        for copy in group: copy.start()
    for copy in arrivals[1:]: copy.start()
    sent=[]
    def send(ref,out):
        copy=pltpu.make_async_copy(ref,out,out_sem.at[len(sent)])
        copy.start(); sent.append(copy)
    arrivals[0].wait()
    width=w_ref.shape[2]
    tiles=[slice(begin,min(begin+256,width)) for begin in range(0,width,256)]
    for half in range(2):
        for quarter in (half,half+2):
            slot=place_ref[0]^quarter
            for i,group in enumerate(pieces):
                @pl.when(slot==i)
                def _(group=group):
                    for copy in group: copy.wait()
        for tile in tiles:
            at=slice(half*width+tile.start,half*width+tile.stop); up_at=slice(FF+at.start,FF+at.stop)
            gate=dot_nn(x_ref[...],w_ref[half,:,tile])
            up=dot_nn(x_ref[...],w_ref[half+2,:,tile])
            gate_up_ref[:,at]=gate.astype(BF)
            gate_up_ref[:,up_at]=up.astype(BF)
            hidden_ref[:,at]=(gate/(1.0+jnp.exp(-gate))*up).astype(BF)
    send(hidden_ref,hidden_out)
    for copy in arrivals[1:]: copy.wait()
    total=jnp.zeros((1,256),F32)
    for begin in range(0,D,256):
        cols=slice(begin,begin+256)
        final=mixed_ref[:,cols]+dot_nn(hidden_ref[...],low_ref[:,cols])
        act_ref[:,cols]=final.astype(BF)
        distance=final-teacher_ref[:,cols].astype(F32)
        seen=obs_ref[...]*distance
        total=total+jnp.sum(seen*distance,axis=0,keepdims=True)
        d_final=cot_ref[:,cols].astype(F32)+weight_ref[0]*seen
        d_final_ref[:,cols]=d_final
        d_low_ref[:,cols]=d_final.astype(BF)
    sum_ref[...]=total
    send(act_ref,act_out)
    send(d_low_ref,d_low_out)
    for begin in range(0,FF,256):
        cols=slice(begin,begin+256); ups=slice(FF+begin,FF+begin+256)
        d_hidden=dot_nt(d_low_ref[...],low_ref[cols,:])
        gate=gate_up_ref[:,cols].astype(F32); up=gate_up_ref[:,ups].astype(F32)
        sig=1.0/(1.0+jnp.exp(-gate))
        gate_up_ref[:,cols]=(d_hidden*up*(sig*(1.0+gate*(1.0-sig)))).astype(BF)
        gate_up_ref[:,ups]=(d_hidden*(gate*sig)).astype(BF)
    send(gate_up_ref,d_up_out)
    for begin in range(0,D,256):
        part=None
        for quarter in range(QUADS):
            one=dot_nt(gate_up_ref[:,quarter*width:(quarter+1)*width],w_ref[quarter,begin:begin+256,:])
            part=one if part is None else part+one
        acc_ref[:,begin:begin+256]=part
    mixed=mixed_ref[...]
    c=lax.rsqrt(jnp.mean(mixed*mixed,axis=1,keepdims=True)+EPSILON)
    scaled=acc_ref[...]*gain_ref[...]
    unit=mixed*c
    d_mixed=d_final_ref[...]+c*(scaled-unit*jnp.mean(unit*scaled,axis=1,keepdims=True))
    d_final_ref[...]=d_mixed
    send(d_final_ref,d_mixed_out)
    x_ref[...]=d_mixed.astype(BF)
    send(x_ref,d_mixed_low_out)
    for begin in range(0,D,256):
        teacher_ref[:,begin:begin+256]=dot_nt(x_ref[...],attn_ref[begin:begin+256,:]).astype(BF)
    send(teacher_ref,d_attn_out)
    for copy in sent: copy.wait()

def feed_forward(place,weight,gain,obs,x,mixed,teacher,cotangent,w_lower,w_attn,pieces):
    rows=x.shape[0]; width=pieces[0].shape[1]
    low=jax.ShapeDtypeStruct((rows,D),BF)
    smem=pl.BlockSpec(memory_space=pltpu.SMEM); vmem=pl.BlockSpec(memory_space=pltpu.VMEM)
    square=pltpu.VMEM((rows,D),BF); wide=pltpu.VMEM((rows,D),F32)
    return pl.pallas_call(
        feed_forward_kernel,
        in_specs=[smem,smem,vmem,vmem]+[ANYWHERE]*13,
        out_specs=[ANYWHERE]*7+[vmem],
        out_shape=[jax.ShapeDtypeStruct((rows,FF),BF),jax.ShapeDtypeStruct((rows,2*FF),BF),low,low,jax.ShapeDtypeStruct((rows,D),F32),low,low,
                   jax.ShapeDtypeStruct((1,256),F32)],
        scratch_shapes=[pltpu.VMEM((QUADS,D,width),BF),pltpu.VMEM((FF,D),BF),pltpu.VMEM((D,D),BF),square,wide,square,square,
                        pltpu.VMEM((rows,2*FF),BF),pltpu.VMEM((rows,FF),BF),square,square,wide,wide,
                        pltpu.SemaphoreType.DMA((6,)),pltpu.SemaphoreType.DMA((7,)),pltpu.SemaphoreType.DMA((7,))],
        compiler_params=pltpu.CompilerParams(vmem_limit_bytes=58*2**20),
        cost_estimate=pl.CostEstimate(flops=10**6, bytes_accessed=10**4, transcendentals=0),
        name="feed_forward",
    )(place,weight,gain,obs,x,mixed,teacher,cotangent,w_lower,w_attn,*pieces)

def attention_backward(place,call,q,k,v,do,attn,lse,cq,ck,gq,gk,cos,sin,qb,kb,sv,mats):
    rows,ext=qb.shape[0],kb.shape[0]
    def quad(j,s): return s[0]^jnp.where(j==0,SEND_ORDER[2*call],SEND_ORDER[2*call+1])
    def col(rows,width): return pl.BlockSpec((rows,width),lambda j,s:(0,quad(j,s)))
    def led(*shape): return pl.BlockSpec((None,)+shape,lambda j,s:(quad(j,s),)+(0,)*len(shape))
    return pl.pallas_call(
        bwd_kernel,
        grid_spec=pltpu.PrefetchScalarGridSpec(
            num_scalar_prefetch=1,grid=(2,),
            in_specs=[col(rows,256),col(ext,256),col(ext,256),col(rows,256),col(rows,256),col(rows,256),led(rows,LANES),led(ext,LANES),
                      led(1,256),led(1,256),full(ext,LANES),full(ext,LANES),full(rows,LANES),full(ext,LANES),led(8,LANES),
                      full(2*LANES,LANES),full(2*LANES,LANES),full(2*LANES,LANES),full(2,2*LANES,LANES)],
            out_specs=[colb(rows,256),colb(ext,512),led(1,256),led(1,256),led(8,LANES)],
            scratch_shapes=[pltpu.VMEM((ext,LANES),F32),pltpu.VMEM((ext,LANES),F32),pltpu.VMEM((ext,LANES),BF),pltpu.VMEM((ext,LANES),BF)]),
        out_shape=[jax.ShapeDtypeStruct((rows,512),BF),jax.ShapeDtypeStruct((ext,1024),BF),
                   jax.ShapeDtypeStruct((QUADS,1,256),F32),jax.ShapeDtypeStruct((QUADS,1,256),F32),jax.ShapeDtypeStruct((QUADS,8,LANES),F32)],
        compiler_params=pltpu.CompilerParams(vmem_limit_bytes=56*2**20),
        cost_estimate=pl.CostEstimate(flops=10**6, bytes_accessed=10**4, transcendentals=0),
        name="attention_backward",
    )(place,q,k,v,do,attn,lse,cq,ck,gq,gk,cos,sin,qb,kb,sv,*mats)

def finish_kernel(layout,spread_ref,weight_ref,grad_ref,sum_ref):
    total=None
    for quarter in range(QUADS):
        for begin,width,base in layout:
            at=slice(base+quarter*width,base+(quarter+1)*width)
            grad=spread_ref[quarter,:,begin:begin+width].astype(F32)
            grad_ref[:,at]=grad
            part=jnp.sum(grad*weight_ref[:,at].astype(F32),axis=1,keepdims=True)
            total=part if total is None else total+part
    sum_ref[...]=total

def finish(spread,weight,layout):
    vmem=pl.BlockSpec(memory_space=pltpu.VMEM)
    return pl.pallas_call(
        lambda *refs: finish_kernel(layout,*refs),in_specs=[vmem]*2,out_specs=[vmem]*2,
        out_shape=[jax.ShapeDtypeStruct(weight.shape,F32),jax.ShapeDtypeStruct((weight.shape[0],1),F32)],
        compiler_params=pltpu.CompilerParams(vmem_limit_bytes=32*2**20),
        cost_estimate=pl.CostEstimate(flops=10**6, bytes_accessed=10**4, transcendentals=0),
        name="finish",
    )(spread,weight)

def features(query_doc,query_var,key_doc,key_var,key_obs,key_inside):
    lane=jnp.arange(HEAD)[None,:]
    var_lane=(lane>=VAR_AT)&(lane<LSE_AT)
    def tile(a): return jnp.concatenate([a,a],axis=1).astype(BF)
    qv=var_lane&((lane-VAR_AT)%8==query_var[:,None])
    q=((lane<VAR_AT)&(lane==query_doc[:,None]))|qv|(lane==OBS_AT)
    kv=var_lane&((lane-VAR_AT)%8==key_var[:,None])
    closed=(lane<VAR_AT)&~((lane==key_doc[:,None])&key_inside[:,None])
    closed=closed|((lane==OBS_AT)&(key_obs[:,None]!=1))
    ones=kv|((lane>=LSE_AT)&(lane<LSE_AT+3))
    k=jnp.where(closed,MASKED,jnp.where(ones,1.0,0.0))
    return tile(q.astype(F32)),tile(k)

def head_scales(bias_f):
    high,mid,low=thirds(bias_f[:HEADS]-bias_f[HEADS:],lambda a: lax.reduce_precision(a,8,7))
    lane=jnp.arange(HEAD)[None,:]
    part=lambda a: a[:,None]
    s=jnp.where(lane<VAR_AT,1.0,jnp.where(lane<VAR_AT+8,part(high),jnp.where(lane<VAR_AT+16,part(mid),jnp.where(lane<LSE_AT,part(low),1.0))))
    s=jnp.where(lane>OBS_AT,0.0,s)
    s=jnp.concatenate([s,s],axis=1).reshape(HEADS//4,4,LANES)
    return jnp.concatenate([s,jnp.zeros_like(s)],axis=1)

def tables(pos):
    half=HEAD//2
    freq=jnp.exp(jnp.arange(half).astype(F32)*(-2.0*math.log(10000.0)/HEAD))
    ang=pos.astype(F32)[:,None]*freq[None,:]
    c,s=jnp.cos(ang),jnp.sin(ang)
    return jnp.concatenate([c,c,c,c],axis=1),jnp.concatenate([-s,s,-s,s],axis=1)


DIGITS = 34
LOWEST = -7


def tied(*values):
    return lax.optimization_barrier(values)


def permuted(shard, axis, flip):
    return lax.ppermute(shard, axis, [(i, i ^ flip) for i in range(lax.axis_size(axis))])


def shifted(shard, by):
    size = lax.axis_size("ctx")
    return lax.ppermute(shard, "ctx", [(i, i + by) for i in range(size) if 0 <= i + by < size])


def returned_far(before, after):
    odd = lax.axis_index("ctx") % 2 == 1
    return lax.ppermute(jnp.where(odd, after, before), "ctx", [(1, 3), (2, 0)])


def returned_near(before, after, far):
    odd = lax.axis_index("ctx") % 2 == 1
    return permuted(added(jnp.where(odd, before, after), far), "ctx", 1)


def ctx_spread(part):
    size = lax.axis_size("ctx")
    return lax.all_to_all(jnp.broadcast_to(part[None], (size,) + part.shape), "ctx", 0, 0)


def halves_of(whole, core):
    half = whole.shape[0] // 2
    return lax.dynamic_slice_in_dim(whole, core * half, half, 0)


def corner_of(near, up):
    part = near.shape[0] // 2
    return jnp.concatenate([permuted(near[:part], "ctx", 2), permuted(up[part:], "ctx", 1)], axis=0)


def with_partner(piece):
    return piece, permuted(piece, "fsdp", 1)


def sides(left, core):
    count = lax.axis_size("fsdp")
    width = left.shape[1] // count
    blocks = [left[:, i * width : (i + 1) * width] for i in range(count)]
    even, odd = jnp.concatenate(blocks[0::2], axis=1), jnp.concatenate(blocks[1::2], axis=1)
    return jnp.where(core == 0, even, odd), jnp.where(core == 0, odd, even)


def added(*parts):
    return sum(part.astype(F32) for part in parts).astype(BF)


def joined(first, second):
    return jnp.concatenate([first, second], axis=0)


def core_scatter(total):
    size = lax.axis_size("fsdp")
    same_core = [[i for i in range(size) if i % 2 == core] for core in range(2)]
    return lax.psum_scatter(total, "fsdp", scatter_dimension=0, axis_index_groups=same_core, tiled=True)


def ctx_parts(part):
    size = lax.axis_size("ctx")
    return lax.all_to_all(part.reshape(size, part.shape[0] // size, part.shape[1]), "ctx", 0, 0)


def ctx_joined(parts):
    total = jnp.sum(parts.astype(F32), axis=0).astype(BF)
    return ctx_spread(total).reshape(-1, parts.shape[2])


def document_ids(doc_lengths, positions):
    doc_ends = jnp.cumsum(doc_lengths)
    return jnp.sum((positions[:, None] >= doc_ends[None, :]).astype(jnp.int32), axis=1)


def rms_scale(vector, scales):
    return vector * lax.rsqrt(jnp.mean(vector * vector, axis=-1, keepdims=True) + EPSILON) * scales


def digits_of(value):
    scaled = value * jnp.asarray(8.0 ** -(LOWEST + np.arange(DIGITS)), F32)
    return jnp.floor(scaled) - 8.0 * jnp.floor(scaled / 8.0)


def value_of(digits):
    return jnp.sum(digits * jnp.asarray(8.0 ** (LOWEST + np.arange(DIGITS)), F32))


def per_device(tokens, teacher, cotangent, lengths, variate, observed, norm_gains, var_bias, qkv_weight, out_weight, ffn_in, ffn_out):
    rows = tokens.shape[1]
    n_context = lax.axis_size("ctx")
    n_shards = lax.axis_size("fsdp")
    ext = rows + 2 * HALF
    start = lax.axis_index("ctx") * rows
    seq_len = observed.shape[1]
    gains_n = norm_gains.shape[1]
    bias_n = var_bias.shape[0]
    shard_id = lax.axis_index("fsdp")
    quartered = n_context == QUADS
    me = lax.axis_index("ctx") if quartered else jnp.int32(0)
    core = shard_id % 2 if quartered else jnp.int32(0)
    place = jnp.stack([me, core]).astype(jnp.int32)

    if quartered:
        quarter = lambda a, width, begin=0: lax.dynamic_slice_in_dim(a, begin + me * width, width, 1)
        shard = jnp.concatenate([quarter(qkv_weight, 256, i * D) for i in range(3)] + [quarter(out_weight, 256)], axis=1)
        whole = lax.all_gather(shard, "fsdp", axis=0, tiled=True)
        whole_in = lax.all_gather(quarter(ffn_in, FF // 2), "fsdp", axis=0, tiled=True)
    else:
        w_attention = jnp.concatenate([qkv_weight, out_weight], axis=1)
        w_attention = lax.all_gather(w_attention, "fsdp", axis=0, tiled=True)
        w_attention = jnp.swapaxes(w_attention.reshape(D, 4, QUADS, 256), 1, 2).reshape(D, QUADS, 1024)
        w_in = lax.all_gather(ffn_in, "fsdp", axis=0, tiled=True).reshape(D, QUADS, FF // 2)
    w_lower = lax.all_gather(ffn_out, "fsdp", axis=0, tiled=True)
    own_count = jnp.sum(observed[0])
    small = jnp.zeros((16, gains_n), BF)
    small = small.at[:4].set(norm_gains).at[4, :bias_n].set(var_bias)
    small = small.at[5, 0].set((own_count // 256).astype(BF)).at[5, 1].set((own_count % 256).astype(BF))
    if quartered:
        beside = permuted(tokens[0], "ctx", 1)
        mine = halves_of(whole, core)
        mine, small = tied(mine, small)
        across = lax.ppermute(beside, "ctx", [(0, 2), (3, 1)])
        odd = me % 2 == 1
        before, behind = jnp.where(odd, beside, across), jnp.where(odd, across, beside)
        near, up = permuted(mine, "ctx", 1), permuted(mine, "ctx", 2)
    else:
        before, behind = shifted(tokens[0], 1), shifted(tokens[0], -1)
        split = lambda w: (w[:, 0],) + tuple(w[i * D // 2 : (i + 1) * D // 2, j] for j in range(1, QUADS) for i in range(2))
        pieces, pieces_in = split(w_attention), split(w_in)

    small = lax.all_to_all(jnp.broadcast_to(small[None], (n_shards,) + small.shape), "fsdp", 0, 0)

    before, behind, small = tied(before, behind, small)

    gains = jnp.moveaxis(small[:, :4], 0, 1).reshape(4, D).astype(F32)
    bias = small[:, 4, :bias_n].reshape(2 * HEADS).astype(F32)
    valid_total = jnp.sum(small[:, 5, 0].astype(F32) * 256.0 + small[:, 5, 1].astype(F32))
    key_pos = start - HALF + jnp.arange(ext, dtype=jnp.int32)
    inside = (key_pos >= 0) & (key_pos < seq_len)
    key_doc = document_ids(lengths[0], key_pos)
    key_var = lax.dynamic_slice_in_dim(jnp.pad(variate[0], HALF), start, ext, 0)
    key_obs = lax.dynamic_slice_in_dim(jnp.pad(observed[0], HALF), start, ext, 0)
    own = slice(HALF, HALF + rows)
    query_feat, key_feat = features(key_doc[own], key_var[own], key_doc, key_var, key_obs, inside)
    cosine, sine = tables(key_pos)
    scales = head_scales(bias)
    mats = blockdiag()
    gain_q, gain_k = gains[2].reshape(-1, 1, 256), gains[3].reshape(-1, 1, 256)

    inputs = jnp.concatenate([before, tokens[0], behind], axis=0).astype(F32)
    inv = lax.rsqrt(jnp.mean(inputs * inputs, axis=-1, keepdims=True) + EPSILON)
    normed = (inputs * inv * gains[0]).astype(BF)

    if quartered:
        near, up, normed, whole_in = tied(near, up, normed, whole_in)
        corner = corner_of(near, up)
        mine_in = halves_of(whole_in, core)
        in_by = [permuted(mine_in, "ctx", flip) for flip in (1, 2, 3)]
        pieces = (whole,) + with_partner(near) + with_partner(up) + with_partner(corner)

    q, k, v, attn, lse, c_q, c_k, w_q, w_kv, w_attn = attention_forward(
        place, normed, pieces, gain_q, gain_k, cosine, sine, query_feat, key_feat, scales, mats
    )
    mixed = tokens[0].astype(F32) + jnp.dot(attn, w_attn, preferred_element_type=F32)
    normed_two = rms_scale(mixed, gains[1]).astype(BF)
    if quartered:
        in_by, normed_two, mixed = tied(in_by, normed_two, mixed)
        pieces_in = (whole_in,) + sum((with_partner(piece) for piece in in_by), ())
    valid_col = key_obs[own].astype(F32)[:, None]
    all_tokens = rows * n_context * n_shards
    hidden, d_gate_low, activations, d_final_low, d_mixed, d_mixed_low, d_attn, squared = feed_forward(
        place, (all_tokens / valid_total)[None], gains[1:2], valid_col, normed_two, mixed, teacher[0], cotangent[0], w_lower, w_attn, pieces_in
    )
    squared = jnp.sum(squared)

    if quartered:
        own_two, other_two = sides(normed_two, core)
        theirs = dot_tn(other_two, d_gate_low).astype(BF)
        hidden, theirs = tied(hidden, theirs)
        swapped = permuted(theirs, "fsdp", 1)
    low_grad = dot_tn(hidden, d_final_low).astype(BF)
    d_mixed_low, low_grad = tied(d_mixed_low, low_grad)
    low_part = lax.psum_scatter(low_grad, "fsdp", scatter_dimension=0, tiled=True)
    out_grad = dot_tn(attn, d_mixed_low).astype(BF)
    if quartered:
        d_gate_low, out_grad = tied(d_gate_low, out_grad)
        in_chip = (dot_tn(own_two, d_gate_low) + swapped.astype(F32)).astype(BF)
        part = lambda j: lax.dynamic_slice_in_dim(in_chip, (me ^ j) * (FF // 2), FF // 2, 1)
        cut = in_chip.shape[0] // 2
        last = part(3)
        d_attn, last = tied(d_attn, last)
        last_near, last_up = permuted(last[:cut], "ctx", 1), permuted(last[cut:], "ctx", 2)
    else:
        in_part = lax.psum_scatter(dot_tn(normed_two, d_gate_low).astype(BF), "fsdp", scatter_dimension=0, tiled=True)
        in_grad = lax.psum(in_part, "ctx").astype(F32)

    d_attn, out_grad = tied(d_attn, out_grad)
    out_part = lax.psum_scatter(out_grad, "fsdp", scatter_dimension=0, tiled=True)
    saved = (q, k, v, d_attn, attn, lse, c_q, c_k, gain_q, gain_k, cosine, sine, query_feat, key_feat, scales, mats)
    d_q1, d_kv1, gain_q1, gain_k1, bias_1 = attention_backward(place, 0, *saved)
    if quartered:
        d_q1, d_kv1, last_near, last_up = tied(d_q1, d_kv1, last_near, last_up)
        d_q1, d_kv1, low_part = tied(d_q1, d_kv1, low_part)
        own_normed, other_normed = sides(normed, core)
        theirs = [dot_tn(other_normed[own], d_q1).astype(BF), dot_tn(other_normed, d_kv1).astype(BF)]
        one, two = part(1), part(2)
        one, two = joined(one[:cut], added(one[cut:], last_up)), joined(added(two[:cut], last_near), two[cut:])
        theirs, d_q1, d_kv1, one, two = tied(theirs, d_q1, d_kv1, one, two)
        swapped = [permuted(t, "fsdp", 1) for t in theirs]
        in_near, in_up = permuted(one, "ctx", 1), permuted(two, "ctx", 2)
        first_q = (dot_tn(own_normed[own], d_q1) + swapped[0].astype(F32)).astype(BF)
        first_kv = (dot_tn(own_normed, d_kv1) + swapped[1].astype(F32)).astype(BF)
        three = jnp.concatenate([first_q[:, :256], first_kv[:, :512]], axis=1)
        one = jnp.concatenate([first_q[:, 256:], first_kv[:, 512:]], axis=1)
        d_attn, three, one = tied(d_attn, three, one)
        last_near, last_up = permuted(three[:cut], "ctx", 1), permuted(three[cut:], "ctx", 2)
        saved = saved[:3] + (d_attn,) + saved[4:]
    d_q2, d_kv2, gain_q2, gain_k2, bias_2 = attention_backward(place, 1, *saved)
    done_first = ((me ^ jnp.arange(QUADS)) % 2 == 1)[:, None, None]
    d_gain_q = jnp.where(done_first, gain_q1, gain_q2).reshape(D)
    d_gain_k = jnp.where(done_first, gain_k1, gain_k2).reshape(D)
    same = jnp.sum(jnp.where(done_first, bias_1, bias_2)[:, :4], axis=-1).reshape(HEADS)
    d_bias = jnp.concatenate([same, -same])

    if quartered:
        extra = jnp.zeros((n_shards, D // n_shards, LANES), F32)
        extra = extra.at[:, 0, :gains_n].set(d_gain_q.reshape(n_shards, gains_n)).at[:, 1, :gains_n].set(d_gain_k.reshape(n_shards, gains_n))
        extra = extra.at[:, 2, :bias_n].set(d_bias.reshape(n_shards, bias_n)).at[:, 3, :DIGITS].set(digits_of(squared)[None])
        extra = extra.reshape(n_shards // 2, 2, D // n_shards, LANES).astype(BF)
        own_extra = jnp.where(core == 0, extra[:, 0], extra[:, 1]).reshape(-1, LANES)
        other_extra = jnp.where(core == 0, extra[:, 1], extra[:, 0]).reshape(-1, LANES)
        d_q2, d_kv2, last_near, last_up = tied(d_q2, d_kv2, last_near, last_up)
        d_q2, d_kv2, in_near, in_up, out_part = tied(d_q2, d_kv2, in_near, in_up, out_part)
        in_total = added(part(0), in_near, in_up)
        d_q2, d_kv2, in_total = tied(d_q2, d_kv2, in_total)
        in_part = core_scatter(in_total)
        other_grads = ctx_parts(joined(out_part, low_part))
    d_ext = dot_nt(d_kv1, w_kv[:, : 2 * 512]) + dot_nt(d_kv2, w_kv[:, 2 * 512 :])
    to_before, to_behind = d_ext[:HALF].astype(BF), d_ext[HALF + rows :].astype(BF)
    if quartered:
        to_before, to_behind, d_q2, d_kv2, other_grads = tied(to_before, to_behind, d_q2, d_kv2, other_grads)
        far = returned_far(to_before, to_behind)
        theirs = [dot_tn(other_normed[own], d_q2).astype(BF), dot_tn(other_normed, d_kv2).astype(BF), other_extra]
        theirs, d_q2, d_kv2, far, in_part = tied(theirs, d_q2, d_kv2, far, in_part)
        swapped = [permuted(t, "fsdp", 1) for t in theirs]
        second_q = (dot_tn(own_normed[own], d_q2) + swapped[0].astype(F32)).astype(BF)
        second_kv = (dot_tn(own_normed, d_kv2) + swapped[1].astype(F32)).astype(BF)
        two = jnp.concatenate([second_q[:, :256], second_kv[:, :512]], axis=1)
        one = joined(one[:cut], added(one[cut:], last_up))
        two = joined(added(two[:cut], last_near), two[cut:])
        near, up = permuted(one, "ctx", 1), permuted(two, "ctx", 2)
        other_grads = ctx_joined(other_grads)
        near, up, in_part, far, other_grads = tied(near, up, in_part, far, other_grads)
        from_others = returned_near(to_before, to_behind, far)
        in_spread = ctx_spread(in_part)
        qkv_total = added(jnp.concatenate([second_q[:, 256:], second_kv[:, 512:]], axis=1), near, up)
        qkv_total = jnp.concatenate([qkv_total, added(own_extra, swapped[2])], axis=1)
        qkv_part = core_scatter(qkv_total)
        qkv_part, in_spread = tied(qkv_part, in_spread)
        spread = ctx_spread(qkv_part)
        from_others = from_others.astype(F32)
        qkv_grad, gain_one = finish(spread, qkv_weight, tuple((i * 256, 256, i * D) for i in range(3)))
        sums = jnp.sum(spread[:, :, 3 * 256 :].astype(F32), axis=0)
        squared = value_of(sums[3, :DIGITS])
        gain_rows, var_bias_grad = sums[:2, :gains_n], sums[2, :bias_n]
        in_grad, gain_two = finish(in_spread, ffn_in, ((0, FF // 2, 0),))
    else:
        from_others = shifted(to_before, -1).astype(F32) + shifted(to_behind, 1).astype(F32)
        order = [SEND_ORDER.index(j) for j in range(QUADS)]
        natural = lambda first, second, width: jnp.concatenate([first, second], axis=1).reshape(-1, QUADS, width)[:, jnp.array(order)]
        grad_q = dot_tn(normed[own], natural(d_q1, d_q2, 256).reshape(rows, D))
        grad_kv = dot_tn(normed, jnp.swapaxes(natural(d_kv1, d_kv2, 512).reshape(ext, QUADS, 2, 256), 1, 2).reshape(ext, 2 * D))
        grad_qkv = jnp.concatenate([grad_q, grad_kv], axis=1).astype(BF)
        qkv_grad = lax.psum(lax.psum_scatter(grad_qkv, "fsdp", scatter_dimension=0, tiled=True), "ctx").astype(F32)
        other_grads = lax.psum(joined(out_part, low_part), "ctx").astype(F32)
        sums = jnp.concatenate([d_gain_q, d_gain_k, d_bias, squared[None]])
        sums = lax.psum(jnp.pad(sums, (0, -sums.shape[0] % (8 * LANES))).reshape(-1, LANES), ("ctx", "fsdp")).reshape(-1)
        gain_rows = lax.dynamic_slice_in_dim(sums[: 2 * D].reshape(2, D), shard_id * gains_n, gains_n, 1)
        var_bias_grad = lax.dynamic_slice_in_dim(sums[2 * D : 2 * D + 2 * HEADS], shard_id * bias_n, bias_n, 0)
        squared = sums[2 * D + 2 * HEADS]
    d_own = d_ext[own] + dot_nt(d_q1, w_q[:, : 2 * 256]) + dot_nt(d_q2, w_q[:, 2 * 256 :])
    loss = squared / (valid_total * D)
    own_gains = norm_gains.astype(F32)
    if not quartered:
        gain_one = jnp.sum(qkv_weight.astype(F32) * qkv_grad, axis=1)
        gain_two = jnp.sum(ffn_in.astype(F32) * in_grad, axis=1)
    gain_one, gain_two = gain_one.reshape(1, -1) / own_gains[:1], gain_two.reshape(1, -1) / own_gains[1:2]
    gains_grad = jnp.concatenate([gain_one, gain_two, gain_rows], axis=0)
    unit = inputs[own] * inv[own]
    scaled = (d_own + from_others) * gains[0]
    input_grad = d_mixed + inv[own] * (scaled - unit * jnp.mean(unit * scaled, axis=-1, keepdims=True))
    other_grads = other_grads.astype(F32)
    return (
        loss,
        activations[None],
        input_grad[None],
        gains_grad,
        var_bias_grad,
        qkv_grad,
        other_grads[: out_part.shape[0]],
        in_grad,
        other_grads[out_part.shape[0] :],
    )


def solution(mesh):
    split = P("fsdp", "ctx", None)
    rows = P("fsdp", None)
    return jax.shard_map(
        per_device,
        mesh=mesh,
        in_specs=(split, split, split, rows, rows, rows, P(None, "fsdp"), P("fsdp"), rows, rows, rows, rows),
        out_specs=(P(), split, split, P(None, "fsdp"), P("fsdp"), rows, rows, rows, rows),
        check_vma=False,
    )
```

```python
import math

import jax
import jax.numpy as jnp
import numpy as np
from jax import lax
from jax.experimental import pallas as pl
from jax.experimental.pallas import tpu as pltpu
from jax.sharding import PartitionSpec as P


D=1024; HEADS=16; HEAD=64; FF=2816; WINDOW=1024
EPSILON=1e-6; MASKED=-1e30
HALF=WINDOW//2
LANES=128
VAR_AT, LSE_AT, OBS_AT = 8, 32, 35
TILE=256
F32=jnp.float32; BF=jnp.bfloat16


def dot_nn(a,b): return lax.dot_general(a,b,(((1,),(0,)),((),())),preferred_element_type=F32)
def dot_nt(a,b): return lax.dot_general(a,b,(((1,),(1,)),((),())),preferred_element_type=F32)
def dot_tn(a,b): return lax.dot_general(a,b,(((0,),(0,)),((),())),preferred_element_type=F32)

def halves(v):
    high=v.astype(BF)
    return jnp.concatenate([high,(v-high.astype(F32)).astype(BF)],axis=1)

def thirds(v,rounded=lambda a: a.astype(BF).astype(F32)):
    high=rounded(v)
    rest=v-high
    mid=rounded(rest)
    return high,mid,rest-mid

def lane_of(shape): return lax.broadcasted_iota(jnp.int32,shape,1)

def place(v,at):
    high,mid,low=thirds(v)
    lane=lane_of(v.shape)%HEAD
    return jnp.where(lane==at,high,jnp.where(lane==at+1,mid,jnp.where(lane==at+2,low,0.0)))

def band(s,t,tiles,key_axis):
    if t not in (0,tiles-1): return s
    key=lax.broadcasted_iota(jnp.int32,s.shape,key_axis)
    query=lax.broadcasted_iota(jnp.int32,s.shape,1-key_axis)
    keep=key>=query if t==0 else key<=query
    return jnp.where(keep,s,MASKED)

def prep(u,gain,cosine,sine,mean_mat,swap_mat):
    mean=dot_nn(halves(u*u),mean_mat)
    c=lax.rsqrt(mean+EPSILON)
    n=u*c*gain
    return n*cosine+dot_nn(halves(n),swap_mat)*sine, c

QUADS=4
SEND_ORDER=(3,1,2,0)
def position(slot): return jnp.where(slot==0,3,jnp.where(slot==3,0,slot))

def piece_copies(place_ref,pieces,w_ref,sem):
    me,core=place_ref[0],place_ref[1]
    half=w_ref.shape[1]//2
    copies=[[pltpu.make_async_copy(pieces[0],w_ref.at[me],sem.at[0])]]
    for slot in range(1,QUADS):
        copies.append([pltpu.make_async_copy(pieces[2*slot-1+side],
            w_ref.at[me^slot,pl.ds(pl.multiple_of((core if side==0 else 1-core)*half,half),half),:],sem.at[2*slot-1+side]) for side in range(2)])
    return copies

def await_quarter(place_ref,pieces,w_ref,sem):
    step=pl.program_id(0)
    copies=piece_copies(place_ref,pieces,w_ref,sem)
    @pl.when(step==0)
    def _():
        for group in copies:
            for copy in group: copy.start()
    slot=step^place_ref[0]
    for i,group in enumerate(copies):
        @pl.when(slot==i)
        def _(group=group):
            for copy in group: copy.wait()

def fwd_kernel(place_ref,xn_ref,p0,p1,p2,p3,p4,p5,p6,gq_ref,gk_ref,cos_ref,sin_ref,qb_ref,kb_ref,sv_ref,mean_ref,swap_ref,
               q_ref,k_ref,v_ref,attn_ref,lse_ref,cq_ref,ck_ref,wq_out,wkv_out,wattn_out,w_ref,sem):
    rows=qb_ref.shape[0]; ext=kb_ref.shape[0]
    await_quarter(place_ref,(p0,p1,p2,p3,p4,p5,p6),w_ref,sem)
    quad=pl.program_id(0)
    wq_out[...]=w_ref[quad,:,0:256]
    wkv_out[...]=w_ref[quad,:,256:768]
    wattn_out[...]=w_ref[quad,:,768:1024]
    tiles=2*HALF//TILE+1
    mean_mat=mean_ref[...]; swap_mat=swap_ref[...]
    first=(lane_of((1,LANES))<HEAD)
    kf=dot_nn(xn_ref[...],w_ref[quad,:,256:512])
    for pair in range(2):
        col=slice(pair*LANES,(pair+1)*LANES)
        rot,c=prep(kf[:,col],gk_ref[:,col],cos_ref[...],sin_ref[...],mean_mat,swap_mat)
        k_ref[:,col]=rot.astype(BF)
        if pair==0: ck_ref[...]=c
        else: ck_ref[...]=jnp.where(lane_of((1,LANES))%HEAD==pair,c,ck_ref[...])
    v_ref[...]=dot_nn(xn_ref[...],w_ref[quad,:,512:768]).astype(BF)
    qf=dot_nn(xn_ref[HALF:HALF+rows,:],w_ref[quad,:,0:256])
    for pair in range(2):
        col=slice(pair*LANES,(pair+1)*LANES)
        rot,c=prep(qf[:,col],gq_ref[:,col],cos_ref[HALF:HALF+rows,:],sin_ref[HALF:HALF+rows,:],mean_mat,swap_mat)
        q_ref[:,col]=rot.astype(BF)
        if pair==0: cq_ref[...]=c
        else: cq_ref[...]=jnp.where(lane_of((1,LANES))%HEAD==pair,c,cq_ref[...])
    own=[first.astype(F32).astype(BF),(1.0-first.astype(F32)).astype(BF)]
    no_obs=(lane_of((1,LANES))%HEAD!=OBS_AT).astype(F32).astype(BF)
    diag=lax.broadcasted_iota(jnp.int32,(TILE,TILE),0)==lax.broadcasted_iota(jnp.int32,(TILE,TILE),1)
    for pair in range(2):
        col=slice(pair*LANES,(pair+1)*LANES)
        for i in range(rows//TILE):
            sums=[]
            for par in range(2):
                m,other=own[par],own[1-par]
                sv=sv_ref[2*pair+par:2*pair+par+1,:].astype(BF)*other
                qi=q_ref[i*TILE:(i+1)*TILE,col]*BF(HEAD**-0.5)*m+qb_ref[i*TILE:(i+1)*TILE,:]*sv
                acc=None
                for t in range(tiles):
                    at=slice((i+t)*TILE,(i+t+1)*TILE)
                    kt=k_ref[at,col]*m+kb_ref[at,:]*other
                    vt=v_ref[at,col]*m+other
                    s=band(dot_nt(qi,kt),t,tiles,1)
                    if t==tiles//2:
                        s=jnp.where(diag,dot_nt(qi*(m+other*no_obs),kt),s)
                    p=jnp.exp(s).astype(BF)
                    o=dot_nn(p,vt)
                    acc=o if acc is None else acc+o
                sums.append(acc)
            total=jnp.where(first,sums[1],sums[0])
            lse_ref[i*TILE:(i+1)*TILE,col]=jnp.log(total)
            out=jnp.where(first,sums[0],sums[1])/pltpu.roll(total,HEAD,1)
            attn_ref[i*TILE:(i+1)*TILE,col]=out.astype(BF)

def prep_back(rot,d_rot,c,gain,cosine,sine,mean_mat,swap_mat):
    x=rot.astype(F32)
    m=dot_nn(halves(x*d_rot),mean_mat)
    e=d_rot*cosine-dot_nn(halves(d_rot),swap_mat)*sine
    swapped=dot_nn(rot,swap_mat[:LANES])
    n=(x*cosine-swapped*sine)/gain
    return c*(gain*e-n*m), jnp.sum(e*n,axis=0,keepdims=True)

def bwd_kernel(place_ref,q_ref,k_ref,v_ref,do_ref,attn_ref,lse_ref,cq_ref,ck_ref,gq_ref,gk_ref,cos_ref,sin_ref,qb_ref,kb_ref,sv_ref,
               mean_ref,swap_ref,cross_ref,spread_ref,
               dq_ref,dkv_ref,dgq_ref,dgk_ref,bias_ref,dk_acc,dv_acc,ke_ref,ve_ref):
    rows=qb_ref.shape[0]; ext=kb_ref.shape[0]
    tiles=2*HALF//TILE+1
    mean_mat=mean_ref[...]; swap_mat=swap_ref[...]
    first=(lane_of((1,LANES))<HEAD)
    own=[first.astype(F32).astype(BF),(1.0-first.astype(F32)).astype(BF)]
    no_obs=(lane_of((1,LANES))%HEAD!=OBS_AT).astype(F32).astype(BF)
    diag=lax.broadcasted_iota(jnp.int32,(TILE,TILE),0)==lax.broadcasted_iota(jnp.int32,(TILE,TILE),1)
    lane=lane_of((1,LANES))%HEAD
    is_var=(lane>=VAR_AT)&(lane<VAR_AT+8)
    bias_ref[...]=jnp.zeros_like(bias_ref)
    def one_pair(pair,_):
        col=pl.ds(pl.multiple_of(pair*LANES,LANES),LANES)
        dk_acc[...]=jnp.zeros_like(dk_acc)
        dv_acc[...]=jnp.zeros_like(dv_acc)
        prod=do_ref[:,col].astype(F32)*attn_ref[:,col].astype(F32)
        delta=place(dot_nn(halves(prod),cross_ref[...]),0).astype(BF)
        lse=place(lse_ref[:,col],LSE_AT).astype(BF)
        dqs=[]
        for par in range(2):
            m,other=own[par],own[1-par]
            head=2*pair+par
            sv=sv_ref[pl.ds(head,1),:].astype(BF)*other
            qm=q_ref[:,col]*BF(HEAD**-0.5)*m
            qe=qm+qb_ref[...]*sv-lse*other
            dm=do_ref[:,col]*m
            de=dm-delta*other
            ke_ref[...]=k_ref[:,col]*m+kb_ref[...]*other
            ve_ref[...]=v_ref[:,col]*m+other
            parts=[]
            for i in range(rows//TILE):
                r=slice(i*TILE,(i+1)*TILE)
                dq=None
                for t in range(tiles):
                    at=slice((i+t)*TILE,(i+t+1)*TILE)
                    kt=ke_ref[at,:]
                    s=band(dot_nt(kt,qe[r]),t,tiles,0)
                    if t==tiles//2:
                        s=jnp.where(diag,dot_nt(kt,qe[r]*(m+other*no_obs)),s)
                    p=jnp.exp(s)
                    ds=(p*dot_nt(ve_ref[at,:],de[r])).astype(BF)
                    dv_acc[at,:]+=dot_nn(p.astype(BF),dm[r])
                    dk_acc[at,:]+=dot_nn(ds,qm[r])
                    part=dot_tn(ds,kt)
                    dq=part if dq is None else dq+part
                parts.append(dq)
            dq=jnp.concatenate(parts,axis=0)
            hot=jnp.where(is_var&(first!=(par==0)),dq*qb_ref[...].astype(F32),0.0)
            bias_ref[pl.ds(head,1),:]=jnp.sum(hot,axis=0,keepdims=True)
            dqs.append(dq)
        d_rot=jnp.where(first,dqs[0],dqs[1])*(HEAD**-0.5)
        spread=spread_ref[pair]
        cosq,sinq=cos_ref[HALF:HALF+rows,:],sin_ref[HALF:HALF+rows,:]
        du,dg=prep_back(q_ref[:,col],d_rot,dot_nn(halves(cq_ref[...]),spread),gq_ref[:,col],cosq,sinq,mean_mat,swap_mat)
        dq_ref[:,col]=du.astype(BF)
        dgq_ref[:,col]=dg
        du,dg=prep_back(k_ref[:,col],dk_acc[...],dot_nn(halves(ck_ref[...]),spread),gk_ref[:,col],cos_ref[...],sin_ref[...],mean_mat,swap_mat)
        dkv_ref[:,col]=du.astype(BF)
        dgk_ref[:,col]=dg
        dkv_ref[:,pl.ds(pl.multiple_of(256+pair*LANES,LANES),LANES)]=dv_acc[...].astype(BF)
        return 0
    lax.fori_loop(0,2,one_pair,0)

def blockdiag():
    i=jnp.arange(LANES)
    mean=jnp.where(i[:,None]//HEAD==i[None]//HEAD,1.0/HEAD,0.0)
    cross=jnp.where(i[:,None]//HEAD!=i[None]//HEAD,1.0,0.0)
    swap=jnp.where(i[None]==i[:,None]+jnp.where(i[:,None]%HEAD<HEAD//2,HEAD//2,-(HEAD//2)),1.0,0.0)
    spread=jnp.stack([jnp.where(i[:,None]==pair+HEAD*(i[None]//HEAD),1.0,0.0) for pair in range(2)])
    two=lambda a: jnp.concatenate([a,a],axis=-2).astype(BF)
    return two(mean),two(swap),two(cross),two(spread)

def full(*shape):
    n=len(shape)
    return pl.BlockSpec(shape,lambda j,s:(0,)*n)
def colb(rows,width): return pl.BlockSpec((rows,width),lambda j,s:(0,j))
def lead(*shape): return pl.BlockSpec((None,)+shape,lambda j,s:(j,)+(0,)*len(shape))
ANYWHERE=pl.BlockSpec(memory_space=pltpu.HBM)

def attention_forward(place,xn,pieces,gq,gk,cos,sin,qb,kb,sv,mats):
    rows,ext=qb.shape[0],kb.shape[0]
    mean_mat,swap_mat,_,_=mats
    n=QUADS*256
    at=lambda j,s:(0,position(j^s[0]))
    return pl.pallas_call(
        fwd_kernel,
        grid_spec=pltpu.PrefetchScalarGridSpec(
            num_scalar_prefetch=1,grid=(QUADS,),
            in_specs=[full(ext,D)]+[ANYWHERE]*7+[lead(1,256),lead(1,256),full(ext,LANES),full(ext,LANES),
                      full(rows,LANES),full(ext,LANES),lead(8,LANES),full(2*LANES,LANES),full(2*LANES,LANES)],
            out_specs=[colb(rows,256),colb(ext,256),colb(ext,256),colb(rows,256),colb(rows,256),lead(rows,LANES),lead(ext,LANES),
                       pl.BlockSpec((D,256),at),pl.BlockSpec((D,512),at),colb(D,256)],
            scratch_shapes=[pltpu.VMEM((QUADS,D,1024),BF),pltpu.SemaphoreType.DMA((7,))]),
        out_shape=[jax.ShapeDtypeStruct((rows,n),BF),jax.ShapeDtypeStruct((ext,n),BF),jax.ShapeDtypeStruct((ext,n),BF),
                   jax.ShapeDtypeStruct((rows,n),BF),jax.ShapeDtypeStruct((rows,n),F32),
                   jax.ShapeDtypeStruct((QUADS,rows,LANES),F32),jax.ShapeDtypeStruct((QUADS,ext,LANES),F32),
                   jax.ShapeDtypeStruct((D,n),BF),jax.ShapeDtypeStruct((D,2*n),BF),jax.ShapeDtypeStruct((D,n),BF)],
        compiler_params=pltpu.CompilerParams(vmem_limit_bytes=56*2**20),
        cost_estimate=pl.CostEstimate(flops=10**6, bytes_accessed=10**4, transcendentals=0),
        name="attention_forward",
    )(place,xn,*pieces,gq,gk,cos,sin,qb,kb,sv,mean_mat,swap_mat)

def feed_forward_kernel(place_ref,weight_ref,gain_ref,obs_ref,x_in,mixed_in,teacher_in,cot_in,low_in,attn_in,p0,p1,p2,p3,p4,p5,p6,
                        hidden_out,d_up_out,act_out,d_low_out,d_mixed_out,d_mixed_low_out,d_attn_out,sum_ref,
                        w_ref,low_ref,attn_ref,x_ref,mixed_ref,teacher_ref,cot_ref,gate_up_ref,hidden_ref,act_ref,d_low_ref,d_final_ref,acc_ref,
                        in_sem,piece_sem,out_sem):
    arrivals=[pltpu.make_async_copy(src,dst,in_sem.at[i]) for i,(src,dst) in enumerate(
        [(x_in,x_ref),(mixed_in,mixed_ref),(low_in,low_ref),(teacher_in,teacher_ref),(cot_in,cot_ref),(attn_in,attn_ref)])]
    pieces=piece_copies(place_ref,(p0,p1,p2,p3,p4,p5,p6),w_ref,piece_sem)
    arrivals[0].start()
    for group in pieces:
        for copy in group: copy.start()
    for copy in arrivals[1:]: copy.start()
    sent=[]
    def send(ref,out):
        copy=pltpu.make_async_copy(ref,out,out_sem.at[len(sent)])
        copy.start(); sent.append(copy)
    arrivals[0].wait()
    width=w_ref.shape[2]
    tiles=[slice(begin,min(begin+256,width)) for begin in range(0,width,256)]
    for half in range(2):
        for quarter in (half,half+2):
            slot=place_ref[0]^quarter
            for i,group in enumerate(pieces):
                @pl.when(slot==i)
                def _(group=group):
                    for copy in group: copy.wait()
        for tile in tiles:
            at=slice(half*width+tile.start,half*width+tile.stop); up_at=slice(FF+at.start,FF+at.stop)
            gate=dot_nn(x_ref[...],w_ref[half,:,tile])
            up=dot_nn(x_ref[...],w_ref[half+2,:,tile])
            gate_up_ref[:,at]=gate.astype(BF)
            gate_up_ref[:,up_at]=up.astype(BF)
            hidden_ref[:,at]=(gate/(1.0+jnp.exp(-gate))*up).astype(BF)
    send(hidden_ref,hidden_out)
    for copy in arrivals[1:]: copy.wait()
    total=jnp.zeros((1,256),F32)
    for begin in range(0,D,256):
        cols=slice(begin,begin+256)
        final=mixed_ref[:,cols]+dot_nn(hidden_ref[...],low_ref[:,cols])
        act_ref[:,cols]=final.astype(BF)
        distance=final-teacher_ref[:,cols].astype(F32)
        seen=obs_ref[...]*distance
        total=total+jnp.sum(seen*distance,axis=0,keepdims=True)
        d_final=cot_ref[:,cols].astype(F32)+weight_ref[0]*seen
        d_final_ref[:,cols]=d_final
        d_low_ref[:,cols]=d_final.astype(BF)
    sum_ref[...]=total
    send(act_ref,act_out)
    send(d_low_ref,d_low_out)
    for begin in range(0,FF,256):
        cols=slice(begin,begin+256); ups=slice(FF+begin,FF+begin+256)
        d_hidden=dot_nt(d_low_ref[...],low_ref[cols,:])
        gate=gate_up_ref[:,cols].astype(F32); up=gate_up_ref[:,ups].astype(F32)
        sig=1.0/(1.0+jnp.exp(-gate))
        gate_up_ref[:,cols]=(d_hidden*up*(sig*(1.0+gate*(1.0-sig)))).astype(BF)
        gate_up_ref[:,ups]=(d_hidden*(gate*sig)).astype(BF)
    send(gate_up_ref,d_up_out)
    for begin in range(0,D,256):
        part=None
        for quarter in range(QUADS):
            one=dot_nt(gate_up_ref[:,quarter*width:(quarter+1)*width],w_ref[quarter,begin:begin+256,:])
            part=one if part is None else part+one
        acc_ref[:,begin:begin+256]=part
    mixed=mixed_ref[...]
    c=lax.rsqrt(jnp.mean(mixed*mixed,axis=1,keepdims=True)+EPSILON)
    scaled=acc_ref[...]*gain_ref[...]
    unit=mixed*c
    d_mixed=d_final_ref[...]+c*(scaled-unit*jnp.mean(unit*scaled,axis=1,keepdims=True))
    d_final_ref[...]=d_mixed
    send(d_final_ref,d_mixed_out)
    x_ref[...]=d_mixed.astype(BF)
    send(x_ref,d_mixed_low_out)
    for begin in range(0,D,256):
        teacher_ref[:,begin:begin+256]=dot_nt(x_ref[...],attn_ref[begin:begin+256,:]).astype(BF)
    send(teacher_ref,d_attn_out)
    for copy in sent: copy.wait()

def feed_forward(place,weight,gain,obs,x,mixed,teacher,cotangent,w_lower,w_attn,pieces):
    rows=x.shape[0]; width=pieces[0].shape[1]
    low=jax.ShapeDtypeStruct((rows,D),BF)
    smem=pl.BlockSpec(memory_space=pltpu.SMEM); vmem=pl.BlockSpec(memory_space=pltpu.VMEM)
    square=pltpu.VMEM((rows,D),BF); wide=pltpu.VMEM((rows,D),F32)
    return pl.pallas_call(
        feed_forward_kernel,
        in_specs=[smem,smem,vmem,vmem]+[ANYWHERE]*13,
        out_specs=[ANYWHERE]*7+[vmem],
        out_shape=[jax.ShapeDtypeStruct((rows,FF),BF),jax.ShapeDtypeStruct((rows,2*FF),BF),low,low,jax.ShapeDtypeStruct((rows,D),F32),low,low,
                   jax.ShapeDtypeStruct((1,256),F32)],
        scratch_shapes=[pltpu.VMEM((QUADS,D,width),BF),pltpu.VMEM((FF,D),BF),pltpu.VMEM((D,D),BF),square,wide,square,square,
                        pltpu.VMEM((rows,2*FF),BF),pltpu.VMEM((rows,FF),BF),square,square,wide,wide,
                        pltpu.SemaphoreType.DMA((6,)),pltpu.SemaphoreType.DMA((7,)),pltpu.SemaphoreType.DMA((7,))],
        compiler_params=pltpu.CompilerParams(vmem_limit_bytes=58*2**20),
        cost_estimate=pl.CostEstimate(flops=10**6, bytes_accessed=10**4, transcendentals=0),
        name="feed_forward",
    )(place,weight,gain,obs,x,mixed,teacher,cotangent,w_lower,w_attn,*pieces)

def attention_backward(place,call,q,k,v,do,attn,lse,cq,ck,gq,gk,cos,sin,qb,kb,sv,mats):
    rows,ext=qb.shape[0],kb.shape[0]
    def quad(j,s): return s[0]^jnp.where(j==0,SEND_ORDER[2*call],SEND_ORDER[2*call+1])
    def col(rows,width): return pl.BlockSpec((rows,width),lambda j,s:(0,quad(j,s)))
    def led(*shape): return pl.BlockSpec((None,)+shape,lambda j,s:(quad(j,s),)+(0,)*len(shape))
    return pl.pallas_call(
        bwd_kernel,
        grid_spec=pltpu.PrefetchScalarGridSpec(
            num_scalar_prefetch=1,grid=(2,),
            in_specs=[col(rows,256),col(ext,256),col(ext,256),col(rows,256),col(rows,256),col(rows,256),led(rows,LANES),led(ext,LANES),
                      led(1,256),led(1,256),full(ext,LANES),full(ext,LANES),full(rows,LANES),full(ext,LANES),led(8,LANES),
                      full(2*LANES,LANES),full(2*LANES,LANES),full(2*LANES,LANES),full(2,2*LANES,LANES)],
            out_specs=[colb(rows,256),colb(ext,512),led(1,256),led(1,256),led(8,LANES)],
            scratch_shapes=[pltpu.VMEM((ext,LANES),F32),pltpu.VMEM((ext,LANES),F32),pltpu.VMEM((ext,LANES),BF),pltpu.VMEM((ext,LANES),BF)]),
        out_shape=[jax.ShapeDtypeStruct((rows,512),BF),jax.ShapeDtypeStruct((ext,1024),BF),
                   jax.ShapeDtypeStruct((QUADS,1,256),F32),jax.ShapeDtypeStruct((QUADS,1,256),F32),jax.ShapeDtypeStruct((QUADS,8,LANES),F32)],
        compiler_params=pltpu.CompilerParams(vmem_limit_bytes=56*2**20),
        cost_estimate=pl.CostEstimate(flops=10**6, bytes_accessed=10**4, transcendentals=0),
        name="attention_backward",
    )(place,q,k,v,do,attn,lse,cq,ck,gq,gk,cos,sin,qb,kb,sv,*mats)

def finish_kernel(layout,spread_ref,weight_ref,grad_ref,sum_ref):
    total=None
    for quarter in range(QUADS):
        for begin,width,base in layout:
            at=slice(base+quarter*width,base+(quarter+1)*width)
            grad=spread_ref[quarter,:,begin:begin+width].astype(F32)
            grad_ref[:,at]=grad
            part=jnp.sum(grad*weight_ref[:,at].astype(F32),axis=1,keepdims=True)
            total=part if total is None else total+part
    sum_ref[...]=total

def finish(spread,weight,layout):
    vmem=pl.BlockSpec(memory_space=pltpu.VMEM)
    return pl.pallas_call(
        lambda *refs: finish_kernel(layout,*refs),in_specs=[vmem]*2,out_specs=[vmem]*2,
        out_shape=[jax.ShapeDtypeStruct(weight.shape,F32),jax.ShapeDtypeStruct((weight.shape[0],1),F32)],
        compiler_params=pltpu.CompilerParams(vmem_limit_bytes=32*2**20),
        cost_estimate=pl.CostEstimate(flops=10**6, bytes_accessed=10**4, transcendentals=0),
        name="finish",
    )(spread,weight)

def features(query_doc,query_var,key_doc,key_var,key_obs,key_inside):
    lane=jnp.arange(HEAD)[None,:]
    var_lane=(lane>=VAR_AT)&(lane<LSE_AT)
    def tile(a): return jnp.concatenate([a,a],axis=1).astype(BF)
    qv=var_lane&((lane-VAR_AT)%8==query_var[:,None])
    q=((lane<VAR_AT)&(lane==query_doc[:,None]))|qv|(lane==OBS_AT)
    kv=var_lane&((lane-VAR_AT)%8==key_var[:,None])
    closed=(lane<VAR_AT)&~((lane==key_doc[:,None])&key_inside[:,None])
    closed=closed|((lane==OBS_AT)&(key_obs[:,None]!=1))
    ones=kv|((lane>=LSE_AT)&(lane<LSE_AT+3))
    k=jnp.where(closed,MASKED,jnp.where(ones,1.0,0.0))
    return tile(q.astype(F32)),tile(k)

def head_scales(bias_f):
    high,mid,low=thirds(bias_f[:HEADS]-bias_f[HEADS:],lambda a: lax.reduce_precision(a,8,7))
    lane=jnp.arange(HEAD)[None,:]
    part=lambda a: a[:,None]
    s=jnp.where(lane<VAR_AT,1.0,jnp.where(lane<VAR_AT+8,part(high),jnp.where(lane<VAR_AT+16,part(mid),jnp.where(lane<LSE_AT,part(low),1.0))))
    s=jnp.where(lane>OBS_AT,0.0,s)
    s=jnp.concatenate([s,s],axis=1).reshape(HEADS//4,4,LANES)
    return jnp.concatenate([s,jnp.zeros_like(s)],axis=1)

def tables(pos):
    half=HEAD//2
    freq=jnp.exp(jnp.arange(half).astype(F32)*(-2.0*math.log(10000.0)/HEAD))
    ang=pos.astype(F32)[:,None]*freq[None,:]
    c,s=jnp.cos(ang),jnp.sin(ang)
    return jnp.concatenate([c,c,c,c],axis=1),jnp.concatenate([-s,s,-s,s],axis=1)


DIGITS = 34
LOWEST = -7


def tied(*values):
    return lax.optimization_barrier(values)


def permuted(shard, axis, flip):
    return lax.ppermute(shard, axis, [(i, i ^ flip) for i in range(lax.axis_size(axis))])


def shifted(shard, by):
    size = lax.axis_size("ctx")
    return lax.ppermute(shard, "ctx", [(i, i + by) for i in range(size) if 0 <= i + by < size])


def returned_far(before, after):
    odd = lax.axis_index("ctx") % 2 == 1
    return lax.ppermute(jnp.where(odd, after, before), "ctx", [(1, 3), (2, 0)])


def returned_near(before, after, far):
    odd = lax.axis_index("ctx") % 2 == 1
    return permuted(added(jnp.where(odd, before, after), far), "ctx", 1)


def ctx_spread(part):
    size = lax.axis_size("ctx")
    return lax.all_to_all(jnp.broadcast_to(part[None], (size,) + part.shape), "ctx", 0, 0)


def halves_of(whole, core):
    half = whole.shape[0] // 2
    return lax.dynamic_slice_in_dim(whole, core * half, half, 0)


def corner_of(near, up):
    part = near.shape[0] // 2
    return jnp.concatenate([permuted(near[:part], "ctx", 2), permuted(up[part:], "ctx", 1)], axis=0)


def with_partner(piece):
    return piece, permuted(piece, "fsdp", 1)


def sides(left, core):
    count = lax.axis_size("fsdp")
    width = left.shape[1] // count
    blocks = [left[:, i * width : (i + 1) * width] for i in range(count)]
    even, odd = jnp.concatenate(blocks[0::2], axis=1), jnp.concatenate(blocks[1::2], axis=1)
    return jnp.where(core == 0, even, odd), jnp.where(core == 0, odd, even)


def added(*parts):
    return sum(part.astype(F32) for part in parts).astype(BF)


def joined(first, second):
    return jnp.concatenate([first, second], axis=0)


def core_scatter(total):
    size = lax.axis_size("fsdp")
    same_core = [[i for i in range(size) if i % 2 == core] for core in range(2)]
    return lax.psum_scatter(total, "fsdp", scatter_dimension=0, axis_index_groups=same_core, tiled=True)


def ctx_parts(part):
    size = lax.axis_size("ctx")
    return lax.all_to_all(part.reshape(size, part.shape[0] // size, part.shape[1]), "ctx", 0, 0)


def ctx_joined(parts):
    total = jnp.sum(parts.astype(F32), axis=0).astype(BF)
    return ctx_spread(total).reshape(-1, parts.shape[2])


def document_ids(doc_lengths, positions):
    doc_ends = jnp.cumsum(doc_lengths)
    return jnp.sum((positions[:, None] >= doc_ends[None, :]).astype(jnp.int32), axis=1)


def rms_scale(vector, scales):
    return vector * lax.rsqrt(jnp.mean(vector * vector, axis=-1, keepdims=True) + EPSILON) * scales


def digits_of(value):
    scaled = value * jnp.asarray(8.0 ** -(LOWEST + np.arange(DIGITS)), F32)
    return jnp.floor(scaled) - 8.0 * jnp.floor(scaled / 8.0)


def value_of(digits):
    return jnp.sum(digits * jnp.asarray(8.0 ** (LOWEST + np.arange(DIGITS)), F32))


def per_device(tokens, teacher, cotangent, lengths, variate, observed, norm_gains, var_bias, qkv_weight, out_weight, ffn_in, ffn_out):
    rows = tokens.shape[1]
    n_context = lax.axis_size("ctx")
    n_shards = lax.axis_size("fsdp")
    ext = rows + 2 * HALF
    start = lax.axis_index("ctx") * rows
    seq_len = observed.shape[1]
    gains_n = norm_gains.shape[1]
    bias_n = var_bias.shape[0]
    shard_id = lax.axis_index("fsdp")
    quartered = n_context == QUADS
    me = lax.axis_index("ctx") if quartered else jnp.int32(0)
    core = shard_id % 2 if quartered else jnp.int32(0)
    place = jnp.stack([me, core]).astype(jnp.int32)

    if quartered:
        quarter = lambda a, width, begin=0: lax.dynamic_slice_in_dim(a, begin + me * width, width, 1)
        shard = jnp.concatenate([quarter(qkv_weight, 256, i * D) for i in range(3)] + [quarter(out_weight, 256)], axis=1)
        whole = lax.all_gather(shard, "fsdp", axis=0, tiled=True)
        whole_in = lax.all_gather(quarter(ffn_in, FF // 2), "fsdp", axis=0, tiled=True)
    else:
        w_attention = jnp.concatenate([qkv_weight, out_weight], axis=1)
        w_attention = lax.all_gather(w_attention, "fsdp", axis=0, tiled=True)
        w_attention = jnp.swapaxes(w_attention.reshape(D, 4, QUADS, 256), 1, 2).reshape(D, QUADS, 1024)
        w_in = lax.all_gather(ffn_in, "fsdp", axis=0, tiled=True).reshape(D, QUADS, FF // 2)
    w_lower = lax.all_gather(ffn_out, "fsdp", axis=0, tiled=True)
    own_count = jnp.sum(observed[0])
    small = jnp.zeros((16, gains_n), BF)
    small = small.at[:4].set(norm_gains).at[4, :bias_n].set(var_bias)
    small = small.at[5, 0].set((own_count // 256).astype(BF)).at[5, 1].set((own_count % 256).astype(BF))
    if quartered:
        beside = permuted(tokens[0], "ctx", 1)
        mine = halves_of(whole, core)
        mine, small = tied(mine, small)
        across = lax.ppermute(beside, "ctx", [(0, 2), (3, 1)])
        odd = me % 2 == 1
        before, behind = jnp.where(odd, beside, across), jnp.where(odd, across, beside)
        near, up = permuted(mine, "ctx", 1), permuted(mine, "ctx", 2)
    else:
        before, behind = shifted(tokens[0], 1), shifted(tokens[0], -1)
        split = lambda w: (w[:, 0],) + tuple(w[i * D // 2 : (i + 1) * D // 2, j] for j in range(1, QUADS) for i in range(2))
        pieces, pieces_in = split(w_attention), split(w_in)

    small = lax.all_to_all(jnp.broadcast_to(small[None], (n_shards,) + small.shape), "fsdp", 0, 0)

    before, behind, small = tied(before, behind, small)
    if quartered:
        before, behind, near = tied(before, behind, near)

    gains = jnp.moveaxis(small[:, :4], 0, 1).reshape(4, D).astype(F32)
    bias = small[:, 4, :bias_n].reshape(2 * HEADS).astype(F32)
    valid_total = jnp.sum(small[:, 5, 0].astype(F32) * 256.0 + small[:, 5, 1].astype(F32))
    key_pos = start - HALF + jnp.arange(ext, dtype=jnp.int32)
    inside = (key_pos >= 0) & (key_pos < seq_len)
    key_doc = document_ids(lengths[0], key_pos)
    key_var = lax.dynamic_slice_in_dim(jnp.pad(variate[0], HALF), start, ext, 0)
    key_obs = lax.dynamic_slice_in_dim(jnp.pad(observed[0], HALF), start, ext, 0)
    own = slice(HALF, HALF + rows)
    query_feat, key_feat = features(key_doc[own], key_var[own], key_doc, key_var, key_obs, inside)
    cosine, sine = tables(key_pos)
    scales = head_scales(bias)
    mats = blockdiag()
    gain_q, gain_k = gains[2].reshape(-1, 1, 256), gains[3].reshape(-1, 1, 256)

    inputs = jnp.concatenate([before, tokens[0], behind], axis=0).astype(F32)
    inv = lax.rsqrt(jnp.mean(inputs * inputs, axis=-1, keepdims=True) + EPSILON)
    normed = (inputs * inv * gains[0]).astype(BF)

    if quartered:
        near, up, normed, whole_in = tied(near, up, normed, whole_in)
        corner = corner_of(near, up)
        mine_in = halves_of(whole_in, core)
        in_by = [permuted(mine_in, "ctx", flip) for flip in (1, 2, 3)]
        pieces = (whole,) + with_partner(near) + with_partner(up) + with_partner(corner)

    q, k, v, attn, lse, c_q, c_k, w_q, w_kv, w_attn = attention_forward(
        place, normed, pieces, gain_q, gain_k, cosine, sine, query_feat, key_feat, scales, mats
    )
    mixed = tokens[0].astype(F32) + jnp.dot(attn, w_attn, preferred_element_type=F32)
    normed_two = rms_scale(mixed, gains[1]).astype(BF)
    if quartered:
        in_by, normed_two, mixed = tied(in_by, normed_two, mixed)
        pieces_in = (whole_in,) + sum((with_partner(piece) for piece in in_by), ())
    valid_col = key_obs[own].astype(F32)[:, None]
    all_tokens = rows * n_context * n_shards
    hidden, d_gate_low, activations, d_final_low, d_mixed, d_mixed_low, d_attn, squared = feed_forward(
        place, (all_tokens / valid_total)[None], gains[1:2], valid_col, normed_two, mixed, teacher[0], cotangent[0], w_lower, w_attn, pieces_in
    )
    squared = jnp.sum(squared)

    if quartered:
        own_two, other_two = sides(normed_two, core)
        theirs = dot_tn(other_two, d_gate_low).astype(BF)
        hidden, theirs = tied(hidden, theirs)
        swapped = permuted(theirs, "fsdp", 1)
    low_grad = dot_tn(hidden, d_final_low).astype(BF)
    d_mixed_low, low_grad = tied(d_mixed_low, low_grad)
    low_part = lax.psum_scatter(low_grad, "fsdp", scatter_dimension=0, tiled=True)
    out_grad = dot_tn(attn, d_mixed_low).astype(BF)
    if quartered:
        d_gate_low, out_grad = tied(d_gate_low, out_grad)
        in_chip = (dot_tn(own_two, d_gate_low) + swapped.astype(F32)).astype(BF)
        part = lambda j: lax.dynamic_slice_in_dim(in_chip, (me ^ j) * (FF // 2), FF // 2, 1)
        cut = in_chip.shape[0] // 2
        last = part(3)
        d_attn, last = tied(d_attn, last)
        last_near, last_up = permuted(last[:cut], "ctx", 1), permuted(last[cut:], "ctx", 2)
    else:
        in_part = lax.psum_scatter(dot_tn(normed_two, d_gate_low).astype(BF), "fsdp", scatter_dimension=0, tiled=True)
        in_grad = lax.psum(in_part, "ctx").astype(F32)

    d_attn, out_grad = tied(d_attn, out_grad)
    out_part = lax.psum_scatter(out_grad, "fsdp", scatter_dimension=0, tiled=True)
    saved = (q, k, v, d_attn, attn, lse, c_q, c_k, gain_q, gain_k, cosine, sine, query_feat, key_feat, scales, mats)
    d_q1, d_kv1, gain_q1, gain_k1, bias_1 = attention_backward(place, 0, *saved)
    if quartered:
        d_q1, d_kv1, last_near, last_up = tied(d_q1, d_kv1, last_near, last_up)
        d_q1, d_kv1, low_part = tied(d_q1, d_kv1, low_part)
        own_normed, other_normed = sides(normed, core)
        theirs = [dot_tn(other_normed[own], d_q1).astype(BF), dot_tn(other_normed, d_kv1).astype(BF)]
        one, two = part(1), part(2)
        one, two = joined(one[:cut], added(one[cut:], last_up)), joined(added(two[:cut], last_near), two[cut:])
        theirs, d_q1, d_kv1, one, two = tied(theirs, d_q1, d_kv1, one, two)
        swapped = [permuted(t, "fsdp", 1) for t in theirs]
        in_near, in_up = permuted(one, "ctx", 1), permuted(two, "ctx", 2)
        first_q = (dot_tn(own_normed[own], d_q1) + swapped[0].astype(F32)).astype(BF)
        first_kv = (dot_tn(own_normed, d_kv1) + swapped[1].astype(F32)).astype(BF)
        three = jnp.concatenate([first_q[:, :256], first_kv[:, :512]], axis=1)
        one = jnp.concatenate([first_q[:, 256:], first_kv[:, 512:]], axis=1)
        d_attn, three, one = tied(d_attn, three, one)
        last_near, last_up = permuted(three[:cut], "ctx", 1), permuted(three[cut:], "ctx", 2)
        saved = saved[:3] + (d_attn,) + saved[4:]
    d_q2, d_kv2, gain_q2, gain_k2, bias_2 = attention_backward(place, 1, *saved)
    done_first = ((me ^ jnp.arange(QUADS)) % 2 == 1)[:, None, None]
    d_gain_q = jnp.where(done_first, gain_q1, gain_q2).reshape(D)
    d_gain_k = jnp.where(done_first, gain_k1, gain_k2).reshape(D)
    same = jnp.sum(jnp.where(done_first, bias_1, bias_2)[:, :4], axis=-1).reshape(HEADS)
    d_bias = jnp.concatenate([same, -same])

    if quartered:
        extra = jnp.zeros((n_shards, D // n_shards, LANES), F32)
        extra = extra.at[:, 0, :gains_n].set(d_gain_q.reshape(n_shards, gains_n)).at[:, 1, :gains_n].set(d_gain_k.reshape(n_shards, gains_n))
        extra = extra.at[:, 2, :bias_n].set(d_bias.reshape(n_shards, bias_n)).at[:, 3, :DIGITS].set(digits_of(squared)[None])
        extra = extra.reshape(n_shards // 2, 2, D // n_shards, LANES).astype(BF)
        own_extra = jnp.where(core == 0, extra[:, 0], extra[:, 1]).reshape(-1, LANES)
        other_extra = jnp.where(core == 0, extra[:, 1], extra[:, 0]).reshape(-1, LANES)
        d_q2, d_kv2, last_near, last_up = tied(d_q2, d_kv2, last_near, last_up)
        d_q2, d_kv2, in_near, in_up, out_part = tied(d_q2, d_kv2, in_near, in_up, out_part)
        in_total = added(part(0), in_near, in_up)
        d_q2, d_kv2, in_total = tied(d_q2, d_kv2, in_total)
        in_part = core_scatter(in_total)
        other_grads = ctx_parts(joined(out_part, low_part))
    d_ext = dot_nt(d_kv1, w_kv[:, : 2 * 512]) + dot_nt(d_kv2, w_kv[:, 2 * 512 :])
    to_before, to_behind = d_ext[:HALF].astype(BF), d_ext[HALF + rows :].astype(BF)
    if quartered:
        to_before, to_behind, d_q2, d_kv2, other_grads = tied(to_before, to_behind, d_q2, d_kv2, other_grads)
        far = returned_far(to_before, to_behind)
        theirs = [dot_tn(other_normed[own], d_q2).astype(BF), dot_tn(other_normed, d_kv2).astype(BF), other_extra]
        theirs, d_q2, d_kv2, far, in_part = tied(theirs, d_q2, d_kv2, far, in_part)
        swapped = [permuted(t, "fsdp", 1) for t in theirs]
        second_q = (dot_tn(own_normed[own], d_q2) + swapped[0].astype(F32)).astype(BF)
        second_kv = (dot_tn(own_normed, d_kv2) + swapped[1].astype(F32)).astype(BF)
        two = jnp.concatenate([second_q[:, :256], second_kv[:, :512]], axis=1)
        one = joined(one[:cut], added(one[cut:], last_up))
        two = joined(added(two[:cut], last_near), two[cut:])
        near, up = permuted(one, "ctx", 1), permuted(two, "ctx", 2)
        other_grads = ctx_joined(other_grads)
        near, up, in_part, far, other_grads = tied(near, up, in_part, far, other_grads)
        from_others = returned_near(to_before, to_behind, far)
        in_spread = ctx_spread(in_part)
        qkv_total = added(jnp.concatenate([second_q[:, 256:], second_kv[:, 512:]], axis=1), near, up)
        qkv_total = jnp.concatenate([qkv_total, added(own_extra, swapped[2])], axis=1)
        qkv_part = core_scatter(qkv_total)
        qkv_part, in_spread = tied(qkv_part, in_spread)
        spread = ctx_spread(qkv_part)
        from_others = from_others.astype(F32)
        qkv_grad, gain_one = finish(spread, qkv_weight, tuple((i * 256, 256, i * D) for i in range(3)))
        sums = jnp.sum(spread[:, :, 3 * 256 :].astype(F32), axis=0)
        squared = value_of(sums[3, :DIGITS])
        gain_rows, var_bias_grad = sums[:2, :gains_n], sums[2, :bias_n]
        in_grad, gain_two = finish(in_spread, ffn_in, ((0, FF // 2, 0),))
    else:
        from_others = shifted(to_before, -1).astype(F32) + shifted(to_behind, 1).astype(F32)
        order = [SEND_ORDER.index(j) for j in range(QUADS)]
        natural = lambda first, second, width: jnp.concatenate([first, second], axis=1).reshape(-1, QUADS, width)[:, jnp.array(order)]
        grad_q = dot_tn(normed[own], natural(d_q1, d_q2, 256).reshape(rows, D))
        grad_kv = dot_tn(normed, jnp.swapaxes(natural(d_kv1, d_kv2, 512).reshape(ext, QUADS, 2, 256), 1, 2).reshape(ext, 2 * D))
        grad_qkv = jnp.concatenate([grad_q, grad_kv], axis=1).astype(BF)
        qkv_grad = lax.psum(lax.psum_scatter(grad_qkv, "fsdp", scatter_dimension=0, tiled=True), "ctx").astype(F32)
        other_grads = lax.psum(joined(out_part, low_part), "ctx").astype(F32)
        sums = jnp.concatenate([d_gain_q, d_gain_k, d_bias, squared[None]])
        sums = lax.psum(jnp.pad(sums, (0, -sums.shape[0] % (8 * LANES))).reshape(-1, LANES), ("ctx", "fsdp")).reshape(-1)
        gain_rows = lax.dynamic_slice_in_dim(sums[: 2 * D].reshape(2, D), shard_id * gains_n, gains_n, 1)
        var_bias_grad = lax.dynamic_slice_in_dim(sums[2 * D : 2 * D + 2 * HEADS], shard_id * bias_n, bias_n, 0)
        squared = sums[2 * D + 2 * HEADS]
    d_own = d_ext[own] + dot_nt(d_q1, w_q[:, : 2 * 256]) + dot_nt(d_q2, w_q[:, 2 * 256 :])
    loss = squared / (valid_total * D)
    own_gains = norm_gains.astype(F32)
    if not quartered:
        gain_one = jnp.sum(qkv_weight.astype(F32) * qkv_grad, axis=1)
        gain_two = jnp.sum(ffn_in.astype(F32) * in_grad, axis=1)
    gain_one, gain_two = gain_one.reshape(1, -1) / own_gains[:1], gain_two.reshape(1, -1) / own_gains[1:2]
    gains_grad = jnp.concatenate([gain_one, gain_two, gain_rows], axis=0)
    unit = inputs[own] * inv[own]
    scaled = (d_own + from_others) * gains[0]
    input_grad = d_mixed + inv[own] * (scaled - unit * jnp.mean(unit * scaled, axis=-1, keepdims=True))
    other_grads = other_grads.astype(F32)
    return (
        loss,
        activations[None],
        input_grad[None],
        gains_grad,
        var_bias_grad,
        qkv_grad,
        other_grads[: out_part.shape[0]],
        in_grad,
        other_grads[out_part.shape[0] :],
    )


def solution(mesh):
    split = P("fsdp", "ctx", None)
    rows = P("fsdp", None)
    return jax.shard_map(
        per_device,
        mesh=mesh,
        in_specs=(split, split, split, rows, rows, rows, P(None, "fsdp"), P("fsdp"), rows, rows, rows, rows),
        out_specs=(P(), split, split, P(None, "fsdp"), P("fsdp"), rows, rows, rows, rows),
        check_vma=False,
    )
```
